128 devices in a mesh: dp: 2 (over z_lo), context: 16 (over x, z_hi, core), tensor: 4 (over y).
Axes of the slice: x: 4, y: 4, z: 4 (z_hi: 2, z_lo: 2; z = z_hi * 2 + z_lo), core: 2. Of those that a mesh axis runs over, the one named last changes fastest.
Arguments:
- hidden_in: bfloat16 [4096, 1024], P(('dp', 'context')), may hold values from -6 to 6
- segments: int32 [2, 2048], P('dp', 'context'), may hold values from 0 to 3, never falling along the last dimension, each value on 1 to 1921 neighbouring positions
- routes: int32 [1, 4096, 8], P(None, ('dp', 'context')), may hold values from 0 to 31, all different within a row; in each aligned block of 128 rows (0 to 127, 128 to 255, ..., all dimensions but the last counted through in order) at most 48 rows name the same one
- norm_attn: bfloat16 [1, 1024], P(None, ('dp', 'context')), may hold values from 0.5 to 1.5
- w_query: bfloat16 [1, 1024, 1024], P(None, ('dp', 'context'), 'tensor'), may hold values from -0.1875 to 0.1875
- w_key: bfloat16 [1, 1024, 512], P(None, ('dp', 'context'), 'tensor'), may hold values from -0.1875 to 0.1875
- w_value: bfloat16 [1, 1024, 512], P(None, ('dp', 'context'), 'tensor'), may hold values from -0.1875 to 0.1875
- w_out: bfloat16 [1, 1024, 1024], P(None, 'tensor', ('dp', 'context')), may hold values from -6 to 6
- norm_ffn: bfloat16 [1, 1024], P(None, ('dp', 'context')), may hold values from 0.5 to 1.5
- w_router: bfloat16 [1, 1024, 32], P(None, ('dp', 'context')), may hold values from -0.09375 to 0.09375
- w_gate: bfloat16 [1, 32, 1024, 512], P(None, 'context', 'dp', 'tensor'), may hold values from -0.1875 to 0.1875
- w_up: bfloat16 [1, 32, 1024, 512], P(None, 'context', 'dp', 'tensor'), may hold values from -0.1875 to 0.1875
- w_down: bfloat16 [1, 32, 512, 1024], P(None, 'context', 'tensor', 'dp'), may hold values from -6 to 6
- cotangent: bfloat16 [4096, 1024], P(('dp', 'context')), may hold values from -6 to 6
Outputs:
- hidden_out: bfloat16 [4096, 1024], P(('dp', 'context'))
- input_grad: float32 [4096, 1024], P(('dp', 'context'))
- norm_attn_grad: float32 [1, 1024], P(None, ('dp', 'context'))
- w_query_grad: float32 [1, 1024, 1024], P(None, ('dp', 'context'), 'tensor')
- w_key_grad: float32 [1, 1024, 512], P(None, ('dp', 'context'), 'tensor')
- w_value_grad: float32 [1, 1024, 512], P(None, ('dp', 'context'), 'tensor')
- w_out_grad: float32 [1, 1024, 1024], P(None, 'tensor', ('dp', 'context'))
- norm_ffn_grad: float32 [1, 1024], P(None, ('dp', 'context'))
- w_router_grad: float32 [1, 1024, 32], P(None, ('dp', 'context'))
- w_gate_grad: float32 [1, 32, 1024, 512], P(None, 'context', 'dp', 'tensor')
- w_up_grad: float32 [1, 32, 1024, 512], P(None, 'context', 'dp', 'tensor')
- w_down_grad: float32 [1, 32, 512, 1024], P(None, 'context', 'tensor', 'dp')
The draws below stay inside these ranges and needn't reach their ends.
Inputs may be any that keep to these rules, and one draw needn't show every extreme that they name: `segments`: along a sequence the numbers never fall; every number of 0 to 3 occurs; one document of each sequence holds 1921 tokens. `routes`: each row names 8 different experts. Within the 128 rows of one device of one layer no expert is named more than 48 times, a bound that some block reaches.
All inputs are finite; a program needn't handle non-finite values.
Results may differ from the reference program's by a relative error of at most 0.035.
Values may be sent and summed in bfloat16 or wider, within the bound.
A program may use at most 128 MiB of HBM per device.

```python
import math
import jax
import jax.numpy as jnp
import numpy as np
from jax import lax

D = 1024
HEADS = 16
KV_HEADS = 8
HEAD = 64
FF = 512
TOP = 8
LAYERS = 1
DOCS = 4
EXPERTS = 32
SEQ = 2048
LOCAL = 128
SEQS = 2
TOKENS = 4096
CAP = 48
N_DP = 2
N_CONTEXT = 16
N_TENSOR = 4


def shard_levels(own_key, shape, pieces, low, high):
    def one(axis_at, blocks):
        steps = jax.random.uniform(jax.random.fold_in(jax.random.fold_in(own_key, 6), axis_at), (blocks,), jnp.float32, low / len(pieces), high / len(pieces))
        return jnp.repeat(jnp.exp(steps), shape[axis_at] // blocks).reshape((-1,) + (1,) * (len(shape) - axis_at - 1))

    factor_of = one(*pieces[0])
    for cut in pieces[1:]:
        factor_of = factor_of * one(*cut)
    return factor_of


def split_up(number_of, total, most, skew):
    loads = [(1 << 20) // math.isqrt(standing ** skew) + 1 for standing in range(2, number_of + 1)]
    rest, counts = total - most - (number_of - 1), [1] * (number_of - 1)
    while rest > 0:
        free = [i for i in range(number_of - 1) if counts[i] < most]
        mass, left = sum([loads[i] for i in free]), rest
        for i in free:
            more = min(most - counts[i], max(1, left * loads[i] // mass), rest)
            counts[i] = counts[i] + more
            rest = rest - more
    return np.array([most] + counts)


def uneven(stream_key, amount, total, reach, lean):
    if amount == 2:
        one = jax.random.randint(stream_key, (), max(1, total - reach), min(reach, total - 1) + 1)
        return jnp.stack([one, total - one])
    tallies = jnp.asarray(split_up(amount, total, reach, lean), jnp.int32)
    pairs = (amount - 1) // 2
    source_of, taker = tallies[1:1 + 2 * pairs:2], tallies[2:2 + 2 * pairs:2]
    slack = jnp.minimum(source_of - 1, reach - taker)
    passed = jax.random.randint(jax.random.fold_in(stream_key, 1), (pairs,), 0, 1 << 20) % (slack + 1)
    tallies = tallies.at[1:1 + 2 * pairs:2].set(source_of - passed).at[2:2 + 2 * pairs:2].set(taker + passed)
    return tallies[jax.random.permutation(jax.random.fold_in(stream_key, 2), amount)]


def deal_out(key, own, number, rows, count, top, most, lean):
    order = jax.random.permutation(key, count)
    heavy_load, common = load_shares(count, rows * top, most, lean, True), load_shares(count, rows * top, most, lean, False)
    places = jnp.arange(count)

    def named(lengths, turn):
        used = int((lengths > 0).sum())
        fixed = max(1, used // 4)
        shifted = fixed + (places - fixed + turn * (used - fixed)) % max(1, count - fixed)
        return jnp.zeros((count,), jnp.int32).at[order[jnp.where(places < fixed, places, shifted)]].set(jnp.asarray(lengths, jnp.int32))

    lengths = jnp.where(number % 4 == 0, named(heavy_load, number // 4), named(common, number - number // 4 - 1))
    mixed = jax.random.permutation(jax.random.fold_in(own, 3), count)
    donor, receiver = mixed[0:count // 2 * 2:2], mixed[1:count // 2 * 2:2]
    room = jnp.minimum(lengths[donor] - 1, most - lengths[receiver]) // 2
    room = jnp.where((donor == order[0]) | (receiver == order[0]) | (lengths[receiver] == 0), 0, jnp.maximum(room, 0))
    shifted = jax.random.randint(jax.random.fold_in(own, 4), (count // 2,), 0, 1 << 20) % (room + 1)
    lengths = lengths.at[donor].add(-shifted).at[receiver].add(shifted)
    labels = jnp.searchsorted(jnp.cumsum(lengths), jnp.arange(rows * top), side="right").astype(jnp.int32)
    listing = labels.reshape(top, rows).T
    listing = listing[jax.random.permutation(jax.random.fold_in(own, 1), rows)]
    turn = jax.random.randint(jax.random.fold_in(own, 2), (rows, 1), 0, top)
    return jnp.take_along_axis(listing, (jnp.arange(top)[None, :] + turn) % top, axis=1)


def load_shares(count, total, most, skew, full):
    loads = [(1 << 20) // math.isqrt(rank ** skew) + 1 for rank in range(1, count + 1)]
    largest = most if full else min(most, max(-(-total // count), total * loads[0] // sum(loads)))
    least = 1 if total - largest >= count - 1 else 0
    given, surplus = [largest] + [least] * (count - 1), total - largest - least * (count - 1)
    while surplus > 0:
        free = [i for i in range(1, count) if given[i] < largest] or [i for i in range(1, count) if given[i] < most]
        pool, remaining = sum([loads[i] for i in free]), surplus
        for i in free:
            extra = min(most - given[i], max(1, remaining * loads[i] // pool), surplus)
            given[i] = given[i] + extra
            surplus = surplus - extra
    return np.array(given)


def gaussian(rng, shape, scale, most, split=(), kind=jnp.bfloat16):
    values = jax.random.normal(rng, shape, jnp.float32) * scale
    if len(split) > 0:
        values = shard_levels(rng, shape, split, -0.22, 0.18) * values
    return jnp.clip(values, min=-most, max=most).astype(kind)


def setup_inputs(seed: int = 0) -> dict:
    splits = jax.random.split(jax.random.key(seed), 15)
    hidden_in = gaussian(splits[0], (TOKENS, D), 1.0, 6.0, ((0, 32),))
    segments = jax.vmap(lambda own: jnp.searchsorted(jnp.cumsum(uneven(own, DOCS, SEQ, SEQ - LOCAL + 1, 0)), jnp.arange(SEQ), side="right"))(jax.random.split(splits[1], SEQS)).reshape((SEQS, SEQ)).astype(jnp.int32)
    routes_keys = jax.random.split(jax.random.fold_in(splits[2], 1), LAYERS * TOKENS // LOCAL)
    routes_turns = jax.random.permutation(jax.random.fold_in(splits[2], 3), LAYERS * TOKENS // LOCAL)
    routes = jax.vmap(lambda own, number: deal_out(jax.random.fold_in(splits[2], 2), own, number, LOCAL, EXPERTS, TOP, CAP, 2))(routes_keys, routes_turns).reshape((LAYERS, TOKENS, TOP))
    norm_attn = jnp.clip(1.0 + 0.1 * jax.random.normal(splits[3], (LAYERS, D), jnp.float32), 0.5, 1.5).astype(jnp.bfloat16)
    w_query = gaussian(splits[4], (LAYERS, D, HEADS * HEAD), D ** -0.5, 0.1875, ((1, 32), (2, 4)))
    w_key = gaussian(splits[5], (LAYERS, D, KV_HEADS * HEAD), D ** -0.5, 0.1875, ((1, 32), (2, 4)))
    w_value = gaussian(splits[6], (LAYERS, D, KV_HEADS * HEAD), D ** -0.5, 0.1875, ((1, 32), (2, 4)))
    w_out = gaussian(splits[7], (LAYERS, HEADS * HEAD, D), (max(1, HEADS * HEAD // 1024)) ** -0.5, 6.0, ((1, 4), (2, 32)))
    norm_ffn = jnp.clip(1.0 + 0.1 * jax.random.normal(splits[8], (LAYERS, D), jnp.float32), 0.5, 1.5).astype(jnp.bfloat16)
    w_router = gaussian(splits[9], (LAYERS, D, EXPERTS), (4 * D) ** -0.5, 0.09375, ((1, 32),))
    w_gate = gaussian(splits[10], (LAYERS, EXPERTS, D, FF), D ** -0.5, 0.1875, ((1, 16), (2, 2), (3, 4)))
    w_up = gaussian(splits[11], (LAYERS, EXPERTS, D, FF), D ** -0.5, 0.1875, ((1, 16), (2, 2), (3, 4)))
    w_down = gaussian(splits[12], (LAYERS, EXPERTS, FF, D), (max(1, FF // 512)) ** -0.5, 6.0, ((1, 16), (2, 4), (3, 2)))
    cotangent = gaussian(splits[13], (TOKENS, D), 1.0, 6.0, ((0, 32),))
    return {"hidden_in": hidden_in, "segments": segments, "routes": routes, "norm_attn": norm_attn, "w_query": w_query, "w_key": w_key, "w_value": w_value, "w_out": w_out, "norm_ffn": norm_ffn, "w_router": w_router, "w_gate": w_gate, "w_up": w_up, "w_down": w_down, "cotangent": cotangent}


EPS = 1e-06
NEG = -1e+30
HIGHEST = lax.Precision.HIGHEST

@jax.custom_vjp
def low(v):
    return lax.optimization_barrier(v.astype(jnp.bfloat16)).astype(jnp.float32)

@jax.custom_vjp
def low_back(v):
    return v

def low_keep(v):
    return (low(v), None)

def low_pass(kept, grad):
    return (grad,)

def back_keep(v):
    return (v, None)

def back_low(kept, grad):
    return (low(grad),)
low.defvjp(low_keep, low_pass)
low_back.defvjp(back_keep, back_low)

def product(left, right):
    return jnp.dot(left, right, precision=HIGHEST, preferred_element_type=jnp.float32)

def rms_norm(values, gain):
    return values * lax.rsqrt(lax.optimization_barrier(jnp.mean(values * values, axis=-1, keepdims=True)) + EPS) * gain

def rotary_tables(positions, width):
    half = width // 2
    rates = jnp.exp(jnp.arange(half, dtype=jnp.float32) * (-2.0 * math.log(10000.0) / width))
    angles = positions.astype(jnp.float32)[:, None] * rates[None, :]
    return (jnp.cos(angles), jnp.sin(angles))

def rotate(values, cosine, sine):
    half = values.shape[-1] // 2
    first = values[..., :half]
    second = values[..., half:]
    cosine = cosine[:, None, :]
    sine = sine[:, None, :]
    return jnp.concatenate([first * cosine - second * sine, second * cosine + first * sine], axis=-1)

def doc_positions(seg_row):
    index = jnp.arange(seg_row.shape[0], dtype=jnp.int32)
    fresh = jnp.concatenate([jnp.ones((1,), jnp.bool_), seg_row[1:] != seg_row[:-1]])
    starts = lax.cummax(jnp.where(fresh, index, jnp.zeros_like(index)), axis=0)
    return index - starts

def route_slots(route_block):
    flat = route_block.reshape(-1)
    onehot = (flat[:, None] == jnp.arange(EXPERTS, dtype=jnp.int32)[None, :]).astype(jnp.int32)
    before = jnp.cumsum(onehot, axis=0) - onehot
    slot = lax.optimization_barrier(jnp.sum(before * onehot, axis=1))
    return (flat * CAP + slot).astype(jnp.int32)

def slot_tables(slot_of_route):
    source = jnp.arange(slot_of_route.shape[0], dtype=jnp.int32) // TOP
    owner_rows = jnp.zeros((EXPERTS * CAP,), jnp.int32).at[slot_of_route].set(source)
    filled = jnp.zeros((EXPERTS * CAP,), jnp.float32).at[slot_of_route].set(1.0)
    return (owner_rows, filled)

def take_rows(table, index):
    return table[index]

def attend_sequence(items):
    queries, keys_all, values_all, seg_row = items
    block = min(512, SEQ)
    key_index = jnp.arange(SEQ, dtype=jnp.int32)

    def one_block(start):
        rows = lax.dynamic_slice_in_dim(queries, start, block, 0)
        row_seg = lax.dynamic_slice_in_dim(seg_row, start, block, 0)
        row_index = start + jnp.arange(block, dtype=jnp.int32)
        scores = low_back(jnp.einsum('qhgd,khd->hgqk', rows, keys_all, precision=HIGHEST))
        allowed = (row_seg[:, None] == seg_row[None, :]) & (key_index[None, :] <= row_index[:, None])
        scores = jnp.where(allowed, scores, NEG)
        weights = jax.nn.softmax(scores, axis=-1)
        return jnp.einsum('hgqk,khd->qhgd', low(weights), values_all, precision=HIGHEST)
    starts = jnp.arange(SEQ // block, dtype=jnp.int32) * block
    result = lax.map(jax.checkpoint(one_block), starts)
    return result.reshape(SEQ, -1)

def reference(hidden_in, segments, routes, norm_attn, w_query, w_key, w_value, w_out, norm_ffn, w_router, w_gate, w_up, w_down, cotangent):
    blocks = N_DP * N_CONTEXT
    group_size = HEADS // KV_HEADS
    slice_width = FF // N_TENSOR
    positions = jax.vmap(doc_positions)(segments).reshape(TOKENS)
    cosine, sine = rotary_tables(positions, HEAD)
    slot_of_route = jax.vmap(route_slots)(routes.reshape(LAYERS * blocks, LOCAL, TOP))
    token_of_slot, filled = jax.vmap(slot_tables)(slot_of_route)
    slot_of_route = slot_of_route.reshape(LAYERS, blocks, LOCAL * TOP)
    token_of_slot = token_of_slot.reshape(LAYERS, blocks, EXPERTS * CAP)
    filled = filled.reshape(LAYERS, blocks, EXPERTS * CAP)
    expert_ids = jnp.arange(EXPERTS, dtype=jnp.int32)

    def forward(start, params):
        residual = start
        for current in range(LAYERS):
            attn_gain, query_map, key_map, value_map, out_map, ffn_gain, router_map, gate_map, up_map, down_map = [item[current] for item in params]
            normed = low(rms_norm(residual, attn_gain))
            queries = rotate(low_back(product(normed, query_map)).reshape(TOKENS, HEADS, HEAD), cosine, sine)
            queries = low(queries * 0.125).reshape(SEQS, SEQ, KV_HEADS, group_size, HEAD)
            keys_all = low(rotate(low_back(product(normed, key_map)).reshape(TOKENS, KV_HEADS, HEAD), cosine, sine))
            keys_all = keys_all.reshape(SEQS, SEQ, KV_HEADS, HEAD)
            values_all = low(low_back(product(normed, value_map))).reshape(SEQS, SEQ, KV_HEADS, HEAD)
            attended = lax.map(attend_sequence, (queries, keys_all, values_all, segments)).reshape(TOKENS, HEADS * HEAD)
            attended = low_back(low(attended))
            hidden = residual + low_back(product(attended, out_map))
            normed_two = low(rms_norm(hidden, ffn_gain))
            logits = low_back(product(normed_two, router_map))
            probs = jax.nn.softmax(logits, axis=-1)
            chosen = (routes[current][:, :, None] == expert_ids[None, None, :]).astype(jnp.float32)
            gate_values = lax.optimization_barrier(jnp.sum(chosen * probs[:, None, :], axis=-1))
            rows = normed_two.reshape(blocks, LOCAL, D)
            buffer = jax.vmap(take_rows)(rows, token_of_slot[current]) * filled[current][:, :, None]
            buffer = buffer.reshape(blocks, EXPERTS, CAP, D)
            returned = jnp.zeros((blocks, EXPERTS, CAP, D), jnp.float32)
            for part in range(N_TENSOR):
                lower = part * slice_width
                inputs = low_back(buffer)
                gate_pre = low_back(jnp.einsum('becd,edf->becf', inputs, gate_map[:, :, lower:lower + slice_width], precision=HIGHEST))
                up_pre = low_back(jnp.einsum('becd,edf->becf', inputs, up_map[:, :, lower:lower + slice_width], precision=HIGHEST))
                inner = low(jax.nn.silu(gate_pre) * up_pre)
                partial_out = jnp.einsum('becf,efd->becd', inner, down_map[:, lower:lower + slice_width, :], precision=HIGHEST)
                returned = returned + low_back(low(partial_out))
            picked = jax.vmap(take_rows)(returned.reshape(blocks, EXPERTS * CAP, D), slot_of_route[current])
            picked = picked.reshape(TOKENS, TOP, D)
            residual = hidden + lax.optimization_barrier(jnp.sum(gate_values[:, :, None] * picked, axis=1))
        return residual
    params = (norm_attn.astype(jnp.float32), w_query.astype(jnp.float32), w_key.astype(jnp.float32), w_value.astype(jnp.float32), w_out.astype(jnp.float32), norm_ffn.astype(jnp.float32), w_router.astype(jnp.float32), w_gate.astype(jnp.float32), w_up.astype(jnp.float32), w_down.astype(jnp.float32))
    result, pullback = jax.vjp(forward, hidden_in.astype(jnp.float32), params)
    input_grad, grads = pullback(cotangent.astype(jnp.float32))
    return (result.astype(jnp.bfloat16), input_grad, grads[0], grads[1], grads[2], grads[3], grads[4], grads[5], grads[6], grads[7], grads[8], grads[9])
```

```python
import functools
import math

import jax
import jax.numpy as jnp
from jax import lax
from jax.experimental import pallas as pl
from jax.experimental.pallas import tpu as pltpu
from jax.sharding import PartitionSpec as P

HEAD = 64
EPS = 1e-06
NEG = -1e30
F32 = jnp.float32
BF16 = jnp.bfloat16
TAIL = 128
VMEM_BYTES = 60 * 1024 * 1024


def dot(a, b):
    return jnp.dot(a, b, preferred_element_type=F32)


def dot_nt(a, b):
    return lax.dot_general(a, b, (((1,), (1,)), ((), ())), preferred_element_type=F32)


def dot_tn(a, b):
    return lax.dot_general(a, b, (((0,), (0,)), ((), ())), preferred_element_type=F32)


def remote(src, dst, send_sem, recv_sem, device):
    return pltpu.make_async_remote_copy(
        src_ref=src,
        dst_ref=dst,
        send_sem=send_sem,
        recv_sem=recv_sem,
        device_id=device,
        device_id_type=pl.DeviceIdType.MESH,
    )


def loop(start, stop, step):
    def body(k, carry):
        step(k)
        return carry

    lax.fori_loop(start, stop, body, 0)


class Gather:
    def __init__(self, count, me, core, peer, sibling, table, sems):
        self.count, self.me, self.core = count, me, core
        self.peer, self.sibling, self.table, self.sems = peer, sibling, table, sems

    def far(self, k):
        mine = self.table.at[self.me, self.core]
        return remote(mine, mine, self.sems.at[0, k], self.sems.at[1, k], self.peer(k))

    def near(self, k):
        chunk = self.table.at[lax.rem(self.me + self.count - k, self.count), self.core]
        return remote(chunk, chunk, self.sems.at[2, k], self.sems.at[3, k], self.sibling)

    def start(self):
        loop(1, self.count, lambda k: self.far(k).start())
        self.near(0).start()

    def forward(self):
        def step(k):
            self.far(k).wait_recv()
            self.near(k).start()

        loop(1, self.count, step)

    def finish(self):
        loop(0, self.count, lambda k: self.near(k).wait_recv())

    def drain(self):
        loop(1, self.count, lambda k: self.far(k).wait_send())
        loop(0, self.count, lambda k: self.near(k).wait_send())


class Scatter:
    def __init__(self, count, me, core, peer, sibling, parts, half, landed, sems):
        self.count, self.me, self.core = count, me, core
        self.peer, self.sibling = peer, sibling
        self.parts, self.half, self.landed, self.sems = parts, half, landed, sems

    def near(self):
        return remote(
            self.parts.at[:, 1 - self.core],
            self.half,
            self.sems.at[0, 0],
            self.sems.at[1, 0],
            self.sibling,
        )

    def far(self, k):
        there = lax.rem(self.me + k, self.count)
        return remote(
            self.half.at[there],
            self.landed.at[k],
            self.sems.at[0, k],
            self.sems.at[1, k],
            self.peer(k),
        )

    def start(self):
        self.near().start()

    def send(self):
        self.near().wait_recv()

        def add(there):
            mine = self.parts[there, self.core].astype(F32)
            self.half[there] = (mine + self.half[there].astype(F32)).astype(BF16)

        def step(k):
            add(lax.rem(self.me + k, self.count))
            self.far(k).start()

        loop(1, self.count, step)
        add(self.me)

    def total(self):
        def step(k, acc):
            self.far(k).wait_recv()
            return acc + self.landed[k].astype(F32)

        return lax.fori_loop(1, self.count, step, self.half[self.me].astype(F32))

    def drain(self):
        self.near().wait_send()
        loop(1, self.count, lambda k: self.far(k).wait_send())


def layer(
    sizes,
    xin,
    cot,
    segc,
    rts,
    wpk,
    wgi,
    wui,
    wdi,
    o_h,
    o_ig,
    o_w,
    o_t,
    o_wg,
    o_wu,
    o_wd,
    wall,
    cotall,
    ball,
    kv,
    wg,
    wu,
    wd,
    a_ref,
    qs,
    p_ref,
    ds_ref,
    o_ref,
    part,
    ybuf,
    hall,
    dall,
    igall,
    dgp_ref,
    dup_ref,
    ug_ref,
    dbs,
    dbs_half,
    dbs_land,
    ys,
    ys_half,
    ys_land,
    gg,
    gu,
    gd,
    gg_land,
    gu_land,
    gd_land,
    dos,
    dq_ref,
    dkv,
    dkv_half,
    dkv_land,
    wgs,
    wgs_half,
    wgs_land,
    tail_y,
    s_wall,
    s_cot,
    s_ball,
    s_kv,
    s_exp,
    s_y1,
    s_dbs,
    s_ys,
    s_grad,
    s_dall,
    s_dkv,
    s_y2,
    s_wgs,
    s_fin,
):
    n_dp, n_ctx, n_ten = sizes
    nj = n_ctx // 2
    nq = n_dp * nj
    rows, width = xin.shape
    seq = n_ctx * rows
    quarter = rows // n_ten
    d, c, r = lax.axis_index("dp"), lax.axis_index("context"), lax.axis_index("tensor")
    core, j = lax.rem(c, 2), c // 2
    q = d * nj + j

    def at(dp, context, tensor):
        return {"dp": dp, "context": context, "tensor": tensor}

    def plane(k):
        there = lax.rem(q + k, nq)
        return at(there // nj, lax.rem(there, nj) * 2 + core, r)

    def along(k):
        return at(d, lax.rem(j + k, nj) * 2 + core, r)

    def tensor(k):
        return at(d, c, lax.rem(r + k, n_ten))

    def holder(o):
        return at(lax.rem(d + o // n_ten, n_dp), c, lax.rem(r + lax.rem(o, n_ten), n_ten))

    sibling = at(d, c + 1 - 2 * core, r)

    barrier = pltpu.get_barrier_semaphore()

    def greet(device):
        pl.semaphore_signal(barrier, inc=1, device_id=device, device_id_type=pl.DeviceIdType.MESH)

    loop(1, nq, lambda k: greet(plane(k)))
    greet(sibling)
    loop(1, n_dp * n_ten, lambda o: greet(holder(o)))
    pl.semaphore_wait(barrier, nq + n_dp * n_ten - 1)

    wide = pl.ds(pl.multiple_of(r * quarter, quarter), quarter)

    g_wall = Gather(nq, q, core, plane, sibling, wall, s_wall)
    wall[q, core] = wpk[...]
    g_wall.start()

    half_d, cut = wgi.shape[1], wgi.shape[2]

    def d_rows(dp):
        return pl.ds(pl.multiple_of(dp * half_d, half_d), half_d)

    def f_rows(ten):
        return pl.ds(pl.multiple_of(ten * cut, cut), cut)

    def expert_copies(o):
        there = lax.rem(d + o // n_ten, n_dp)
        place = wg.at[d_rows(d), f_rows(r)]
        place_u = wu.at[d_rows(d), f_rows(r)]
        place_d = wd.at[f_rows(r), d_rows(d)]
        return (
            remote(wgi.at[there], place, s_exp.at[0, o], s_exp.at[1, o], holder(o)),
            remote(wui.at[there], place_u, s_exp.at[2, o], s_exp.at[3, o], holder(o)),
            remote(wdi.at[there], place_d, s_exp.at[4, o], s_exp.at[5, o], holder(o)),
        )

    def start_experts(o):
        for copy in expert_copies(o):
            copy.start()

    x = xin[...].astype(F32)
    inv = lax.rsqrt(jnp.mean(x * x, axis=-1, keepdims=True) + EPS)
    lane = lax.broadcasted_iota(jnp.int32, (1, 128), 1)
    low_half = lax.rem(lane, HEAD) < HEAD // 2
    group_of = lane // HEAD
    rate = jnp.exp(
        lax.rem(lane, HEAD // 2).astype(F32) * (-2.0 * math.log(10000.0) / HEAD)
    )
    row_index = c * rows + lax.broadcasted_iota(jnp.int32, (rows, 1), 0)
    angle = row_index.astype(F32) * rate
    cosine = jnp.cos(angle)
    sine = jnp.where(low_half, -1.0, 1.0) * jnp.sin(angle)

    def partner(z):
        return jnp.where(
            low_half, pltpu.roll(z, 128 - HEAD // 2, 1), pltpu.roll(z, HEAD // 2, 1)
        )

    def rope(z):
        return z * cosine + partner(z) * sine

    def unrope(z):
        return z * cosine - partner(z) * sine

    wg[d_rows(d), f_rows(r)] = wgi[d]
    wu[d_rows(d), f_rows(r)] = wui[d]
    wd[f_rows(r), d_rows(d)] = wdi[d]
    g_cot = Gather(nq, q, core, plane, sibling, cotall, s_cot)
    cotall[q, core] = cot[wide]

    g_wall.forward()
    g_wall.finish()
    loop(1, n_dp * n_ten, start_experts)
    g_cot.start()

    tails = wall[:, :, :, 768:896].reshape(width, TAIL)
    gains = tails.astype(F32).T
    attn_gain, ffn_gain = gains[32:33], gains[33:34]
    a_ref[...] = (x * inv * attn_gain).astype(BF16)

    qkv = dot(a_ref[...], wall[:, :, :, 0:512].reshape(width, 512))
    for t in range(2):
        turned = rope(qkv[:, 128 * t : 128 * t + 128]) * 0.125
        for g in range(2):
            qs[2 * t + g] = jnp.where(group_of == g, turned, 0.0).astype(BF16)
    kv[j, core, :, 0:128] = rope(qkv[:, 256:384]).astype(BF16)
    kv[j, core, :, 128:256] = qkv[:, 384:512].astype(BF16)
    g_kv = Gather(nj, j, core, along, sibling, kv, s_kv)
    g_kv.start()

    numbers = wall[pl.ds(d * nj, nj), :, :, 768:896].reshape(nj * 64, TAIL).astype(F32)
    held = jnp.where((lane >= 34) & (lane < 38), numbers, 1e9)
    mine = segc[...]
    first = jnp.zeros((rows, 1), F32)
    for s in range(1, 4):
        below = jnp.sum(jnp.where(held < s - 0.5, 1.0, 0.0), axis=0, keepdims=True)
        below = jnp.sum(below, axis=1, keepdims=True)
        first = jnp.where(mine == s, below, first)
    first = first.astype(jnp.int32)
    columns = lax.broadcasted_iota(jnp.int32, (rows, seq), 1)
    allowed = (columns >= first) & (columns <= row_index)

    g_kv.forward()
    g_kv.finish()

    o_ref[...] = jnp.zeros_like(o_ref)

    def head_forward(i):
        scores = dot_nt(qs[i], kv[:, :, :, 0:128].reshape(seq, 128))
        scores = jnp.where(allowed, scores, NEG)
        top = jnp.max(scores, axis=-1, keepdims=True)
        expo = jnp.where(allowed, jnp.exp(scores - top), 0.0)
        weights = (expo * (1.0 / jnp.sum(expo, axis=-1, keepdims=True))).astype(BF16)
        p_ref[i] = weights
        out = dot(weights, kv[:, :, :, 128:256].reshape(seq, 128))
        o_ref[i // 2] += jnp.where(group_of == lax.rem(i, 2), out, 0.0)

    loop(0, 4, head_forward)
    o_low = jnp.concatenate([o_ref[0], o_ref[1]], axis=1).astype(BF16)
    w_out = wall[:, :, :, 512:768].reshape(width, 256)
    part[0] = dot_nt(o_low, w_out).astype(BF16).reshape(n_ten, quarter, width)

    def tensor_copy(which, sems, k):
        return remote(
            part.at[which, lax.rem(r + k, n_ten)],
            ybuf.at[which, k],
            sems.at[0, k],
            sems.at[1, k],
            tensor(k),
        )

    loop(1, n_ten, lambda k: tensor_copy(0, s_y1, k).start())
    g_cot.forward()
    hidden = xin[wide].astype(F32) + part[0, r].astype(F32)
    for k in range(1, n_ten):
        tensor_copy(0, s_y1, k).wait_recv()
        hidden = hidden + ybuf[0, k].astype(F32)

    inv_two = lax.rsqrt(jnp.mean(hidden * hidden, axis=-1, keepdims=True) + EPS)
    b_own = (hidden * inv_two * ffn_gain).astype(BF16)
    logits = jnp.where(lane < 32, dot(b_own, tails), NEG)
    expo = jnp.exp(logits - jnp.max(logits, axis=-1, keepdims=True))
    probs = expo / jnp.sum(expo, axis=-1, keepdims=True)
    routed = jnp.zeros((quarter, 128), F32)
    routes = rts[wide]
    for k in range(routes.shape[1]):
        routed = routed + jnp.where(routes[:, k : k + 1] == lane, 1.0, 0.0)
    gates = probs * routed
    gates_high = gates.astype(BF16).astype(F32)
    ball[q, core, :, 0:width] = b_own
    ball[q, core, :, width : width + TAIL] = (
        gates_high + pltpu.roll(gates - gates_high, 32, 1)
    ).astype(BF16)
    g_ball = Gather(nq, q, core, plane, sibling, ball, s_ball)
    g_ball.start()
    g_ball.forward()
    g_cot.finish()

    def wait_experts(o):
        for copy in expert_copies(o):
            copy.wait_recv()

    loop(1, n_dp * n_ten, wait_experts)
    g_ball.finish()

    expert = 2 * c + d
    gate_lane = (lane == expert) | (lane == expert + 32)
    block = 8 * quarter
    steps = nq // 4

    def tokens(ref, i, cut_at, cut_to):
        return ref[pl.ds(4 * i, 4), :, :, cut_at:cut_to].reshape(block, cut_to - cut_at)

    def rows_of(i):
        return pl.ds(pl.multiple_of(i * block, block), block)

    def expert_block(i):
        b = tokens(ball, i, 0, width)
        packed = tokens(ball, i, width, width + TAIL).astype(F32)
        gate = jnp.sum(jnp.where(gate_lane, packed, 0.0), axis=-1, keepdims=True)
        gp = dot(b, wg[...])
        up = dot(b, wu[...])
        du = dot_nt(tokens(cotall, i, 0, width), wd[...])
        sigma = 1.0 / (1.0 + jnp.exp(-gp))
        silu = gp * sigma
        u = (silu * up).astype(BF16).astype(F32)
        dgate = jnp.sum(du * u, axis=-1, keepdims=True)
        du = gate * du
        dgp = (du * up * sigma * (1.0 + gp * (1.0 - sigma))).astype(BF16)
        dup = (du * silu).astype(BF16)
        dgp_ref[rows_of(i)] = dgp
        dup_ref[rows_of(i)] = dup
        ug_ref[rows_of(i)] = (gate * u).astype(BF16)
        db = dot_nt(dgp, wg[...]) + dot_nt(dup, wu[...])
        dbs[pl.ds(4 * i, 4), :, :, 0:width] = db.astype(BF16).reshape(4, 2, quarter, width)
        dbs[pl.ds(4 * i, 4), :, :, width : width + TAIL] = (
            jnp.where(lane == expert, dgate, 0.0).astype(BF16).reshape(4, 2, quarter, TAIL)
        )

    loop(0, steps, expert_block)
    x_dbs = Scatter(nq, q, core, plane, sibling, dbs, dbs_half, dbs_land, s_dbs)
    x_dbs.start()

    def down_block(i):
        y = dot(ug_ref[rows_of(i)], wd[...])
        ys[pl.ds(4 * i, 4)] = y.astype(BF16).reshape(4, 2, quarter, width)

    loop(0, steps, down_block)
    x_dbs.send()
    x_ys = Scatter(nq, q, core, plane, sibling, ys, ys_half, ys_land, s_ys)
    x_ys.start()

    all_cot = cotall[...].reshape(nq * 2 * quarter, width)
    all_b = ball[:, :, :, 0:width].reshape(nq * 2 * quarter, width)
    gd[...] = dot_tn(ug_ref[...], all_cot).astype(BF16)
    gg[...] = dot_tn(all_b, dgp_ref[...]).astype(BF16)
    gu[...] = dot_tn(all_b, dup_ref[...]).astype(BF16)

    def grad_copies(o):
        dp, ten = lax.rem(d + o // n_ten, n_dp), lax.rem(r + lax.rem(o, n_ten), n_ten)
        return (
            remote(
                gg.at[d_rows(dp), f_rows(ten)], gg_land.at[o], s_grad.at[0, o], s_grad.at[1, o],
                holder(o),
            ),
            remote(
                gu.at[d_rows(dp), f_rows(ten)], gu_land.at[o], s_grad.at[2, o], s_grad.at[3, o],
                holder(o),
            ),
            remote(
                gd.at[f_rows(ten), d_rows(dp)], gd_land.at[o], s_grad.at[4, o], s_grad.at[5, o],
                holder(o),
            ),
        )

    def start_grads(o):
        for copy in grad_copies(o):
            copy.start()

    summed = x_dbs.total()
    x_ys.send()
    dprobs = routed * summed[:, width : width + TAIL]
    dlogits = probs * (dprobs - jnp.sum(probs * dprobs, axis=-1, keepdims=True))
    dlogits = jnp.where(lane < 32, dlogits, 0.0).astype(BF16)
    db = summed[:, 0:width] + dot_nt(dlogits, tails)
    w_db = db * ffn_gain
    grad_hidden = (
        cot[wide].astype(F32)
        + inv_two * w_db
        - hidden * inv_two**3 * (jnp.sum(w_db * hidden, axis=-1, keepdims=True) / width)
    )
    ffn_gain_rows = (db * hidden * inv_two).astype(BF16)
    dall[r] = grad_hidden.astype(BF16)

    def spread(table, sems, k):
        mine = table.at[r]
        return remote(mine, mine, sems.at[0, k], sems.at[1, k], tensor(k))

    loop(1, n_ten, lambda k: spread(dall, s_dall, k).start())
    one_hot = lax.broadcasted_iota(jnp.int32, (rows, TAIL), 1)
    ones_ffn = jnp.where(one_hot[0:quarter] == 32, 1.0, 0.0).astype(BF16)
    ones_attn = jnp.where(one_hot == 33, 1.0, 0.0).astype(BF16)
    tail_grad = dot_tn(b_own, dlogits) + dot_tn(ffn_gain_rows, ones_ffn)
    loop(1, n_ten, lambda k: spread(dall, s_dall, k).wait_recv())

    d_attn = dall[...].reshape(rows, width)
    do = dot(d_attn, w_out).astype(BF16)
    loop(1, n_dp * n_ten, start_grads)
    for t in range(2):
        tile = do[:, 128 * t : 128 * t + 128].astype(F32)
        for g in range(2):
            dos[2 * t + g] = jnp.where(group_of == g, tile, 0.0).astype(BF16)

    dq_ref[...] = jnp.zeros_like(dq_ref)

    def head_backward(i):
        go = dos[i]
        delta = jnp.sum(go.astype(F32) * o_ref[i // 2], axis=-1, keepdims=True)
        dp = dot_nt(go, kv[:, :, :, 128:256].reshape(seq, 128))
        grad = (p_ref[i].astype(F32) * (dp - delta)).astype(BF16)
        ds_ref[i] = grad
        dq = dot(grad, kv[:, :, :, 0:128].reshape(seq, 128))
        dq_ref[i // 2] += jnp.where(group_of == lax.rem(i, 2), dq, 0.0)

    loop(0, 4, head_backward)
    all_q = qs[...].reshape(4 * rows, 128)
    all_do = dos[...].reshape(4 * rows, 128)
    for i in range(4):
        span = slice(i * (seq // 4), (i + 1) * (seq // 4))
        place = slice(i * (nj // 4), (i + 1) * (nj // 4))
        dk = dot_tn(ds_ref[:, :, span].reshape(4 * rows, seq // 4), all_q)
        dv = dot_tn(p_ref[:, :, span].reshape(4 * rows, seq // 4), all_do)
        dkv[place, :, :, 0:128] = dk.astype(BF16).reshape(nj // 4, 2, rows, 128)
        dkv[place, :, :, 128:256] = dv.astype(BF16).reshape(nj // 4, 2, rows, 128)
    x_dkv = Scatter(nj, j, core, along, sibling, dkv, dkv_half, dkv_land, s_dkv)
    x_dkv.start()

    def to_rows(grad):
        return grad.astype(BF16).reshape(nq, 2, 32, grad.shape[1])

    a_low = a_ref[...]
    wgs[:, :, :, 512:768] = to_rows(dot_tn(d_attn, o_low))
    x_dkv.send()
    dq_lin = jnp.concatenate([unrope(dq_ref[0]), unrope(dq_ref[1])], axis=1) * 0.125
    dq_lin = dq_lin.astype(BF16)
    wgs[:, :, :, 0:256] = to_rows(dot_tn(a_low, dq_lin))
    da = dot_nt(dq_lin, wall[:, :, :, 0:256].reshape(width, 256))
    grad_kv = x_dkv.total()
    dkv_lin = jnp.concatenate([unrope(grad_kv[:, 0:128]), grad_kv[:, 128:256]], axis=1)
    dkv_lin = dkv_lin.astype(BF16)
    da = da + dot_nt(dkv_lin, wall[:, :, :, 256:512].reshape(width, 256))
    part[1] = da.astype(BF16).reshape(n_ten, quarter, width)
    loop(1, n_ten, lambda k: tensor_copy(1, s_y2, k).start())
    wgs[:, :, :, 256:512] = to_rows(dot_tn(a_low, dkv_lin))
    attn_gain_rows = (da * xin[...].astype(F32) * inv).astype(BF16)
    wgs[:, :, :, 768:896] = to_rows(tail_grad + dot_tn(attn_gain_rows, ones_attn))
    x_wgs = Scatter(nq, q, core, plane, sibling, wgs, wgs_half, wgs_land, s_wgs)
    x_wgs.start()

    hall[r] = (hidden + x_ys.total()).astype(BF16)
    loop(1, n_ten, lambda k: spread(hall, s_fin, k).start())

    grad_a = part[1, r].astype(F32)
    for k in range(1, n_ten):
        tensor_copy(1, s_y2, k).wait_recv()
        grad_a = grad_a + ybuf[1, k].astype(F32)
    x_own = xin[wide].astype(F32)
    inv_own = lax.rsqrt(jnp.mean(x_own * x_own, axis=-1, keepdims=True) + EPS)
    w_da = grad_a * attn_gain
    grad_x = (
        grad_hidden
        + inv_own * w_da
        - x_own * inv_own**3 * (jnp.sum(w_da * x_own, axis=-1, keepdims=True) / width)
    )
    igall[r] = grad_x.astype(BF16)

    def spread_ig(k):
        mine = igall.at[r]
        return remote(mine, mine, s_fin.at[2, k], s_fin.at[3, k], tensor(k))

    loop(1, n_ten, lambda k: spread_ig(k).start())
    x_wgs.send()

    def wait_grads(o):
        for copy in grad_copies(o):
            copy.wait_recv()

    loop(1, n_dp * n_ten, wait_grads)

    def reduce_grads(out, land, own):
        same = own
        for k in range(1, n_ten):
            same = same + land[k].astype(F32)
        out[d] = same
        other = land[n_ten].astype(F32)
        for k in range(1, n_ten):
            other = other + land[n_ten + k].astype(F32)
        out[1 - d] = other

    reduce_grads(o_wg, gg_land, gg[d_rows(d), f_rows(r)].astype(F32))
    reduce_grads(o_wu, gu_land, gu[d_rows(d), f_rows(r)].astype(F32))
    reduce_grads(o_wd, gd_land, gd[f_rows(r), d_rows(d)].astype(F32))

    loop(1, n_ten, lambda k: spread(hall, s_fin, k).wait_recv())
    o_h[...] = hall[...]
    loop(1, n_ten, lambda k: spread_ig(k).wait_recv())
    o_ig[...] = igall[...].astype(F32)

    grads = x_wgs.total()
    o_w[...] = grads[:, 0:768]
    tail_y[0] = grads[:, 768:896]

    def tail_copy(k):
        return remote(tail_y.at[0], tail_y.at[k], s_fin.at[4, k], s_fin.at[5, k], tensor(k))

    loop(1, n_ten, lambda k: tail_copy(k).start())
    tail_sum = grads[:, 768:896]
    for k in range(1, n_ten):
        tail_copy(k).wait_recv()
        tail_sum = tail_sum + tail_y[k]
    o_t[...] = tail_sum

    for gather in (g_wall, g_cot, g_kv, g_ball):
        gather.drain()
    for scatter in (x_dbs, x_ys, x_dkv, x_wgs):
        scatter.drain()

    def drain_tensor(k):
        tensor_copy(0, s_y1, k).wait_send()
        tensor_copy(1, s_y2, k).wait_send()
        spread(dall, s_dall, k).wait_send()
        spread(hall, s_fin, k).wait_send()
        spread_ig(k).wait_send()
        tail_copy(k).wait_send()

    loop(1, n_ten, drain_tensor)

    def drain_experts(o):
        for copy in expert_copies(o) + grad_copies(o):
            copy.wait_send()

    loop(1, n_dp * n_ten, drain_experts)


def call_layer(sizes, xin, cot, segc, rts, wpk, wgi, wui, wdi):
    n_dp, n_ctx, n_ten = sizes
    nj = n_ctx // 2
    nq = n_dp * nj
    rows, width = xin.shape
    seq = n_ctx * rows
    quarter = rows // n_ten
    half_d, cut = wgi.shape[1], wgi.shape[2]
    hidden_units = cut * n_ten
    packed = wpk.shape[1]
    all_rows = nq * 2 * quarter
    holders = n_dp * n_ten

    def shape(*dims, kind=F32):
        return jax.ShapeDtypeStruct(dims, kind)

    def low(*dims):
        return pltpu.VMEM(dims, BF16)

    def full(*dims):
        return pltpu.VMEM(dims, F32)

    def sems(*dims):
        return pltpu.SemaphoreType.DMA(dims)

    scratch = [
        low(nq, 2, 32, packed),
        low(nq, 2, quarter, width),
        low(nq, 2, quarter, width + TAIL),
        low(nj, 2, rows, 256),
        low(width, hidden_units),
        low(width, hidden_units),
        low(hidden_units, width),
        low(rows, width),
        low(4, rows, 128),
        low(4, rows, seq),
        low(4, rows, seq),
        full(2, rows, 128),
        low(2, n_ten, quarter, width),
        low(2, n_ten, quarter, width),
        low(n_ten, quarter, width),
        low(n_ten, quarter, width),
        low(n_ten, quarter, width),
        low(all_rows, hidden_units),
        low(all_rows, hidden_units),
        low(all_rows, hidden_units),
        low(nq, 2, quarter, width + TAIL),
        low(nq, quarter, width + TAIL),
        low(nq, quarter, width + TAIL),
        low(nq, 2, quarter, width),
        low(nq, quarter, width),
        low(nq, quarter, width),
        low(width, hidden_units),
        low(width, hidden_units),
        low(hidden_units, width),
        low(holders, half_d, cut),
        low(holders, half_d, cut),
        low(holders, cut, half_d),
        low(4, rows, 128),
        full(2, rows, 128),
        low(nj, 2, rows, 256),
        low(nj, rows, 256),
        low(nj, rows, 256),
        low(nq, 2, 32, packed),
        low(nq, 32, packed),
        low(nq, 32, packed),
        full(n_ten, 32, TAIL),
        sems(4, nq),
        sems(4, nq),
        sems(4, nq),
        sems(4, nj),
        sems(6, holders),
        sems(2, n_ten),
        sems(2, nq),
        sems(2, nq),
        sems(6, holders),
        sems(2, n_ten),
        sems(2, nj),
        sems(2, n_ten),
        sems(2, nq),
        sems(6, n_ten),
    ]
    flops = 2 * (9 * all_rows * width * hidden_units + 4 * rows * width * 768)
    return pl.pallas_call(
        functools.partial(layer, sizes),
        out_shape=(
            shape(n_ten, quarter, width, kind=BF16),
            shape(n_ten, quarter, width),
            shape(32, 768),
            shape(32, TAIL),
            shape(2, half_d, cut),
            shape(2, half_d, cut),
            shape(2, cut, half_d),
        ),
        in_specs=[pl.BlockSpec(memory_space=pltpu.VMEM)] * 8,
        out_specs=[pl.BlockSpec(memory_space=pltpu.VMEM)] * 7,
        scratch_shapes=scratch,
        compiler_params=pltpu.CompilerParams(
            collective_id=0, has_side_effects=True, vmem_limit_bytes=VMEM_BYTES
        ),
        cost_estimate=pl.CostEstimate(flops=flops, bytes_accessed=8 << 20, transcendentals=0),
    )(xin, cot, segc, rts, wpk, wgi, wui, wdi)


def swap_heads(table):
    a, b, c, d = [table[:, HEAD * i : HEAD * i + HEAD] for i in range(4)]
    return jnp.concatenate([a, c, b, d], axis=1)


def per_device(
    hidden_in,
    segments,
    routes,
    norm_attn,
    w_query,
    w_key,
    w_value,
    w_out,
    norm_ffn,
    w_router,
    w_gate,
    w_up,
    w_down,
    cotangent,
):
    sizes = (lax.axis_size("dp"), lax.axis_size("context"), lax.axis_size("tensor"))
    rows = hidden_in.shape[0]
    per_row = rows // 32
    packed = jnp.concatenate(
        [
            swap_heads(w_query[0]),
            w_key[0],
            w_value[0],
            swap_heads(w_out[0].T),
            w_router[0],
            norm_attn[0][:, None],
            norm_ffn[0][:, None],
            segments[0].reshape(32, per_row).astype(BF16),
            jnp.zeros((32, TAIL - 34 - per_row), BF16),
        ],
        axis=1,
    )
    out, grad, w_grads, tail, gate_grad, up_grad, down_grad = call_layer(
        sizes,
        hidden_in,
        cotangent,
        segments[0][:, None],
        routes[0],
        packed,
        w_gate[0],
        w_up[0],
        w_down[0],
    )
    return (
        out.reshape(hidden_in.shape),
        grad.reshape(hidden_in.shape),
        tail[:, 33][None],
        swap_heads(w_grads[:, 0:256])[None],
        w_grads[:, 256:384][None],
        w_grads[:, 384:512][None],
        swap_heads(w_grads[:, 512:768]).T[None],
        tail[:, 32][None],
        tail[:, 0:32][None],
        gate_grad[None],
        up_grad[None],
        down_grad[None],
    )


def solution(mesh):
    in_specs = (
        P(("dp", "context"), None),
        P("dp", "context"),
        P(None, ("dp", "context"), None),
        P(None, ("dp", "context")),
        P(None, ("dp", "context"), "tensor"),
        P(None, ("dp", "context"), "tensor"),
        P(None, ("dp", "context"), "tensor"),
        P(None, "tensor", ("dp", "context")),
        P(None, ("dp", "context")),
        P(None, ("dp", "context"), None),
        P(None, "context", "dp", "tensor"),
        P(None, "context", "dp", "tensor"),
        P(None, "context", "tensor", "dp"),
        P(("dp", "context"), None),
    )
    out_specs = (
        P(("dp", "context"), None),
        P(("dp", "context"), None),
        P(None, ("dp", "context")),
        P(None, ("dp", "context"), "tensor"),
        P(None, ("dp", "context"), "tensor"),
        P(None, ("dp", "context"), "tensor"),
        P(None, "tensor", ("dp", "context")),
        P(None, ("dp", "context")),
        P(None, ("dp", "context"), None),
        P(None, "context", "dp", "tensor"),
        P(None, "context", "dp", "tensor"),
        P(None, "context", "tensor", "dp"),
    )
    return jax.shard_map(
        per_device, mesh=mesh, in_specs=in_specs, out_specs=out_specs, check_vma=False
    )
```

```python
import functools
import math

import jax
import jax.numpy as jnp
from jax import lax
from jax.experimental import pallas as pl
from jax.experimental.pallas import tpu as pltpu
from jax.sharding import PartitionSpec as P

HEAD = 64
EPS = 1e-06
NEG = -1e30
F32 = jnp.float32
BF16 = jnp.bfloat16
TAIL = 128
VMEM_BYTES = 60 * 1024 * 1024


def dot(a, b):
    return jnp.dot(a, b, preferred_element_type=F32)


def dot_nt(a, b):
    return lax.dot_general(a, b, (((1,), (1,)), ((), ())), preferred_element_type=F32)


def dot_tn(a, b):
    return lax.dot_general(a, b, (((0,), (0,)), ((), ())), preferred_element_type=F32)


def remote(src, dst, send_sem, recv_sem, device):
    return pltpu.make_async_remote_copy(
        src_ref=src,
        dst_ref=dst,
        send_sem=send_sem,
        recv_sem=recv_sem,
        device_id=device,
        device_id_type=pl.DeviceIdType.MESH,
    )


def loop(start, stop, step):
    def body(k, carry):
        step(k)
        return carry

    lax.fori_loop(start, stop, body, 0)


class Gather:
    def __init__(self, count, me, core, peer, sibling, table, sems):
        self.count, self.me, self.core = count, me, core
        self.peer, self.sibling, self.table, self.sems = peer, sibling, table, sems

    def far(self, k):
        mine = self.table.at[self.me, self.core]
        return remote(mine, mine, self.sems.at[0, k], self.sems.at[1, k], self.peer(k))

    def near(self, k):
        chunk = self.table.at[lax.rem(self.me + self.count - k, self.count), self.core]
        return remote(chunk, chunk, self.sems.at[2, k], self.sems.at[3, k], self.sibling)

    def start(self):
        loop(1, self.count, lambda k: self.far(k).start())
        self.near(0).start()

    def forward(self):
        def step(k):
            self.far(k).wait_recv()
            self.near(k).start()

        loop(1, self.count, step)

    def finish(self):
        loop(0, self.count, lambda k: self.near(k).wait_recv())

    def drain(self):
        loop(1, self.count, lambda k: self.far(k).wait_send())
        loop(0, self.count, lambda k: self.near(k).wait_send())


class Scatter:
    def __init__(self, count, me, core, peer, sibling, parts, half, landed, sems):
        self.count, self.me, self.core = count, me, core
        self.peer, self.sibling = peer, sibling
        self.parts, self.half, self.landed, self.sems = parts, half, landed, sems

    def near(self):
        return remote(
            self.parts.at[:, 1 - self.core],
            self.half,
            self.sems.at[0, 0],
            self.sems.at[1, 0],
            self.sibling,
        )

    def far(self, k):
        there = lax.rem(self.me + k, self.count)
        return remote(
            self.half.at[there],
            self.landed.at[k],
            self.sems.at[0, k],
            self.sems.at[1, k],
            self.peer(k),
        )

    def start(self):
        self.near().start()

    def send(self):
        self.near().wait_recv()

        def add(there):
            mine = self.parts[there, self.core].astype(F32)
            self.half[there] = (mine + self.half[there].astype(F32)).astype(BF16)

        def step(k):
            add(lax.rem(self.me + k, self.count))
            self.far(k).start()

        loop(1, self.count, step)
        add(self.me)

    def total(self):
        def step(k, acc):
            self.far(k).wait_recv()
            return acc + self.landed[k].astype(F32)

        return lax.fori_loop(1, self.count, step, self.half[self.me].astype(F32))

    def drain(self):
        self.near().wait_send()
        loop(1, self.count, lambda k: self.far(k).wait_send())


def layer(
    sizes,
    xin,
    cot,
    segc,
    rts,
    wpk,
    wgi,
    wui,
    wdi,
    o_h,
    o_ig,
    o_w,
    o_t,
    o_wg,
    o_wu,
    o_wd,
    wall,
    cotall,
    ball,
    kv,
    wg,
    wu,
    wd,
    a_ref,
    qs,
    p_ref,
    ds_ref,
    o_ref,
    part,
    ybuf,
    hall,
    dall,
    igall,
    dgp_ref,
    dup_ref,
    ug_ref,
    dbs,
    dbs_half,
    dbs_land,
    ys,
    ys_half,
    ys_land,
    gg,
    gu,
    gd,
    gg_land,
    gu_land,
    gd_land,
    gg_out,
    gu_out,
    gd_out,
    dos,
    dq_ref,
    dkv,
    dkv_half,
    dkv_land,
    wgs,
    wgs_half,
    wgs_land,
    tail_y,
    s_wall,
    s_cot,
    s_ball,
    s_kv,
    s_exp,
    s_y1,
    s_dbs,
    s_ys,
    s_grad,
    s_dall,
    s_dkv,
    s_y2,
    s_wgs,
    s_fin,
):
    n_dp, n_ctx, n_ten = sizes
    nj = n_ctx // 2
    nq = n_dp * nj
    rows, width = xin.shape
    seq = n_ctx * rows
    quarter = rows // n_ten
    d, c, r = lax.axis_index("dp"), lax.axis_index("context"), lax.axis_index("tensor")
    core, j = lax.rem(c, 2), c // 2
    q = d * nj + j

    def at(dp, context, tensor):
        return {"dp": dp, "context": context, "tensor": tensor}

    def plane(k):
        there = lax.rem(q + k, nq)
        return at(there // nj, lax.rem(there, nj) * 2 + core, r)

    def along(k):
        return at(d, lax.rem(j + k, nj) * 2 + core, r)

    def tensor(k):
        return at(d, c, lax.rem(r + k, n_ten))

    partner_dp = at(1 - d, c, r)
    sibling = at(d, c + 1 - 2 * core, r)

    barrier = pltpu.get_barrier_semaphore()

    def greet(device):
        pl.semaphore_signal(barrier, inc=1, device_id=device, device_id_type=pl.DeviceIdType.MESH)

    loop(1, nq, lambda k: greet(plane(k)))
    greet(sibling)
    loop(1, n_ten, lambda k: greet(tensor(k)))
    pl.semaphore_wait(barrier, nq + n_ten - 1)

    wide = pl.ds(pl.multiple_of(r * quarter, quarter), quarter)

    g_wall = Gather(nq, q, core, plane, sibling, wall, s_wall)
    wall[q, core] = wpk[...]
    g_wall.start()

    half_d, cut = wgi.shape[1], wgi.shape[2]

    def d_rows(dp):
        return pl.ds(pl.multiple_of(dp * half_d, half_d), half_d)

    def f_rows(ten):
        return pl.ds(pl.multiple_of(ten * cut, cut), cut)

    here_g, here_u, here_d = (d_rows(d), f_rows(r)), (d_rows(d), f_rows(r)), (f_rows(r), d_rows(d))
    there_g, there_d = (d_rows(1 - d), f_rows(r)), (f_rows(r), d_rows(1 - d))

    def triple(sources, places, first_sem, k, device):
        return [
            remote(src, dst, s_exp.at[first_sem + 2 * i, k], s_exp.at[first_sem + 2 * i + 1, k], device)
            for i, (src, dst) in enumerate(zip(sources, places))
        ]

    landing = (wg.at[here_g], wu.at[here_u], wd.at[here_d])
    passed_on = (wg.at[there_g], wu.at[there_g], wd.at[there_d])

    def own_copies(k):
        return triple((wgi.at[d], wui.at[d], wdi.at[d]), landing, 0, k, tensor(k))

    def across_copies():
        return triple((wgi.at[1 - d], wui.at[1 - d], wdi.at[1 - d]), landing, 0, 0, partner_dp)

    def passed_copies(k):
        return triple(passed_on, passed_on, 6, k, tensor(k))

    def start_all(copies):
        for copy in copies:
            copy.start()

    def wait_recv_all(copies):
        for copy in copies:
            copy.wait_recv()

    def wait_send_all(copies):
        for copy in copies:
            copy.wait_send()

    loop(1, n_ten, lambda k: start_all(own_copies(k)))

    x = xin[...].astype(F32)
    inv = lax.rsqrt(jnp.mean(x * x, axis=-1, keepdims=True) + EPS)
    lane = lax.broadcasted_iota(jnp.int32, (1, 128), 1)
    low_half = lax.rem(lane, HEAD) < HEAD // 2
    group_of = lane // HEAD
    rate = jnp.exp(
        lax.rem(lane, HEAD // 2).astype(F32) * (-2.0 * math.log(10000.0) / HEAD)
    )
    row_index = c * rows + lax.broadcasted_iota(jnp.int32, (rows, 1), 0)
    angle = row_index.astype(F32) * rate
    cosine = jnp.cos(angle)
    sine = jnp.where(low_half, -1.0, 1.0) * jnp.sin(angle)

    def partner(z):
        return jnp.where(
            low_half, pltpu.roll(z, 128 - HEAD // 2, 1), pltpu.roll(z, HEAD // 2, 1)
        )

    def rope(z):
        return z * cosine + partner(z) * sine

    def unrope(z):
        return z * cosine - partner(z) * sine

    wg[here_g] = wgi[d]
    wu[here_u] = wui[d]
    wd[here_d] = wdi[d]
    g_cot = Gather(nq, q, core, plane, sibling, cotall, s_cot)
    cotall[q, core] = cot[wide]

    g_wall.forward()
    start_all(across_copies())
    g_wall.finish()

    tails = wall[:, :, :, 768:896].reshape(width, TAIL)
    gains = tails.astype(F32).T
    attn_gain, ffn_gain = gains[32:33], gains[33:34]
    a_ref[...] = (x * inv * attn_gain).astype(BF16)

    qkv = dot(a_ref[...], wall[:, :, :, 0:512].reshape(width, 512))
    for t in range(2):
        turned = rope(qkv[:, 128 * t : 128 * t + 128]) * 0.125
        for g in range(2):
            qs[2 * t + g] = jnp.where(group_of == g, turned, 0.0).astype(BF16)
    kv[j, core, :, 0:128] = rope(qkv[:, 256:384]).astype(BF16)
    kv[j, core, :, 128:256] = qkv[:, 384:512].astype(BF16)
    g_kv = Gather(nj, j, core, along, sibling, kv, s_kv)
    g_kv.start()

    numbers = wall[pl.ds(d * nj, nj), :, :, 768:896].reshape(nj * 64, TAIL).astype(F32)
    held = jnp.where((lane >= 34) & (lane < 38), numbers, 1e9)
    mine = segc[...]
    first = jnp.zeros((rows, 1), F32)
    for s in range(1, 4):
        below = jnp.sum(jnp.where(held < s - 0.5, 1.0, 0.0), axis=0, keepdims=True)
        below = jnp.sum(below, axis=1, keepdims=True)
        first = jnp.where(mine == s, below, first)
    first = first.astype(jnp.int32)
    columns = lax.broadcasted_iota(jnp.int32, (rows, seq), 1)
    allowed = (columns >= first) & (columns <= row_index)

    wait_recv_all(across_copies())
    loop(1, n_ten, lambda k: start_all(passed_copies(k)))
    g_kv.forward()
    g_kv.finish()
    g_cot.start()

    o_ref[...] = jnp.zeros_like(o_ref)

    def head_forward(i):
        scores = dot_nt(qs[i], kv[:, :, :, 0:128].reshape(seq, 128))
        scores = jnp.where(allowed, scores, NEG)
        top = jnp.max(scores, axis=-1, keepdims=True)
        expo = jnp.where(allowed, jnp.exp(scores - top), 0.0)
        weights = (expo * (1.0 / jnp.sum(expo, axis=-1, keepdims=True))).astype(BF16)
        p_ref[i] = weights
        out = dot(weights, kv[:, :, :, 128:256].reshape(seq, 128))
        o_ref[i // 2] += jnp.where(group_of == lax.rem(i, 2), out, 0.0)

    loop(0, 4, head_forward)
    o_low = jnp.concatenate([o_ref[0], o_ref[1]], axis=1).astype(BF16)
    w_out = wall[:, :, :, 512:768].reshape(width, 256)
    part[0] = dot_nt(o_low, w_out).astype(BF16).reshape(n_ten, quarter, width)

    def tensor_copy(which, sems, k):
        return remote(
            part.at[which, lax.rem(r + k, n_ten)],
            ybuf.at[which, k],
            sems.at[0, k],
            sems.at[1, k],
            tensor(k),
        )

    loop(1, n_ten, lambda k: tensor_copy(0, s_y1, k).start())
    hidden = xin[wide].astype(F32) + part[0, r].astype(F32)
    for k in range(1, n_ten):
        tensor_copy(0, s_y1, k).wait_recv()
        hidden = hidden + ybuf[0, k].astype(F32)

    inv_two = lax.rsqrt(jnp.mean(hidden * hidden, axis=-1, keepdims=True) + EPS)
    b_own = (hidden * inv_two * ffn_gain).astype(BF16)
    logits = jnp.where(lane < 32, dot(b_own, tails), NEG)
    expo = jnp.exp(logits - jnp.max(logits, axis=-1, keepdims=True))
    probs = expo / jnp.sum(expo, axis=-1, keepdims=True)
    routed = jnp.zeros((quarter, 128), F32)
    routes = rts[wide]
    for k in range(routes.shape[1]):
        routed = routed + jnp.where(routes[:, k : k + 1] == lane, 1.0, 0.0)
    gates = probs * routed
    gates_high = gates.astype(BF16).astype(F32)
    ball[q, core, :, 0:width] = b_own
    ball[q, core, :, width : width + TAIL] = (
        gates_high + pltpu.roll(gates - gates_high, 32, 1)
    ).astype(BF16)
    g_ball = Gather(nq, q, core, plane, sibling, ball, s_ball)
    g_ball.start()
    g_cot.forward()
    g_ball.forward()
    loop(1, n_ten, lambda k: wait_recv_all(own_copies(k)))
    loop(1, n_ten, lambda k: wait_recv_all(passed_copies(k)))
    g_cot.finish()
    g_ball.finish()

    expert = 2 * c + d
    gate_lane = (lane == expert) | (lane == expert + 32)
    block = 8 * quarter
    steps = nq // 4

    def tokens(ref, i, cut_at, cut_to):
        return ref[pl.ds(4 * i, 4), :, :, cut_at:cut_to].reshape(block, cut_to - cut_at)

    def rows_of(i):
        return pl.ds(pl.multiple_of(i * block, block), block)

    def expert_block(i):
        b = tokens(ball, i, 0, width)
        packed = tokens(ball, i, width, width + TAIL).astype(F32)
        gate = jnp.sum(jnp.where(gate_lane, packed, 0.0), axis=-1, keepdims=True)
        gp = dot(b, wg[...])
        up = dot(b, wu[...])
        du = dot_nt(tokens(cotall, i, 0, width), wd[...])
        sigma = 1.0 / (1.0 + jnp.exp(-gp))
        silu = gp * sigma
        u = (silu * up).astype(BF16).astype(F32)
        dgate = jnp.sum(du * u, axis=-1, keepdims=True)
        du = gate * du
        dgp = (du * up * sigma * (1.0 + gp * (1.0 - sigma))).astype(BF16)
        dup = (du * silu).astype(BF16)
        dgp_ref[rows_of(i)] = dgp
        dup_ref[rows_of(i)] = dup
        ug_ref[rows_of(i)] = (gate * u).astype(BF16)
        db = dot_nt(dgp, wg[...]) + dot_nt(dup, wu[...])
        dbs[pl.ds(4 * i, 4), :, :, 0:width] = db.astype(BF16).reshape(4, 2, quarter, width)
        dbs[pl.ds(4 * i, 4), :, :, width : width + TAIL] = (
            jnp.where(lane == expert, dgate, 0.0).astype(BF16).reshape(4, 2, quarter, TAIL)
        )

    loop(0, steps, expert_block)
    x_dbs = Scatter(nq, q, core, plane, sibling, dbs, dbs_half, dbs_land, s_dbs)
    x_dbs.start()

    def down_block(i):
        y = dot(ug_ref[rows_of(i)], wd[...])
        ys[pl.ds(4 * i, 4)] = y.astype(BF16).reshape(4, 2, quarter, width)

    loop(0, steps, down_block)
    x_dbs.send()
    x_ys = Scatter(nq, q, core, plane, sibling, ys, ys_half, ys_land, s_ys)
    x_ys.start()

    def grad_copy(which, table, land, k):
        place = f_rows(lax.rem(r + k, n_ten))
        cut_out = table.at[place] if which == 2 else table.at[:, place]
        return remote(
            cut_out, land.at[k], s_grad.at[2 * which, k], s_grad.at[2 * which + 1, k], tensor(k)
        )

    def grad_copies(k):
        return [
            grad_copy(0, gg, gg_land, k),
            grad_copy(1, gu, gu_land, k),
            grad_copy(2, gd, gd_land, k),
        ]

    all_cot = cotall[...].reshape(nq * 2 * quarter, width)
    all_b = ball[:, :, :, 0:width].reshape(nq * 2 * quarter, width)
    gd[...] = dot_tn(ug_ref[...], all_cot).astype(BF16)
    loop(1, n_ten, lambda k: grad_copy(2, gd, gd_land, k).start())
    gg[...] = dot_tn(all_b, dgp_ref[...]).astype(BF16)
    gu[...] = dot_tn(all_b, dup_ref[...]).astype(BF16)

    summed = x_dbs.total()
    x_ys.send()
    dprobs = routed * summed[:, width : width + TAIL]
    dlogits = probs * (dprobs - jnp.sum(probs * dprobs, axis=-1, keepdims=True))
    dlogits = jnp.where(lane < 32, dlogits, 0.0).astype(BF16)
    db = summed[:, 0:width] + dot_nt(dlogits, tails)
    w_db = db * ffn_gain
    grad_hidden = (
        cot[wide].astype(F32)
        + inv_two * w_db
        - hidden * inv_two**3 * (jnp.sum(w_db * hidden, axis=-1, keepdims=True) / width)
    )
    ffn_gain_rows = (db * hidden * inv_two).astype(BF16)
    dall[r] = grad_hidden.astype(BF16)

    def spread(table, sems, k):
        mine = table.at[r]
        return remote(mine, mine, sems.at[0, k], sems.at[1, k], tensor(k))

    loop(1, n_ten, lambda k: spread(dall, s_dall, k).start())
    one_hot = lax.broadcasted_iota(jnp.int32, (rows, TAIL), 1)
    ones_ffn = jnp.where(one_hot[0:quarter] == 32, 1.0, 0.0).astype(BF16)
    ones_attn = jnp.where(one_hot == 33, 1.0, 0.0).astype(BF16)
    tail_grad = dot_tn(b_own, dlogits) + dot_tn(ffn_gain_rows, ones_ffn)
    loop(1, n_ten, lambda k: spread(dall, s_dall, k).wait_recv())

    loop(1, n_ten, lambda k: grad_copy(0, gg, gg_land, k).start())
    d_attn = dall[...].reshape(rows, width)
    do = dot(d_attn, w_out).astype(BF16)
    for t in range(2):
        tile = do[:, 128 * t : 128 * t + 128].astype(F32)
        for g in range(2):
            dos[2 * t + g] = jnp.where(group_of == g, tile, 0.0).astype(BF16)

    dq_ref[...] = jnp.zeros_like(dq_ref)

    def head_backward(i):
        go = dos[i]
        delta = jnp.sum(go.astype(F32) * o_ref[i // 2], axis=-1, keepdims=True)
        dp = dot_nt(go, kv[:, :, :, 128:256].reshape(seq, 128))
        grad = (p_ref[i].astype(F32) * (dp - delta)).astype(BF16)
        ds_ref[i] = grad
        dq = dot(grad, kv[:, :, :, 0:128].reshape(seq, 128))
        dq_ref[i // 2] += jnp.where(group_of == lax.rem(i, 2), dq, 0.0)

    loop(0, 4, head_backward)
    all_q = qs[...].reshape(4 * rows, 128)
    all_do = dos[...].reshape(4 * rows, 128)
    for i in range(4):
        span = slice(i * (seq // 4), (i + 1) * (seq // 4))
        place = slice(i * (nj // 4), (i + 1) * (nj // 4))
        dk = dot_tn(ds_ref[:, :, span].reshape(4 * rows, seq // 4), all_q)
        dv = dot_tn(p_ref[:, :, span].reshape(4 * rows, seq // 4), all_do)
        dkv[place, :, :, 0:128] = dk.astype(BF16).reshape(nj // 4, 2, rows, 128)
        dkv[place, :, :, 128:256] = dv.astype(BF16).reshape(nj // 4, 2, rows, 128)
    x_dkv = Scatter(nj, j, core, along, sibling, dkv, dkv_half, dkv_land, s_dkv)
    x_dkv.start()

    def to_rows(grad):
        return grad.astype(BF16).reshape(nq, 2, 32, grad.shape[1])

    a_low = a_ref[...]
    wgs[:, :, :, 512:768] = to_rows(dot_tn(d_attn, o_low))
    x_dkv.send()
    dq_lin = jnp.concatenate([unrope(dq_ref[0]), unrope(dq_ref[1])], axis=1) * 0.125
    dq_lin = dq_lin.astype(BF16)
    wgs[:, :, :, 0:256] = to_rows(dot_tn(a_low, dq_lin))
    da = dot_nt(dq_lin, wall[:, :, :, 0:256].reshape(width, 256))
    grad_kv = x_dkv.total()
    dkv_lin = jnp.concatenate([unrope(grad_kv[:, 0:128]), grad_kv[:, 128:256]], axis=1)
    dkv_lin = dkv_lin.astype(BF16)
    da = da + dot_nt(dkv_lin, wall[:, :, :, 256:512].reshape(width, 256))
    part[1] = da.astype(BF16).reshape(n_ten, quarter, width)
    loop(1, n_ten, lambda k: tensor_copy(1, s_y2, k).start())
    wgs[:, :, :, 256:512] = to_rows(dot_tn(a_low, dkv_lin))
    attn_gain_rows = (da * xin[...].astype(F32) * inv).astype(BF16)
    wgs[:, :, :, 768:896] = to_rows(tail_grad + dot_tn(attn_gain_rows, ones_attn))
    x_wgs = Scatter(nq, q, core, plane, sibling, wgs, wgs_half, wgs_land, s_wgs)
    x_wgs.start()

    hall[r] = (hidden + x_ys.total()).astype(BF16)
    loop(1, n_ten, lambda k: spread(hall, s_fin, k).start())

    grad_a = part[1, r].astype(F32)
    for k in range(1, n_ten):
        tensor_copy(1, s_y2, k).wait_recv()
        grad_a = grad_a + ybuf[1, k].astype(F32)
    x_own = xin[wide].astype(F32)
    inv_own = lax.rsqrt(jnp.mean(x_own * x_own, axis=-1, keepdims=True) + EPS)
    w_da = grad_a * attn_gain
    grad_x = (
        grad_hidden
        + inv_own * w_da
        - x_own * inv_own**3 * (jnp.sum(w_da * x_own, axis=-1, keepdims=True) / width)
    )
    igall[r] = grad_x.astype(BF16)

    def spread_ig(k):
        mine = igall.at[r]
        return remote(mine, mine, s_fin.at[2, k], s_fin.at[3, k], tensor(k))

    loop(1, n_ten, lambda k: spread_ig(k).start())
    loop(1, n_ten, lambda k: grad_copy(1, gu, gu_land, k).start())
    x_wgs.send()

    def reduce_grads(table, land, place, land_place):
        same = table[place].astype(F32)
        for k in range(1, n_ten):
            same = same + land[(k, *land_place)].astype(F32)
        return same

    sides = ((gg, gg_land, gg_out), (gu, gu_land, gu_out), (gd, gd_land, gd_out))
    whole = slice(None)

    def half_sum(i, dp):
        table, land, _ = sides[i]
        if i == 2:
            return reduce_grads(table, land, (f_rows(r), d_rows(dp)), (whole, d_rows(dp)))
        return reduce_grads(table, land, (d_rows(dp), f_rows(r)), (d_rows(dp), whole))

    def half_copy(i):
        out = sides[i][2]
        return remote(
            out.at[0], out.at[1], s_grad.at[2 * i, 0], s_grad.at[2 * i + 1, 0], partner_dp
        )

    for i, out in ((2, o_wd), (0, o_wg), (1, o_wu)):
        loop(1, n_ten, lambda k: grad_copy(i, *sides[i][:2], k).wait_recv())
        sides[i][2][0] = half_sum(i, 1 - d).astype(BF16)
        half_copy(i).start()
        out[d] = half_sum(i, d)

    loop(1, n_ten, lambda k: spread(hall, s_fin, k).wait_recv())
    o_h[...] = hall[...]
    loop(1, n_ten, lambda k: spread_ig(k).wait_recv())
    o_ig[...] = igall[...].astype(F32)

    for i, out in enumerate((o_wg, o_wu, o_wd)):
        half_copy(i).wait_recv()
        out[1 - d] = sides[i][2][1].astype(F32)

    grads = x_wgs.total()
    o_w[...] = grads[:, 0:768]
    tail_y[0] = grads[:, 768:896]

    def tail_copy(k):
        return remote(tail_y.at[0], tail_y.at[k], s_fin.at[4, k], s_fin.at[5, k], tensor(k))

    loop(1, n_ten, lambda k: tail_copy(k).start())
    tail_sum = grads[:, 768:896]
    for k in range(1, n_ten):
        tail_copy(k).wait_recv()
        tail_sum = tail_sum + tail_y[k]
    o_t[...] = tail_sum

    for gather in (g_wall, g_cot, g_kv, g_ball):
        gather.drain()
    for scatter in (x_dbs, x_ys, x_dkv, x_wgs):
        scatter.drain()

    def drain_tensor(k):
        tensor_copy(0, s_y1, k).wait_send()
        tensor_copy(1, s_y2, k).wait_send()
        spread(dall, s_dall, k).wait_send()
        spread(hall, s_fin, k).wait_send()
        spread_ig(k).wait_send()
        tail_copy(k).wait_send()

    loop(1, n_ten, drain_tensor)

    wait_send_all(across_copies())

    def drain_experts(k):
        wait_send_all(own_copies(k))
        wait_send_all(passed_copies(k))
        wait_send_all(grad_copies(k))

    loop(1, n_ten, drain_experts)
    for i in range(3):
        half_copy(i).wait_send()


def call_layer(sizes, xin, cot, segc, rts, wpk, wgi, wui, wdi):
    n_dp, n_ctx, n_ten = sizes
    nj = n_ctx // 2
    nq = n_dp * nj
    rows, width = xin.shape
    seq = n_ctx * rows
    quarter = rows // n_ten
    half_d, cut = wgi.shape[1], wgi.shape[2]
    hidden_units = cut * n_ten
    packed = wpk.shape[1]
    all_rows = nq * 2 * quarter

    def shape(*dims, kind=F32):
        return jax.ShapeDtypeStruct(dims, kind)

    def low(*dims):
        return pltpu.VMEM(dims, BF16)

    def full(*dims):
        return pltpu.VMEM(dims, F32)

    def sems(*dims):
        return pltpu.SemaphoreType.DMA(dims)

    scratch = [
        low(nq, 2, 32, packed),
        low(nq, 2, quarter, width),
        low(nq, 2, quarter, width + TAIL),
        low(nj, 2, rows, 256),
        low(width, hidden_units),
        low(width, hidden_units),
        low(hidden_units, width),
        low(rows, width),
        low(4, rows, 128),
        low(4, rows, seq),
        low(4, rows, seq),
        full(2, rows, 128),
        low(2, n_ten, quarter, width),
        low(2, n_ten, quarter, width),
        low(n_ten, quarter, width),
        low(n_ten, quarter, width),
        low(n_ten, quarter, width),
        low(all_rows, hidden_units),
        low(all_rows, hidden_units),
        low(all_rows, hidden_units),
        low(nq, 2, quarter, width + TAIL),
        low(nq, quarter, width + TAIL),
        low(nq, quarter, width + TAIL),
        low(nq, 2, quarter, width),
        low(nq, quarter, width),
        low(nq, quarter, width),
        low(width, hidden_units),
        low(width, hidden_units),
        low(hidden_units, width),
        low(n_ten, width, cut),
        low(n_ten, width, cut),
        low(n_ten, cut, width),
        low(2, half_d, cut),
        low(2, half_d, cut),
        low(2, cut, half_d),
        low(4, rows, 128),
        full(2, rows, 128),
        low(nj, 2, rows, 256),
        low(nj, rows, 256),
        low(nj, rows, 256),
        low(nq, 2, 32, packed),
        low(nq, 32, packed),
        low(nq, 32, packed),
        full(n_ten, 32, TAIL),
        sems(4, nq),
        sems(4, nq),
        sems(4, nq),
        sems(4, nj),
        sems(12, n_ten),
        sems(2, n_ten),
        sems(2, nq),
        sems(2, nq),
        sems(6, n_ten),
        sems(2, n_ten),
        sems(2, nj),
        sems(2, n_ten),
        sems(2, nq),
        sems(6, n_ten),
    ]
    flops = 2 * (9 * all_rows * width * hidden_units + 4 * rows * width * 768)
    return pl.pallas_call(
        functools.partial(layer, sizes),
        out_shape=(
            shape(n_ten, quarter, width, kind=BF16),
            shape(n_ten, quarter, width),
            shape(32, 768),
            shape(32, TAIL),
            shape(2, half_d, cut),
            shape(2, half_d, cut),
            shape(2, cut, half_d),
        ),
        in_specs=[pl.BlockSpec(memory_space=pltpu.VMEM)] * 8,
        out_specs=[pl.BlockSpec(memory_space=pltpu.VMEM)] * 7,
        scratch_shapes=scratch,
        compiler_params=pltpu.CompilerParams(
            collective_id=0, has_side_effects=True, vmem_limit_bytes=VMEM_BYTES
        ),
        cost_estimate=pl.CostEstimate(flops=flops, bytes_accessed=8 << 20, transcendentals=0),
    )(xin, cot, segc, rts, wpk, wgi, wui, wdi)


def swap_heads(table):
    a, b, c, d = [table[:, HEAD * i : HEAD * i + HEAD] for i in range(4)]
    return jnp.concatenate([a, c, b, d], axis=1)


def per_device(
    hidden_in,
    segments,
    routes,
    norm_attn,
    w_query,
    w_key,
    w_value,
    w_out,
    norm_ffn,
    w_router,
    w_gate,
    w_up,
    w_down,
    cotangent,
):
    sizes = (lax.axis_size("dp"), lax.axis_size("context"), lax.axis_size("tensor"))
    rows = hidden_in.shape[0]
    per_row = rows // 32
    packed = jnp.concatenate(
        [
            swap_heads(w_query[0]),
            w_key[0],
            w_value[0],
            swap_heads(w_out[0].T),
            w_router[0],
            norm_attn[0][:, None],
            norm_ffn[0][:, None],
            segments[0].reshape(32, per_row).astype(BF16),
            jnp.zeros((32, TAIL - 34 - per_row), BF16),
        ],
        axis=1,
    )
    out, grad, w_grads, tail, gate_grad, up_grad, down_grad = call_layer(
        sizes,
        hidden_in,
        cotangent,
        segments[0][:, None],
        routes[0],
        packed,
        w_gate[0],
        w_up[0],
        w_down[0],
    )
    return (
        out.reshape(hidden_in.shape),
        grad.reshape(hidden_in.shape),
        tail[:, 33][None],
        swap_heads(w_grads[:, 0:256])[None],
        w_grads[:, 256:384][None],
        w_grads[:, 384:512][None],
        swap_heads(w_grads[:, 512:768]).T[None],
        tail[:, 32][None],
        tail[:, 0:32][None],
        gate_grad[None],
        up_grad[None],
        down_grad[None],
    )


def solution(mesh):
    in_specs = (
        P(("dp", "context"), None),
        P("dp", "context"),
        P(None, ("dp", "context"), None),
        P(None, ("dp", "context")),
        P(None, ("dp", "context"), "tensor"),
        P(None, ("dp", "context"), "tensor"),
        P(None, ("dp", "context"), "tensor"),
        P(None, "tensor", ("dp", "context")),
        P(None, ("dp", "context")),
        P(None, ("dp", "context"), None),
        P(None, "context", "dp", "tensor"),
        P(None, "context", "dp", "tensor"),
        P(None, "context", "tensor", "dp"),
        P(("dp", "context"), None),
    )
    out_specs = (
        P(("dp", "context"), None),
        P(("dp", "context"), None),
        P(None, ("dp", "context")),
        P(None, ("dp", "context"), "tensor"),
        P(None, ("dp", "context"), "tensor"),
        P(None, ("dp", "context"), "tensor"),
        P(None, "tensor", ("dp", "context")),
        P(None, ("dp", "context")),
        P(None, ("dp", "context"), None),
        P(None, "context", "dp", "tensor"),
        P(None, "context", "dp", "tensor"),
        P(None, "context", "tensor", "dp"),
    )
    return jax.shard_map(
        per_device, mesh=mesh, in_specs=in_specs, out_specs=out_specs, check_vma=False
    )
```

```python
import functools
import math

import jax
import jax.numpy as jnp
from jax import lax
from jax.experimental import pallas as pl
from jax.experimental.pallas import tpu as pltpu
from jax.sharding import PartitionSpec as P

HEAD = 64
EPS = 1e-06
NEG = -1e30
F32 = jnp.float32
BF16 = jnp.bfloat16
TAIL = 128
VMEM_BYTES = 60 * 1024 * 1024


def dot(a, b):
    return jnp.dot(a, b, preferred_element_type=F32)


def dot_nt(a, b):
    return lax.dot_general(a, b, (((1,), (1,)), ((), ())), preferred_element_type=F32)


def dot_tn(a, b):
    return lax.dot_general(a, b, (((0,), (0,)), ((), ())), preferred_element_type=F32)


def remote(src, dst, send_sem, recv_sem, device):
    return pltpu.make_async_remote_copy(
        src_ref=src,
        dst_ref=dst,
        send_sem=send_sem,
        recv_sem=recv_sem,
        device_id=device,
        device_id_type=pl.DeviceIdType.MESH,
    )


def loop(start, stop, step):
    def body(k, carry):
        step(k)
        return carry

    lax.fori_loop(start, stop, body, 0)


class Gather:
    def __init__(self, count, me, core, peer, sibling, table, landed, sems):
        self.count, self.me, self.core = count, me, core
        self.peer, self.sibling, self.table = peer, sibling, table
        self.landed, self.sems = landed, sems

    def far(self, k):
        mine = self.table.at[self.me, self.core]
        return remote(mine, mine, self.sems.at[0], self.landed.at[k], self.peer(k))

    def near(self, k):
        chunk = self.table.at[lax.rem(self.me + self.count - k, self.count), self.core]
        return remote(chunk, chunk, self.sems.at[1], self.sems.at[2], self.sibling)

    def start(self):
        loop(1, self.count, lambda k: self.far(k).start())
        self.near(0).start()

    def forward(self):
        def step(k):
            self.far(k).wait_recv()
            self.near(k).start()

        loop(1, self.count, step)

    def near_all(self, side):
        whole = self.table.at[:, side]
        return remote(whole, whole, self.sems.at[1], self.sems.at[2], self.sibling)

    def finish(self):
        self.near_all(1 - self.core).wait_recv()

    def drain(self):
        others = self.table.at[pl.ds(0, self.count - 1), self.core]
        remote(others, others, self.sems.at[0], self.landed.at[0], self.sibling).wait_send()
        self.near_all(self.core).wait_send()


class Scatter:
    def __init__(self, count, me, core, peer, sibling, parts, half, landed, sems):
        self.count, self.me, self.core = count, me, core
        self.peer, self.sibling = peer, sibling
        self.parts, self.half, self.landed, self.sems = parts, half, landed, sems

    def near(self):
        return remote(
            self.parts.at[:, 1 - self.core],
            self.half,
            self.sems.at[0],
            self.sems.at[1],
            self.sibling,
        )

    def far(self, k):
        there = lax.rem(self.me + k, self.count)
        return remote(
            self.half.at[there],
            self.landed.at[k],
            self.sems.at[2],
            self.sems.at[3],
            self.peer(k),
        )

    def far_all(self):
        return remote(
            self.half.at[pl.ds(1, self.count - 1)],
            self.landed.at[pl.ds(1, self.count - 1)],
            self.sems.at[2],
            self.sems.at[3],
            self.sibling,
        )

    def start(self):
        self.near().start()

    def send(self):
        self.near().wait_recv()

        def add(there):
            mine = self.parts[there, self.core].astype(F32)
            self.half[there] = (mine + self.half[there].astype(F32)).astype(BF16)

        def step(k):
            add(lax.rem(self.me + k, self.count))
            self.far(k).start()

        loop(1, self.count, step)
        add(self.me)

    def total(self):
        self.far_all().wait_recv()

        def step(k, acc):
            return acc + self.landed[k].astype(F32)

        return lax.fori_loop(1, self.count, step, self.half[self.me].astype(F32))

    def drain(self):
        self.near().wait_send()
        self.far_all().wait_send()


def layer(
    sizes,
    xin,
    cot,
    seg,
    rts,
    gain_a,
    gain_f,
    wq,
    wk,
    wv,
    wo,
    wr,
    wgi,
    wui,
    wdi,
    o_h,
    o_ig,
    o_q,
    o_k,
    o_v,
    o_o,
    o_t,
    o_wg,
    o_wu,
    o_wd,
    wall,
    wall_out,
    cotall,
    ball,
    kv,
    wg,
    wu,
    wd,
    x_ref,
    rt_ref,
    ig_ref,
    w_ref,
    t_ref,
    og_ref,
    ou_ref,
    od_ref,
    a_ref,
    qs,
    p_ref,
    ds_ref,
    o_ref,
    part,
    ybuf,
    hall,
    dall,
    igall,
    dgp_ref,
    dup_ref,
    ug_ref,
    dbs,
    dbs_half,
    dbs_land,
    ys,
    ys_half,
    ys_land,
    gg,
    gu,
    gd,
    gg_land,
    gu_land,
    gd_land,
    gg_out,
    gu_out,
    gd_out,
    dos,
    dq_ref,
    dkv,
    dkv_half,
    dkv_land,
    wgo,
    wgo_half,
    wgo_land,
    wgq,
    wgq_half,
    wgq_land,
    wgk,
    wgk_half,
    wgk_land,
    tail_y,
    l_wall,
    s_wall,
    l_wout,
    s_wout,
    l_cot,
    s_cot,
    l_ball,
    s_ball,
    l_kv,
    s_kv,
    s_exp,
    s_y1,
    s_dbs,
    s_ys,
    s_grad,
    s_dall,
    s_dkv,
    s_y2,
    s_wgo,
    s_wgq,
    s_wgk,
    s_fin,
    s_in,
    s_out,
):
    n_dp, n_ctx, n_ten = sizes
    nj = n_ctx // 2
    nq = n_dp * nj
    rows, width = xin.shape
    seq = n_ctx * rows
    quarter = rows // n_ten
    d, c, r = lax.axis_index("dp"), lax.axis_index("context"), lax.axis_index("tensor")
    core, j = lax.rem(c, 2), c // 2
    q = d * nj + j

    def at(dp, context, tensor):
        return {"dp": dp, "context": context, "tensor": tensor}

    def plane(k):
        there = lax.rem(q + k, nq)
        return at(there // nj, lax.rem(there, nj) * 2 + core, r)

    def along(k):
        return at(d, lax.rem(j + k, nj) * 2 + core, r)

    def tensor(k):
        return at(d, c, lax.rem(r + k, n_ten))

    partner_dp = at(1 - d, c, r)
    sibling = at(d, c + 1 - 2 * core, r)

    wide = pl.ds(pl.multiple_of(r * quarter, quarter), quarter)
    half_d, cut = wgi.shape[1], wgi.shape[2]

    def d_rows(dp):
        return pl.ds(pl.multiple_of(dp * half_d, half_d), half_d)

    def f_rows(ten):
        return pl.ds(pl.multiple_of(ten * cut, cut), cut)

    here_g, here_u, here_d = (d_rows(d), f_rows(r)), (d_rows(d), f_rows(r)), (f_rows(r), d_rows(d))
    there_g, there_d = (d_rows(1 - d), f_rows(r)), (f_rows(r), d_rows(1 - d))

    barrier = pltpu.get_barrier_semaphore()

    def greet(device):
        pl.semaphore_signal(barrier, inc=1, device_id=device, device_id_type=pl.DeviceIdType.MESH)

    loop(1, nq, lambda k: greet(plane(k)))
    greet(sibling)
    loop(1, n_ten, lambda k: greet(tensor(k)))

    loads = [
        pltpu.make_async_copy(src, dst, s_in.at[i])
        for i, (src, dst) in enumerate(
            (
                (xin, x_ref),
                (cot.at[wide], cotall.at[q, core]),
                (wgi.at[d], wg.at[here_g]),
                (wui.at[d], wu.at[here_u]),
                (wdi.at[d], wd.at[here_d]),
            )
        )
    ]
    for load in loads:
        load.start()

    lane = lax.broadcasted_iota(jnp.int32, (1, 128), 1)
    group_of = lane // HEAD

    def swap_heads(table):
        one, two = table[:, 0:128], table[:, 128:256]
        return (
            jnp.where(group_of == 0, one, pltpu.roll(two, HEAD, 1)),
            jnp.where(group_of == 0, pltpu.roll(one, HEAD, 1), two),
        )

    def diagonal(count, extent, first):
        up = lax.broadcasted_iota(jnp.int32, (count, extent), 0)
        return up + first == lax.broadcasted_iota(jnp.int32, (count, extent), 1)

    def as_column(row, count, first):
        picked = jnp.where(diagonal(count, row.shape[1], first), row, 0.0)
        return jnp.sum(picked, axis=1, keepdims=True)

    for i, tile in enumerate(swap_heads(wq[...].astype(F32))):
        wall[q, core, :, 128 * i : 128 * i + 128] = tile.astype(BF16)
    for i, tile in enumerate(swap_heads(wo[...].astype(F32))):
        wall_out[q, core, :, 128 * i : 128 * i + 128] = tile.astype(BF16)
    wall[q, core, :, 256:384] = wk[...]
    wall[q, core, :, 384:512] = wv[...]
    numbers_here = seg[...].astype(F32)
    tail = jnp.where(lane == 32, as_column(gain_a[...].astype(F32), 32, 0), 0.0)
    tail = jnp.where(lane == 33, as_column(gain_f[...].astype(F32), 32, 0), tail)
    for i in range(rows // 32):
        tail = jnp.where(lane == 34 + i, as_column(numbers_here, 32, 32 * i), tail)
    wall[q, core, :, 512:640] = tail.astype(BF16)
    wall[q, core, :, 512:544] = wr[...]

    pl.semaphore_wait(barrier, nq + n_ten - 1)

    g_wall = Gather(nq, q, core, plane, sibling, wall, l_wall, s_wall)
    g_wall.start()
    g_wout = Gather(nq, q, core, plane, sibling, wall_out, l_wout, s_wout)

    def triple(sources, places, first_sem, k, device):
        return [
            remote(src, dst, s_exp.at[first_sem + 2 * i, k], s_exp.at[first_sem + 2 * i + 1, k], device)
            for i, (src, dst) in enumerate(zip(sources, places))
        ]

    landing = (wg.at[here_g], wu.at[here_u], wd.at[here_d])
    passed_on = (wg.at[there_g], wu.at[there_g], wd.at[there_d])

    def own_copies(k):
        return triple((wgi.at[d], wui.at[d], wdi.at[d]), landing, 0, k, tensor(k))

    def across_copies():
        return triple((wgi.at[1 - d], wui.at[1 - d], wdi.at[1 - d]), landing, 0, 0, partner_dp)

    def passed_copy(i, k):
        place = passed_on[i]
        return remote(place, place, s_exp.at[6 + 2 * i, k], s_exp.at[7 + 2 * i, k], tensor(k))

    def passed_copies(k):
        return [passed_copy(i, k) for i in range(3)]

    def start_all(copies):
        for copy in copies:
            copy.start()

    def wait_recv_all(copies):
        for copy in copies:
            copy.wait_recv()

    def wait_send_all(copies):
        for copy in copies:
            copy.wait_send()

    loop(1, n_ten, lambda k: start_all(own_copies(k)))

    loads[0].wait()
    x = x_ref[...].astype(F32)
    inv = lax.rsqrt(jnp.mean(x * x, axis=-1, keepdims=True) + EPS)
    low_half = lax.rem(lane, HEAD) < HEAD // 2
    rate = jnp.exp(
        lax.rem(lane, HEAD // 2).astype(F32) * (-2.0 * math.log(10000.0) / HEAD)
    )
    row_index = c * rows + lax.broadcasted_iota(jnp.int32, (rows, 1), 0)
    angle = row_index.astype(F32) * rate
    cosine = jnp.cos(angle)
    sine = jnp.where(low_half, -1.0, 1.0) * jnp.sin(angle)

    def partner(z):
        return jnp.where(
            low_half, pltpu.roll(z, 128 - HEAD // 2, 1), pltpu.roll(z, HEAD // 2, 1)
        )

    def rope(z):
        return z * cosine + partner(z) * sine

    def unrope(z):
        return z * cosine - partner(z) * sine

    named = jnp.zeros((128, rows), F32)
    of_expert = lax.broadcasted_iota(jnp.int32, (128, rows), 0)
    for k in range(rts.shape[0]):
        named = named + jnp.where(rts[k : k + 1, :] == of_expert, 1.0, 0.0)
    rt_ref[...] = named.T
    for load in loads[1:]:
        load.wait()
    g_cot = Gather(nq, q, core, plane, sibling, cotall, l_cot, s_cot)

    g_wall.forward()
    start_all(across_copies())
    g_wall.finish()

    tails = wall[:, :, :, 512:640].reshape(width, TAIL)
    gains = tails.astype(F32).T
    attn_gain, ffn_gain = gains[32:33], gains[33:34]
    a_ref[...] = (x * inv * attn_gain).astype(BF16)

    qkv = dot(a_ref[...], wall[:, :, :, 0:512].reshape(width, 512))
    for t in range(2):
        turned = rope(qkv[:, 128 * t : 128 * t + 128]) * 0.125
        for g in range(2):
            qs[2 * t + g] = jnp.where(group_of == g, turned, 0.0).astype(BF16)
    kv[j, core, :, 0:128] = rope(qkv[:, 256:384]).astype(BF16)
    kv[j, core, :, 128:256] = qkv[:, 384:512].astype(BF16)
    g_kv = Gather(nj, j, core, along, sibling, kv, l_kv, s_kv)
    g_kv.start()
    g_wout.start()

    numbers = wall[pl.ds(d * nj, nj), :, :, 512:640].reshape(nj * 64, TAIL).astype(F32)
    held = jnp.where((lane >= 34) & (lane < 38), numbers, 1e9)
    mine = as_column(numbers_here, rows, 0)
    first = jnp.zeros((rows, 1), F32)
    for s in range(1, 4):
        below = jnp.sum(jnp.where(held < s - 0.5, 1.0, 0.0), axis=0, keepdims=True)
        below = jnp.sum(below, axis=1, keepdims=True)
        first = jnp.where(mine == s, below, first)
    first = first.astype(jnp.int32)
    columns = lax.broadcasted_iota(jnp.int32, (rows, seq), 1)
    allowed = (columns >= first) & (columns <= row_index)

    wait_recv_all(across_copies())
    loop(1, n_ten, lambda k: passed_copy(0, k).start())
    g_kv.forward()
    g_kv.finish()
    g_wout.forward()
    g_cot.start()

    o_ref[...] = jnp.zeros_like(o_ref)

    def head_forward(i):
        scores = dot_nt(qs[i], kv[:, :, :, 0:128].reshape(seq, 128))
        scores = jnp.where(allowed, scores, NEG)
        top = jnp.max(scores, axis=-1, keepdims=True)
        expo = jnp.where(allowed, jnp.exp(scores - top), 0.0)
        weights = (expo * (1.0 / jnp.sum(expo, axis=-1, keepdims=True))).astype(BF16)
        p_ref[i] = weights
        out = dot(weights, kv[:, :, :, 128:256].reshape(seq, 128))
        o_ref[i // 2] += jnp.where(group_of == lax.rem(i, 2), out, 0.0)

    loop(0, 4, head_forward)
    g_wout.finish()
    o_low = jnp.concatenate([o_ref[0], o_ref[1]], axis=1).astype(BF16)
    w_out = wall_out[...].reshape(width, 256)
    part[0] = dot_nt(o_low, w_out).astype(BF16).reshape(n_ten, quarter, width)

    def tensor_copy(which, sems, k):
        return remote(
            part.at[which, lax.rem(r + k, n_ten)],
            ybuf.at[which, k],
            sems.at[0, k],
            sems.at[1, k],
            tensor(k),
        )

    loop(1, n_ten, lambda k: tensor_copy(0, s_y1, k).start())
    hidden = x_ref[wide].astype(F32) + part[0, r].astype(F32)
    for k in range(1, n_ten):
        tensor_copy(0, s_y1, k).wait_recv()
        hidden = hidden + ybuf[0, k].astype(F32)

    inv_two = lax.rsqrt(jnp.mean(hidden * hidden, axis=-1, keepdims=True) + EPS)
    b_own = (hidden * inv_two * ffn_gain).astype(BF16)
    logits = jnp.where(lane < 32, dot(b_own, tails), NEG)
    expo = jnp.exp(logits - jnp.max(logits, axis=-1, keepdims=True))
    probs = expo / jnp.sum(expo, axis=-1, keepdims=True)
    routed = rt_ref[wide]
    gates = probs * routed
    gates_high = gates.astype(BF16).astype(F32)
    ball[q, core, :, 0:width] = b_own
    ball[q, core, :, width : width + TAIL] = (
        gates_high + pltpu.roll(gates - gates_high, 32, 1)
    ).astype(BF16)
    g_ball = Gather(nq, q, core, plane, sibling, ball, l_ball, s_ball)
    g_ball.start()
    loop(1, n_ten, lambda k: start_all([passed_copy(1, k), passed_copy(2, k)]))
    g_cot.forward()
    g_ball.forward()
    loop(1, n_ten, lambda k: wait_recv_all(own_copies(k)))
    loop(1, n_ten, lambda k: wait_recv_all(passed_copies(k)))
    g_cot.finish()
    g_ball.finish()

    expert = 2 * c + d
    gate_lane = (lane == expert) | (lane == expert + 32)
    block = 8 * quarter
    steps = nq // 4

    def tokens(ref, i, cut_at, cut_to):
        return ref[pl.ds(4 * i, 4), :, :, cut_at:cut_to].reshape(block, cut_to - cut_at)

    def rows_of(i):
        return pl.ds(pl.multiple_of(i * block, block), block)

    def expert_block(i):
        b = tokens(ball, i, 0, width)
        packed = tokens(ball, i, width, width + TAIL).astype(F32)
        gate = jnp.sum(jnp.where(gate_lane, packed, 0.0), axis=-1, keepdims=True)
        gp = dot(b, wg[...])
        up = dot(b, wu[...])
        du = dot_nt(tokens(cotall, i, 0, width), wd[...])
        sigma = 1.0 / (1.0 + jnp.exp(-gp))
        silu = gp * sigma
        u = (silu * up).astype(BF16).astype(F32)
        dgate = jnp.sum(du * u, axis=-1, keepdims=True)
        du = gate * du
        dgp = (du * up * sigma * (1.0 + gp * (1.0 - sigma))).astype(BF16)
        dup = (du * silu).astype(BF16)
        dgp_ref[rows_of(i)] = dgp
        dup_ref[rows_of(i)] = dup
        ug_ref[rows_of(i)] = (gate * u).astype(BF16)
        db = dot_nt(dgp, wg[...]) + dot_nt(dup, wu[...])
        dbs[pl.ds(4 * i, 4), :, :, 0:width] = db.astype(BF16).reshape(4, 2, quarter, width)
        dbs[pl.ds(4 * i, 4), :, :, width : width + TAIL] = (
            jnp.where(lane == expert, dgate, 0.0).astype(BF16).reshape(4, 2, quarter, TAIL)
        )

    loop(0, steps, expert_block)
    x_dbs = Scatter(nq, q, core, plane, sibling, dbs, dbs_half, dbs_land, s_dbs)
    x_dbs.start()

    def down_block(i):
        y = dot(ug_ref[rows_of(i)], wd[...])
        ys[pl.ds(4 * i, 4)] = y.astype(BF16).reshape(4, 2, quarter, width)

    loop(0, steps, down_block)
    x_dbs.send()
    x_ys = Scatter(nq, q, core, plane, sibling, ys, ys_half, ys_land, s_ys)
    x_ys.start()

    def grad_copy(which, table, land, k):
        place = f_rows(lax.rem(r + k, n_ten))
        cut_out = table.at[place] if which == 2 else table.at[:, place]
        return remote(
            cut_out, land.at[k], s_grad.at[2 * which, k], s_grad.at[2 * which + 1, k], tensor(k)
        )

    def grad_copies(k):
        return [
            grad_copy(0, gg, gg_land, k),
            grad_copy(1, gu, gu_land, k),
            grad_copy(2, gd, gd_land, k),
        ]

    all_cot = cotall[...].reshape(nq * 2 * quarter, width)
    all_b = ball[:, :, :, 0:width].reshape(nq * 2 * quarter, width)
    gd[...] = dot_tn(ug_ref[...], all_cot).astype(BF16)
    loop(1, n_ten, lambda k: grad_copy(2, gd, gd_land, k).start())
    gg[...] = dot_tn(all_b, dgp_ref[...]).astype(BF16)
    gu[...] = dot_tn(all_b, dup_ref[...]).astype(BF16)

    summed = x_dbs.total()
    dprobs = routed * summed[:, width : width + TAIL]
    dlogits = probs * (dprobs - jnp.sum(probs * dprobs, axis=-1, keepdims=True))
    dlogits = jnp.where(lane < 32, dlogits, 0.0).astype(BF16)
    db = summed[:, 0:width] + dot_nt(dlogits, tails)
    w_db = db * ffn_gain
    grad_hidden = (
        cotall[q, core].astype(F32)
        + inv_two * w_db
        - hidden * inv_two**3 * (jnp.sum(w_db * hidden, axis=-1, keepdims=True) / width)
    )
    ffn_gain_rows = (db * hidden * inv_two).astype(BF16)
    dall[r] = grad_hidden.astype(BF16)

    def spread(table, sems, k):
        mine = table.at[r]
        return remote(mine, mine, sems.at[0, k], sems.at[1, k], tensor(k))

    loop(1, n_ten, lambda k: spread(dall, s_dall, k).start())
    x_ys.send()
    one_hot = lax.broadcasted_iota(jnp.int32, (rows, TAIL), 1)
    ones_ffn = jnp.where(one_hot[0:quarter] == 32, 1.0, 0.0).astype(BF16)
    ones_attn = jnp.where(one_hot == 33, 1.0, 0.0).astype(BF16)
    tail_grad = dot_tn(b_own, dlogits) + dot_tn(ffn_gain_rows, ones_ffn)
    loop(1, n_ten, lambda k: spread(dall, s_dall, k).wait_recv())

    loop(1, n_ten, lambda k: grad_copy(0, gg, gg_land, k).start())
    d_attn = dall[...].reshape(rows, width)

    def to_rows(grad):
        return grad.astype(BF16).reshape(nq, 2, 32, grad.shape[1])

    wgo[...] = to_rows(dot_tn(d_attn, o_low))
    x_wgo = Scatter(nq, q, core, plane, sibling, wgo, wgo_half, wgo_land, s_wgo)
    x_wgo.start()
    do = dot(d_attn, w_out).astype(BF16)
    for t in range(2):
        tile = do[:, 128 * t : 128 * t + 128].astype(F32)
        for g in range(2):
            dos[2 * t + g] = jnp.where(group_of == g, tile, 0.0).astype(BF16)

    dq_ref[...] = jnp.zeros_like(dq_ref)
    x_wgo.send()

    def head_backward(i):
        go = dos[i]
        delta = jnp.sum(go.astype(F32) * o_ref[i // 2], axis=-1, keepdims=True)
        dp = dot_nt(go, kv[:, :, :, 128:256].reshape(seq, 128))
        grad = (p_ref[i].astype(F32) * (dp - delta)).astype(BF16)
        ds_ref[i] = grad
        dq = dot(grad, kv[:, :, :, 0:128].reshape(seq, 128))
        dq_ref[i // 2] += jnp.where(group_of == lax.rem(i, 2), dq, 0.0)

    loop(0, 4, head_backward)
    all_q = qs[...].reshape(4 * rows, 128)
    all_do = dos[...].reshape(4 * rows, 128)
    for i in range(4):
        span = slice(i * (seq // 4), (i + 1) * (seq // 4))
        place = slice(i * (nj // 4), (i + 1) * (nj // 4))
        dk = dot_tn(ds_ref[:, :, span].reshape(4 * rows, seq // 4), all_q)
        dv = dot_tn(p_ref[:, :, span].reshape(4 * rows, seq // 4), all_do)
        dkv[place, :, :, 0:128] = dk.astype(BF16).reshape(nj // 4, 2, rows, 128)
        dkv[place, :, :, 128:256] = dv.astype(BF16).reshape(nj // 4, 2, rows, 128)
    x_dkv = Scatter(nj, j, core, along, sibling, dkv, dkv_half, dkv_land, s_dkv)
    x_dkv.start()

    a_low = a_ref[...]
    dq_lin = jnp.concatenate([unrope(dq_ref[0]), unrope(dq_ref[1])], axis=1) * 0.125
    dq_lin = dq_lin.astype(BF16)
    x_dkv.send()
    start_all([grad_copy(1, gu, gu_land, 1), grad_copy(1, gu, gu_land, n_ten - 1)])
    wgq[...] = to_rows(dot_tn(a_low, dq_lin))
    x_wgq = Scatter(nq, q, core, plane, sibling, wgq, wgq_half, wgq_land, s_wgq)
    x_wgq.start()
    da = dot_nt(dq_lin, wall[:, :, :, 0:256].reshape(width, 256))
    x_wgq.send()
    grad_kv = x_dkv.total()
    dkv_lin = jnp.concatenate([unrope(grad_kv[:, 0:128]), grad_kv[:, 128:256]], axis=1)
    dkv_lin = dkv_lin.astype(BF16)
    da = da + dot_nt(dkv_lin, wall[:, :, :, 256:512].reshape(width, 256))
    part[1] = da.astype(BF16).reshape(n_ten, quarter, width)
    loop(1, n_ten, lambda k: tensor_copy(1, s_y2, k).start())
    wgk[:, :, :, 0:256] = to_rows(dot_tn(a_low, dkv_lin))
    attn_gain_rows = (da * x_ref[...].astype(F32) * inv).astype(BF16)
    wgk[:, :, :, 256:384] = to_rows(tail_grad + dot_tn(attn_gain_rows, ones_attn))
    x_wgk = Scatter(nq, q, core, plane, sibling, wgk, wgk_half, wgk_land, s_wgk)
    x_wgk.start()

    hall[r] = (hidden + x_ys.total()).astype(BF16)
    x_wgk.send()
    loop(1, n_ten, lambda k: spread(hall, s_fin, k).start())

    grad_a = part[1, r].astype(F32)
    for k in range(1, n_ten):
        tensor_copy(1, s_y2, k).wait_recv()
        grad_a = grad_a + ybuf[1, k].astype(F32)
    x_own = x_ref[wide].astype(F32)
    inv_own = lax.rsqrt(jnp.mean(x_own * x_own, axis=-1, keepdims=True) + EPS)
    w_da = grad_a * attn_gain
    grad_x = (
        grad_hidden
        + inv_own * w_da
        - x_own * inv_own**3 * (jnp.sum(w_da * x_own, axis=-1, keepdims=True) / width)
    )
    igall[r] = grad_x.astype(BF16)

    def spread_ig(k):
        mine = igall.at[r]
        return remote(mine, mine, s_fin.at[2, k], s_fin.at[3, k], tensor(k))

    loop(1, n_ten, lambda k: spread_ig(k).start())
    loop(2, n_ten - 1, lambda k: grad_copy(1, gu, gu_land, k).start())

    def reduce_grads(table, land, place, land_place):
        same = table[place].astype(F32)
        for k in range(1, n_ten):
            same = same + land[(k, *land_place)].astype(F32)
        return same

    sides = ((gg, gg_land, gg_out), (gu, gu_land, gu_out), (gd, gd_land, gd_out))
    whole = slice(None)

    def half_sum(i, dp):
        table, land, _ = sides[i]
        if i == 2:
            return reduce_grads(table, land, (f_rows(r), d_rows(dp)), (whole, d_rows(dp)))
        return reduce_grads(table, land, (d_rows(dp), f_rows(r)), (d_rows(dp), whole))

    def half_copy(i):
        out = sides[i][2]
        return remote(
            out.at[0], out.at[1], s_grad.at[2 * i, 0], s_grad.at[2 * i + 1, 0], partner_dp
        )

    for i, out in ((2, od_ref), (0, og_ref), (1, ou_ref)):
        loop(1, n_ten, lambda k: grad_copy(i, *sides[i][:2], k).wait_recv())
        sides[i][2][0] = half_sum(i, 1 - d).astype(BF16)
        half_copy(i).start()
        out[d] = half_sum(i, d)

    stores = []

    def store(src, dst):
        stores.append(pltpu.make_async_copy(src, dst, s_out.at[len(stores)]))
        stores[-1].start()

    for i, out, dst in ((2, od_ref, o_wd), (0, og_ref, o_wg), (1, ou_ref, o_wu)):
        half_copy(i).wait_recv()
        out[1 - d] = sides[i][2][1].astype(F32)
        store(out, dst)

    loop(1, n_ten, lambda k: spread(hall, s_fin, k).wait_recv())
    store(hall, o_h)
    loop(1, n_ten, lambda k: spread_ig(k).wait_recv())
    ig_ref[...] = igall[...].astype(F32)
    store(ig_ref, o_ig)

    def store_pair(first, total, dst):
        for i, tile in enumerate(swap_heads(total)):
            w_ref[:, first + 128 * i : first + 128 * i + 128] = tile
        store(w_ref.at[:, first : first + 256], dst)

    store_pair(512, x_wgo.total(), o_o)
    store_pair(0, x_wgq.total(), o_q)
    grads = x_wgk.total()
    w_ref[:, 256:512] = grads[:, 0:256]
    store(w_ref.at[:, 256:384], o_k)
    store(w_ref.at[:, 384:512], o_v)
    tail_y[0] = grads[:, 256:384]

    def tail_copy(k):
        return remote(tail_y.at[0], tail_y.at[k], s_fin.at[4, k], s_fin.at[5, k], tensor(k))

    loop(1, n_ten, lambda k: tail_copy(k).start())
    tail_sum = grads[:, 256:384]
    for k in range(1, n_ten):
        tail_copy(k).wait_recv()
        tail_sum = tail_sum + tail_y[k]
    t_ref[...] = tail_sum
    store(t_ref, o_t)

    for copy in stores:
        copy.wait()
    for gather in (g_wall, g_wout, g_cot, g_kv, g_ball):
        gather.drain()
    for scatter in (x_dbs, x_ys, x_dkv, x_wgo, x_wgq, x_wgk):
        scatter.drain()

    def drain_tensor(k):
        tensor_copy(0, s_y1, k).wait_send()
        tensor_copy(1, s_y2, k).wait_send()
        spread(dall, s_dall, k).wait_send()
        spread(hall, s_fin, k).wait_send()
        spread_ig(k).wait_send()
        tail_copy(k).wait_send()

    loop(1, n_ten, drain_tensor)

    wait_send_all(across_copies())

    def drain_experts(k):
        wait_send_all(own_copies(k))
        wait_send_all(passed_copies(k))
        wait_send_all(grad_copies(k))

    loop(1, n_ten, drain_experts)
    for i in range(3):
        half_copy(i).wait_send()


def call_layer(sizes, xin, cot, seg, rts, gain_a, gain_f, wq, wk, wv, wo, wr, wgi, wui, wdi):
    n_dp, n_ctx, n_ten = sizes
    nj = n_ctx // 2
    nq = n_dp * nj
    rows, width = xin.shape
    seq = n_ctx * rows
    quarter = rows // n_ten
    half_d, cut = wgi.shape[1], wgi.shape[2]
    hidden_units = cut * n_ten
    all_rows = nq * 2 * quarter

    def shape(*dims, kind=F32):
        return jax.ShapeDtypeStruct(dims, kind)

    def low(*dims):
        return pltpu.VMEM(dims, BF16)

    def full(*dims):
        return pltpu.VMEM(dims, F32)

    def sems(*dims):
        return pltpu.SemaphoreType.DMA(dims)

    scratch = [
        low(nq, 2, 32, 640),
        low(nq, 2, 32, 256),
        low(nq, 2, quarter, width),
        low(nq, 2, quarter, width + TAIL),
        low(nj, 2, rows, 256),
        low(width, hidden_units),
        low(width, hidden_units),
        low(hidden_units, width),
        low(rows, width),
        full(rows, 128),
        full(n_ten, quarter, width),
        full(32, 768),
        full(32, TAIL),
        full(2, half_d, cut),
        full(2, half_d, cut),
        full(2, cut, half_d),
        low(rows, width),
        low(4, rows, 128),
        low(4, rows, seq),
        low(4, rows, seq),
        full(2, rows, 128),
        low(2, n_ten, quarter, width),
        low(2, n_ten, quarter, width),
        low(n_ten, quarter, width),
        low(n_ten, quarter, width),
        low(n_ten, quarter, width),
        low(all_rows, hidden_units),
        low(all_rows, hidden_units),
        low(all_rows, hidden_units),
        low(nq, 2, quarter, width + TAIL),
        low(nq, quarter, width + TAIL),
        low(nq, quarter, width + TAIL),
        low(nq, 2, quarter, width),
        low(nq, quarter, width),
        low(nq, quarter, width),
        low(width, hidden_units),
        low(width, hidden_units),
        low(hidden_units, width),
        low(n_ten, width, cut),
        low(n_ten, width, cut),
        low(n_ten, cut, width),
        low(2, half_d, cut),
        low(2, half_d, cut),
        low(2, cut, half_d),
        low(4, rows, 128),
        full(2, rows, 128),
        low(nj, 2, rows, 256),
        low(nj, rows, 256),
        low(nj, rows, 256),
        low(nq, 2, 32, 256),
        low(nq, 32, 256),
        low(nq, 32, 256),
        low(nq, 2, 32, 256),
        low(nq, 32, 256),
        low(nq, 32, 256),
        low(nq, 2, 32, 384),
        low(nq, 32, 384),
        low(nq, 32, 384),
        full(n_ten, 32, TAIL),
        sems(nq),
        sems(3),
        sems(nq),
        sems(3),
        sems(nq),
        sems(3),
        sems(nq),
        sems(3),
        sems(nj),
        sems(3),
        sems(12, n_ten),
        sems(2, n_ten),
        sems(4),
        sems(4),
        sems(6, n_ten),
        sems(2, n_ten),
        sems(4),
        sems(2, n_ten),
        sems(4),
        sems(4),
        sems(4),
        sems(6, n_ten),
        sems(5),
        sems(10),
    ]
    far, near = pl.BlockSpec(memory_space=pltpu.HBM), pl.BlockSpec(memory_space=pltpu.VMEM)
    flops = 2 * (9 * all_rows * width * hidden_units + 4 * rows * width * 768)
    return pl.pallas_call(
        functools.partial(layer, sizes),
        out_shape=(
            shape(n_ten, quarter, width, kind=BF16),
            shape(n_ten, quarter, width),
            shape(32, 256),
            shape(32, 128),
            shape(32, 128),
            shape(32, 256),
            shape(32, TAIL),
            shape(2, half_d, cut),
            shape(2, half_d, cut),
            shape(2, cut, half_d),
        ),
        in_specs=[far, far] + [near] * 9 + [far] * 3,
        out_specs=[far] * 10,
        scratch_shapes=scratch,
        compiler_params=pltpu.CompilerParams(
            collective_id=0, has_side_effects=True, vmem_limit_bytes=VMEM_BYTES
        ),
        cost_estimate=pl.CostEstimate(flops=flops, bytes_accessed=8 << 20, transcendentals=0),
    )(xin, cot, seg, rts, gain_a, gain_f, wq, wk, wv, wo, wr, wgi, wui, wdi)


def hand_over(*refs):
    sources, tail = refs[:9], refs[9]
    results, gain_a, gain_f, router, sems = refs[10:19], *refs[19:]
    copies = [
        pltpu.make_async_copy(src, dst, sems.at[i])
        for i, (src, dst) in enumerate(zip(sources, results))
    ]
    for copy in copies:
        copy.start()
    router[...] = tail[:, 0:32]
    up = lax.broadcasted_iota(jnp.int32, (32, 32), 0)
    same = up == lax.broadcasted_iota(jnp.int32, (32, 32), 1)
    gain_a[...] = jnp.sum(jnp.where(same, tail[:, 33:34], 0.0), axis=0, keepdims=True)
    gain_f[...] = jnp.sum(jnp.where(same, tail[:, 32:33], 0.0), axis=0, keepdims=True)
    for copy in copies:
        copy.wait()


def call_hand_over(arrays, tail):
    far, near = pl.BlockSpec(memory_space=pltpu.HBM), pl.BlockSpec(memory_space=pltpu.VMEM)
    small = [(1, 32), (1, 32), (32, 32)]
    return pl.pallas_call(
        hand_over,
        out_shape=[jax.ShapeDtypeStruct(a.shape, a.dtype) for a in arrays]
        + [jax.ShapeDtypeStruct(dims, F32) for dims in small],
        in_specs=[near] * (len(arrays) + 1),
        out_specs=[far] * len(arrays) + [near] * 3,
        scratch_shapes=[pltpu.SemaphoreType.DMA((len(arrays),))],
        compiler_params=pltpu.CompilerParams(vmem_limit_bytes=VMEM_BYTES),
    )(*arrays, tail)


def per_device(
    hidden_in,
    segments,
    routes,
    norm_attn,
    w_query,
    w_key,
    w_value,
    w_out,
    norm_ffn,
    w_router,
    w_gate,
    w_up,
    w_down,
    cotangent,
):
    sizes = (lax.axis_size("dp"), lax.axis_size("context"), lax.axis_size("tensor"))
    out, grad, wq, wk, wv, wo, tail, gate_grad, up_grad, down_grad = call_layer(
        sizes,
        hidden_in,
        cotangent,
        segments,
        routes[0].T,
        norm_attn,
        norm_ffn,
        w_query[0],
        w_key[0],
        w_value[0],
        w_out[0].T,
        w_router[0],
        w_gate[0],
        w_up[0],
        w_down[0],
    )
    arrays = (
        out.reshape(hidden_in.shape),
        grad.reshape(hidden_in.shape),
        wq,
        wk,
        wv,
        wo,
        gate_grad,
        up_grad,
        down_grad,
    )
    results = call_hand_over(arrays, tail)
    out, grad, wq, wk, wv, wo, gate_grad, up_grad, down_grad, gain_a, gain_f, router = results
    return (
        out,
        grad,
        gain_a,
        wq[None],
        wk[None],
        wv[None],
        wo.T[None],
        gain_f,
        router[None],
        gate_grad[None],
        up_grad[None],
        down_grad[None],
    )


def solution(mesh):
    in_specs = (
        P(("dp", "context"), None),
        P("dp", "context"),
        P(None, ("dp", "context"), None),
        P(None, ("dp", "context")),
        P(None, ("dp", "context"), "tensor"),
        P(None, ("dp", "context"), "tensor"),
        P(None, ("dp", "context"), "tensor"),
        P(None, "tensor", ("dp", "context")),
        P(None, ("dp", "context")),
        P(None, ("dp", "context"), None),
        P(None, "context", "dp", "tensor"),
        P(None, "context", "dp", "tensor"),
        P(None, "context", "tensor", "dp"),
        P(("dp", "context"), None),
    )
    out_specs = (
        P(("dp", "context"), None),
        P(("dp", "context"), None),
        P(None, ("dp", "context")),
        P(None, ("dp", "context"), "tensor"),
        P(None, ("dp", "context"), "tensor"),
        P(None, ("dp", "context"), "tensor"),
        P(None, "tensor", ("dp", "context")),
        P(None, ("dp", "context")),
        P(None, ("dp", "context"), None),
        P(None, "context", "dp", "tensor"),
        P(None, "context", "dp", "tensor"),
        P(None, "context", "tensor", "dp"),
    )
    return jax.shard_map(
        per_device, mesh=mesh, in_specs=in_specs, out_specs=out_specs, check_vma=False
    )
```

```python
import functools
import math

import jax
import jax.numpy as jnp
from jax import lax
from jax.experimental import pallas as pl
from jax.experimental.pallas import tpu as pltpu
from jax.sharding import PartitionSpec as P

HEAD = 64
EPS = 1e-06
NEG = -1e30
F32 = jnp.float32
BF16 = jnp.bfloat16
TAIL = 128
VMEM_BYTES = 60 * 1024 * 1024


def dot(a, b):
    return jnp.dot(a, b, preferred_element_type=F32)


def dot_nt(a, b):
    return lax.dot_general(a, b, (((1,), (1,)), ((), ())), preferred_element_type=F32)


def dot_tn(a, b):
    return lax.dot_general(a, b, (((0,), (0,)), ((), ())), preferred_element_type=F32)


def remote(src, dst, send_sem, recv_sem, device):
    return pltpu.make_async_remote_copy(
        src_ref=src,
        dst_ref=dst,
        send_sem=send_sem,
        recv_sem=recv_sem,
        device_id=device,
        device_id_type=pl.DeviceIdType.MESH,
    )


def loop(start, stop, step):
    def body(k, carry):
        step(k)
        return carry

    lax.fori_loop(start, stop, body, 0)


class Gather:
    def __init__(self, count, me, core, peer, sibling, table, landed, sems):
        self.count, self.me, self.core = count, me, core
        self.peer, self.sibling, self.table = peer, sibling, table
        self.landed, self.sems = landed, sems

    def far(self, k):
        mine = self.table.at[self.me, self.core]
        return remote(mine, mine, self.sems.at[0], self.landed.at[k], self.peer(k))

    def near(self, k):
        chunk = self.table.at[lax.rem(self.me + self.count - k, self.count), self.core]
        return remote(chunk, chunk, self.sems.at[1], self.sems.at[2], self.sibling)

    def start(self):
        loop(1, self.count, lambda k: self.far(k).start())
        self.near(0).start()

    def forward(self):
        def step(k):
            self.far(k).wait_recv()
            self.near(k).start()

        loop(1, self.count, step)

    def near_all(self, side):
        whole = self.table.at[:, side]
        return remote(whole, whole, self.sems.at[1], self.sems.at[2], self.sibling)

    def finish(self):
        self.near_all(1 - self.core).wait_recv()

    def drain(self):
        others = self.table.at[pl.ds(0, self.count - 1), self.core]
        remote(others, others, self.sems.at[0], self.landed.at[0], self.sibling).wait_send()
        self.near_all(self.core).wait_send()


class Scatter:
    def __init__(self, count, me, core, peer, sibling, parts, half, landed, sems):
        self.count, self.me, self.core = count, me, core
        self.peer, self.sibling = peer, sibling
        self.parts, self.half, self.landed, self.sems = parts, half, landed, sems

    def near(self):
        return remote(
            self.parts.at[:, 1 - self.core],
            self.half,
            self.sems.at[0],
            self.sems.at[1],
            self.sibling,
        )

    def far(self, k):
        there = lax.rem(self.me + k, self.count)
        return remote(
            self.half.at[there],
            self.landed.at[k],
            self.sems.at[2],
            self.sems.at[3],
            self.peer(k),
        )

    def far_all(self):
        return remote(
            self.half.at[pl.ds(1, self.count - 1)],
            self.landed.at[pl.ds(1, self.count - 1)],
            self.sems.at[2],
            self.sems.at[3],
            self.sibling,
        )

    def start(self):
        self.near().start()

    def send(self):
        self.near().wait_recv()

        def add(there):
            mine = self.parts[there, self.core].astype(F32)
            self.half[there] = (mine + self.half[there].astype(F32)).astype(BF16)

        def step(k):
            add(lax.rem(self.me + k, self.count))
            self.far(k).start()

        loop(1, self.count, step)
        add(self.me)

    def total(self):
        self.far_all().wait_recv()

        def step(k, acc):
            return acc + self.landed[k].astype(F32)

        return lax.fori_loop(1, self.count, step, self.half[self.me].astype(F32))

    def drain(self):
        self.near().wait_send()
        self.far_all().wait_send()


class Plane:
    def __init__(self, d, x, zh, nx, core, sibling, x_peer, z_peer):
        self.d, self.x, self.zh, self.nx = d, x, zh, nx
        self.core, self.sibling = core, sibling
        self.x_peer, self.z_peer = x_peer, z_peer

    def x_at(self, k):
        return lax.rem(self.x + k + self.nx, self.nx)

    def z_at(self, k):
        z = lax.rem(2 * self.d + self.zh + k + 4, 4)
        return z // 2, lax.rem(z, 2)


def upper(rows):
    return pl.ds(0, rows // 2)


def lower(rows):
    return pl.ds(rows // 2, rows // 2)


class PlaneGather:
    def __init__(self, plane, table, landed, sems):
        self.plane, self.table, self.landed, self.sems = plane, table, landed, sems
        rows = table.shape[4]
        self.up, self.down = upper(rows), lower(rows)

    def line(self, k):
        d, zh = self.plane.z_at(k)
        return self.table.at[d, :, zh, self.plane.core, self.up]

    def column(self, k):
        return self.table.at[:, self.plane.x_at(k), :, self.plane.core, self.down]

    def send(self, part, stage, k, device):
        remote(part, part, self.sems.at[stage], self.landed.at[stage, k], device).start()

    def landing(self, part, stage, k):
        return remote(
            part, part, self.sems.at[stage], self.landed.at[stage, k], self.plane.sibling
        )

    def pass_on(self, k):
        for part in (self.line(-k), self.column(-k)):
            remote(part, part, self.sems.at[2], self.sems.at[3], self.plane.sibling).start()

    def start(self):
        p = self.plane
        chunk = self.table.at[p.d, p.x, p.zh, p.core]

        def step(k):
            self.send(chunk.at[self.up], 0, k, p.x_peer(k))
            self.send(chunk.at[self.down], 0, k, p.z_peer(k))

        loop(1, p.nx, step)

    def forward(self):
        p = self.plane
        loop(1, p.nx, lambda k: self.landing(self.table.at[0, 0, 0, p.core], 0, k).wait_recv())

        def step(k):
            self.send(self.line(0), 1, k, p.z_peer(k))
            self.send(self.column(0), 1, k, p.x_peer(k))

        loop(1, p.nx, step)
        self.pass_on(0)

    def forward_rest(self):
        p = self.plane

        def arrive(k):
            self.landing(self.table.at[0, :, 0, p.core], 1, k).wait_recv()
            self.pass_on(k)

        loop(1, p.nx, arrive)

    def near_all(self, side):
        whole = self.table.at[:, :, :, side]
        return remote(whole, whole, self.sems.at[2], self.sems.at[3], self.plane.sibling)

    def finish(self):
        self.near_all(1 - self.plane.core).wait_recv()

    def drain(self):
        core, others = self.plane.core, pl.ds(0, self.plane.nx - 1)
        self.landing(self.table.at[0, others, 0, core], 0, 0).wait_send()
        self.landing(self.table.at[:, others, :, core], 1, 0).wait_send()
        self.near_all(core).wait_send()


class PlaneScatter:
    def __init__(self, plane, parts, half, line, column, last, landed, sems):
        self.plane, self.parts, self.half = plane, parts, half
        self.line, self.column, self.last = line, column, last
        self.landed, self.sems = landed, sems
        rows = parts.shape[4]
        self.up, self.down = upper(rows), lower(rows)

    def copy(self, src, dst, stage, k, device):
        return remote(src, dst, self.sems.at[stage], self.landed.at[stage, k], device)

    def near(self):
        p = self.plane
        away = self.parts.at[:, :, :, 1 - p.core]
        return remote(away, self.half, self.sems.at[2], self.sems.at[3], p.sibling)

    def start(self):
        self.near().start()

    def send(self):
        p = self.plane
        self.near().wait_recv()

        def add(i):
            spot = (i // (2 * p.nx), lax.rem(i // 2, p.nx), lax.rem(i, 2))
            mine = self.parts[(*spot, p.core)].astype(F32)
            self.half[spot] = (mine + self.half[spot].astype(F32)).astype(BF16)

        loop(0, 4 * p.nx, add)

        def step(k):
            d, zh = p.z_at(k)
            there = self.half.at[d, :, zh, self.up]
            self.copy(there, self.line.at[k], 0, k, p.z_peer(k)).start()
            there = self.half.at[:, p.x_at(k), :, self.down]
            self.copy(there, self.column.at[k], 0, k, p.x_peer(k)).start()

        loop(1, p.nx, step)

    def middle(self):
        p = self.plane

        def arrive(k):
            two = self.line.at[pl.ds(0, 2)]
            self.copy(two, two, 0, k, p.sibling).wait_recv()

        loop(1, p.nx, arrive)

        def add_line(k):
            spot = (p.d, p.x_at(k), p.zh, self.up)
            total = self.half[spot].astype(F32)
            for i in range(1, p.nx):
                total = total + self.line[i, p.x_at(k)].astype(F32)
            self.half[spot] = total.astype(BF16)

        def add_column(k):
            d, zh = p.z_at(k)
            spot = (d, p.x, zh, self.down)
            total = self.half[spot].astype(F32)
            for i in range(1, p.nx):
                total = total + self.column[i, d, zh].astype(F32)
            self.half[spot] = total.astype(BF16)

        def step(k):
            add_line(k)
            spot = self.half.at[p.d, p.x_at(k), p.zh, self.up]
            self.copy(spot, self.last.at[k, self.up], 1, k, p.x_peer(k)).start()
            add_column(k)
            d, zh = p.z_at(k)
            spot = self.half.at[d, p.x, zh, self.down]
            self.copy(spot, self.last.at[k, self.down], 1, k, p.z_peer(k)).start()

        loop(1, p.nx, step)
        add_line(0)
        add_column(0)

    def total(self):
        p = self.plane
        total = self.half[p.d, p.x, p.zh].astype(F32)
        for k in range(1, p.nx):
            self.copy(self.last.at[k], self.last.at[k], 1, k, p.sibling).wait_recv()
            total = total + self.last[k].astype(F32)
        return total

    def drain(self):
        p, others = self.plane, pl.ds(0, self.plane.nx - 1)
        self.near().wait_send()
        first = self.half.at[:, others]
        self.copy(first, first, 0, 0, p.sibling).wait_send()
        second = self.half.at[0, others, 0]
        self.copy(second, second, 1, 0, p.sibling).wait_send()


def layer(
    sizes,
    xin,
    cot,
    seg,
    rts,
    gain_a,
    gain_f,
    wq,
    wk,
    wv,
    wo,
    wr,
    wgi,
    wui,
    wdi,
    o_h,
    o_ig,
    o_q,
    o_k,
    o_v,
    o_o,
    o_t,
    o_wg,
    o_wu,
    o_wd,
    wall,
    wall_out,
    cotall,
    ball,
    kv,
    wg,
    wu,
    wd,
    x_ref,
    rt_ref,
    ig_ref,
    w_ref,
    t_ref,
    og_ref,
    ou_ref,
    od_ref,
    a_ref,
    qs,
    p_ref,
    ds_ref,
    o_ref,
    part,
    ybuf,
    hall,
    dall,
    igall,
    dgp_ref,
    dup_ref,
    ug_ref,
    dbs,
    dbs_half,
    dbs_line,
    dbs_column,
    dbs_last,
    ys,
    ys_half,
    ys_line,
    ys_column,
    ys_last,
    gg,
    gu,
    gd,
    gg_land,
    gu_land,
    gd_land,
    gg_relay,
    gu_relay,
    gd_relay,
    gg_out,
    gu_out,
    gd_out,
    dos,
    dq_ref,
    dkv,
    dkv_half,
    dkv_land,
    wgo,
    wgo_half,
    wgo_line,
    wgo_column,
    wgo_last,
    wgq,
    wgq_half,
    wgq_line,
    wgq_column,
    wgq_last,
    wgk,
    wgk_half,
    wgk_line,
    wgk_column,
    wgk_last,
    tail_y,
    l_wall,
    s_wall,
    l_wout,
    s_wout,
    l_cot,
    s_cot,
    l_ball,
    s_ball,
    l_kv,
    s_kv,
    s_exp,
    s_y1,
    l_dbs,
    s_dbs,
    l_ys,
    s_ys,
    s_grad,
    s_dall,
    s_dkv,
    s_y2,
    l_wgo,
    s_wgo,
    l_wgq,
    s_wgq,
    l_wgk,
    s_wgk,
    s_fin,
    s_in,
    s_out,
):
    n_dp, n_ctx, n_ten = sizes
    nj = n_ctx // 2
    nq = n_dp * nj
    rows, width = xin.shape
    seq = n_ctx * rows
    quarter = rows // n_ten
    d, c, r = lax.axis_index("dp"), lax.axis_index("context"), lax.axis_index("tensor")
    core, j = lax.rem(c, 2), c // 2

    def at(dp, context, tensor):
        return {"dp": dp, "context": context, "tensor": tensor}

    nx = nj // 2
    x_here, zh = j // 2, lax.rem(j, 2)

    def x_peer(k):
        return at(d, (lax.rem(x_here + k, nx) * 2 + zh) * 2 + core, r)

    def z_peer(k):
        z = lax.rem(2 * d + zh + k, 4)
        return at(z // 2, (x_here * 2 + lax.rem(z, 2)) * 2 + core, r)

    def along(k):
        return at(d, lax.rem(j + k, nj) * 2 + core, r)

    def tensor(k):
        return at(d, c, lax.rem(r + k, n_ten))

    partner_dp = at(1 - d, c, r)
    sibling = at(d, c + 1 - 2 * core, r)
    plane = Plane(d, x_here, zh, nx, core, sibling, x_peer, z_peer)
    own = (d, x_here, zh, core)

    wide = pl.ds(pl.multiple_of(r * quarter, quarter), quarter)
    half_d, cut = wgi.shape[1], wgi.shape[2]

    def d_rows(dp):
        return pl.ds(pl.multiple_of(dp * half_d, half_d), half_d)

    def f_rows(ten):
        return pl.ds(pl.multiple_of(ten * cut, cut), cut)

    here_g, here_u, here_d = (d_rows(d), f_rows(r)), (d_rows(d), f_rows(r)), (f_rows(r), d_rows(d))
    there_g, there_d = (d_rows(1 - d), f_rows(r)), (f_rows(r), d_rows(1 - d))

    barrier = pltpu.get_barrier_semaphore()

    def greet(device):
        pl.semaphore_signal(barrier, inc=1, device_id=device, device_id_type=pl.DeviceIdType.MESH)

    loop(1, nj, lambda k: greet(along(k)))
    loop(1, nx, lambda k: greet(z_peer(k)))
    greet(sibling)
    loop(1, n_ten, lambda k: greet(tensor(k)))

    loads = [
        pltpu.make_async_copy(src, dst, s_in.at[i])
        for i, (src, dst) in enumerate(
            (
                (xin, x_ref),
                (cot.at[wide], cotall.at[own]),
                (wgi.at[d], wg.at[here_g]),
                (wui.at[d], wu.at[here_u]),
                (wdi.at[d], wd.at[here_d]),
            )
        )
    ]
    for load in loads:
        load.start()

    lane = lax.broadcasted_iota(jnp.int32, (1, 128), 1)
    group_of = lane // HEAD

    def swap_heads(table):
        one, two = table[:, 0:128], table[:, 128:256]
        return (
            jnp.where(group_of == 0, one, pltpu.roll(two, HEAD, 1)),
            jnp.where(group_of == 0, pltpu.roll(one, HEAD, 1), two),
        )

    def diagonal(count, extent, first):
        up = lax.broadcasted_iota(jnp.int32, (count, extent), 0)
        return up + first == lax.broadcasted_iota(jnp.int32, (count, extent), 1)

    def as_column(row, count, first):
        picked = jnp.where(diagonal(count, row.shape[1], first), row, 0.0)
        return jnp.sum(picked, axis=1, keepdims=True)

    for i, tile in enumerate(swap_heads(wq[...].astype(F32))):
        wall[(*own, slice(None), slice(128 * i, 128 * i + 128))] = tile.astype(BF16)
    for i, tile in enumerate(swap_heads(wo[...].astype(F32))):
        wall_out[(*own, slice(None), slice(128 * i, 128 * i + 128))] = tile.astype(BF16)
    wall[(*own, slice(None), slice(256, 384))] = wk[...]
    wall[(*own, slice(None), slice(384, 512))] = wv[...]
    numbers_here = seg[...].astype(F32)
    tail = jnp.where(lane == 32, as_column(gain_a[...].astype(F32), 32, 0), 0.0)
    tail = jnp.where(lane == 33, as_column(gain_f[...].astype(F32), 32, 0), tail)
    for i in range(rows // 32):
        tail = jnp.where(lane == 34 + i, as_column(numbers_here, 32, 32 * i), tail)
    wall[(*own, slice(None), slice(512, 640))] = tail.astype(BF16)
    wall[(*own, slice(None), slice(512, 544))] = wr[...]

    pl.semaphore_wait(barrier, nj + nx + n_ten - 2)

    g_wall = PlaneGather(plane, wall, l_wall, s_wall)
    g_wall.start()
    g_wout = PlaneGather(plane, wall_out, l_wout, s_wout)

    def triple(sources, places, first_sem, k, device):
        return [
            remote(src, dst, s_exp.at[first_sem + 2 * i, k], s_exp.at[first_sem + 2 * i + 1, k], device)
            for i, (src, dst) in enumerate(zip(sources, places))
        ]

    landing = (wg.at[here_g], wu.at[here_u], wd.at[here_d])
    passed_on = (wg.at[there_g], wu.at[there_g], wd.at[there_d])
    sides_y = (1, n_ten - 1)

    def own_copies(k):
        return triple((wgi.at[d], wui.at[d], wdi.at[d]), landing, 0, k, tensor(k))

    def across_copies():
        return triple((wgi.at[1 - d], wui.at[1 - d], wdi.at[1 - d]), landing, 0, 0, partner_dp)

    def passed_copy(i, k):
        place = passed_on[i]
        return remote(place, place, s_exp.at[6 + 2 * i, k], s_exp.at[7 + 2 * i, k], tensor(k))

    def passed_copies(k):
        return [passed_copy(i, k) for i in range(3)]

    def relay_copies(dp, first_sem, side):
        ten = lax.rem(r + sides_y[1 - side], n_ten)
        step, narrow = half_d // 2, cut // 2
        d_half = pl.ds(pl.multiple_of(dp * half_d + side * step, step), step)
        f_half = pl.ds(pl.multiple_of(ten * cut + side * narrow, narrow), narrow)
        parts = (
            wg.at[d_half, f_rows(ten)],
            wu.at[d_half, f_rows(ten)],
            wd.at[f_half, d_rows(dp)],
        )
        return triple(parts, parts, first_sem, n_ten + side, tensor(sides_y[side]))

    def start_all(copies):
        for copy in copies:
            copy.start()

    def wait_recv_all(copies):
        for copy in copies:
            copy.wait_recv()

    def wait_send_all(copies):
        for copy in copies:
            copy.wait_send()

    for k in sides_y:
        start_all(own_copies(k))

    loads[0].wait()
    x = x_ref[...].astype(F32)
    inv = lax.rsqrt(jnp.mean(x * x, axis=-1, keepdims=True) + EPS)
    low_half = lax.rem(lane, HEAD) < HEAD // 2
    rate = jnp.exp(
        lax.rem(lane, HEAD // 2).astype(F32) * (-2.0 * math.log(10000.0) / HEAD)
    )
    row_index = c * rows + lax.broadcasted_iota(jnp.int32, (rows, 1), 0)
    angle = row_index.astype(F32) * rate
    cosine = jnp.cos(angle)
    sine = jnp.where(low_half, -1.0, 1.0) * jnp.sin(angle)

    def partner(z):
        return jnp.where(
            low_half, pltpu.roll(z, 128 - HEAD // 2, 1), pltpu.roll(z, HEAD // 2, 1)
        )

    def rope(z):
        return z * cosine + partner(z) * sine

    def unrope(z):
        return z * cosine - partner(z) * sine

    named = jnp.zeros((128, rows), F32)
    of_expert = lax.broadcasted_iota(jnp.int32, (128, rows), 0)
    for k in range(rts.shape[0]):
        named = named + jnp.where(rts[k : k + 1, :] == of_expert, 1.0, 0.0)
    rt_ref[...] = named.T
    for load in loads[1:]:
        load.wait()
    g_cot = PlaneGather(plane, cotall, l_cot, s_cot)

    g_wall.forward()
    g_wall.forward_rest()
    start_all(across_copies())
    g_wall.finish()
    for k in sides_y:
        wait_recv_all(own_copies(k))
    for side in range(2):
        start_all(relay_copies(d, 0, side))

    tails = wall[:, :, :, :, :, 512:640].reshape(width, TAIL)
    gains = tails.astype(F32).T
    attn_gain, ffn_gain = gains[32:33], gains[33:34]
    a_ref[...] = (x * inv * attn_gain).astype(BF16)

    qkv = dot(a_ref[...], wall[:, :, :, :, :, 0:512].reshape(width, 512))
    for t in range(2):
        turned = rope(qkv[:, 128 * t : 128 * t + 128]) * 0.125
        for g in range(2):
            qs[2 * t + g] = jnp.where(group_of == g, turned, 0.0).astype(BF16)
    kv[j, core, :, 0:128] = rope(qkv[:, 256:384]).astype(BF16)
    kv[j, core, :, 128:256] = qkv[:, 384:512].astype(BF16)
    g_kv = Gather(nj, j, core, along, sibling, kv, l_kv, s_kv)
    g_kv.start()
    g_wout.start()

    numbers = wall[d, :, :, :, :, 512:640].reshape(nj * 64, TAIL).astype(F32)
    held = jnp.where((lane >= 34) & (lane < 38), numbers, 1e9)
    mine = as_column(numbers_here, rows, 0)
    first = jnp.zeros((rows, 1), F32)
    for s in range(1, 4):
        below = jnp.sum(jnp.where(held < s - 0.5, 1.0, 0.0), axis=0, keepdims=True)
        below = jnp.sum(below, axis=1, keepdims=True)
        first = jnp.where(mine == s, below, first)
    first = first.astype(jnp.int32)
    columns = lax.broadcasted_iota(jnp.int32, (rows, seq), 1)
    allowed = (columns >= first) & (columns <= row_index)

    g_kv.forward()
    g_wout.forward()
    g_wout.forward_rest()
    g_kv.finish()
    wait_recv_all(across_copies())
    for k in sides_y:
        passed_copy(0, k).start()
    g_cot.start()

    o_ref[...] = jnp.zeros_like(o_ref)

    def head_forward(i):
        scores = dot_nt(qs[i], kv[:, :, :, 0:128].reshape(seq, 128))
        scores = jnp.where(allowed, scores, NEG)
        top = jnp.max(scores, axis=-1, keepdims=True)
        expo = jnp.where(allowed, jnp.exp(scores - top), 0.0)
        weights = (expo * (1.0 / jnp.sum(expo, axis=-1, keepdims=True))).astype(BF16)
        p_ref[i] = weights
        out = dot(weights, kv[:, :, :, 128:256].reshape(seq, 128))
        o_ref[i // 2] += jnp.where(group_of == lax.rem(i, 2), out, 0.0)

    loop(0, 4, head_forward)
    g_wout.finish()
    o_low = jnp.concatenate([o_ref[0], o_ref[1]], axis=1).astype(BF16)
    w_out = wall_out[...].reshape(width, 256)
    part[0] = dot_nt(o_low, w_out).astype(BF16).reshape(n_ten, quarter, width)

    def tensor_copy(which, sems, k):
        return remote(
            part.at[which, lax.rem(r + k, n_ten)],
            ybuf.at[which, k],
            sems.at[0, k],
            sems.at[1, k],
            tensor(k),
        )

    loop(1, n_ten, lambda k: tensor_copy(0, s_y1, k).start())
    hidden = x_ref[wide].astype(F32) + part[0, r].astype(F32)
    for k in range(1, n_ten):
        tensor_copy(0, s_y1, k).wait_recv()
        hidden = hidden + ybuf[0, k].astype(F32)

    inv_two = lax.rsqrt(jnp.mean(hidden * hidden, axis=-1, keepdims=True) + EPS)
    b_own = (hidden * inv_two * ffn_gain).astype(BF16)
    logits = jnp.where(lane < 32, dot(b_own, tails), NEG)
    expo = jnp.exp(logits - jnp.max(logits, axis=-1, keepdims=True))
    probs = expo / jnp.sum(expo, axis=-1, keepdims=True)
    routed = rt_ref[wide]
    gates = probs * routed
    gates_high = gates.astype(BF16).astype(F32)
    ball[(*own, slice(None), slice(0, width))] = b_own
    ball[(*own, slice(None), slice(width, width + TAIL))] = (
        gates_high + pltpu.roll(gates - gates_high, 32, 1)
    ).astype(BF16)
    g_ball = PlaneGather(plane, ball, l_ball, s_ball)
    g_ball.start()
    for k in sides_y:
        start_all([passed_copy(1, k), passed_copy(2, k)])
    g_cot.forward()
    g_cot.forward_rest()
    g_ball.forward()
    for k in sides_y:
        wait_recv_all(passed_copies(k))
    for side in range(2):
        start_all(relay_copies(1 - d, 6, side))
    g_ball.forward_rest()
    for side in range(2):
        wait_recv_all(relay_copies(d, 0, side))
        wait_recv_all(relay_copies(1 - d, 6, side))
    g_cot.finish()
    g_ball.finish()

    expert = 2 * c + d
    gate_lane = (lane == expert) | (lane == expert + 32)
    block = 8 * quarter
    steps = 4

    def place_of(i):
        whole = slice(None)
        return (i // 2, pl.ds(2 * lax.rem(i, 2), 2), whole, whole, whole)

    def tokens(ref, i, cut_at, cut_to):
        return ref[(*place_of(i), slice(cut_at, cut_to))].reshape(block, cut_to - cut_at)

    def rows_of(i):
        return pl.ds(pl.multiple_of(i * block, block), block)

    def expert_block(i):
        b = tokens(ball, i, 0, width)
        packed = tokens(ball, i, width, width + TAIL).astype(F32)
        gate = jnp.sum(jnp.where(gate_lane, packed, 0.0), axis=-1, keepdims=True)
        gp = dot(b, wg[...])
        up = dot(b, wu[...])
        du = dot_nt(tokens(cotall, i, 0, width), wd[...])
        sigma = 1.0 / (1.0 + jnp.exp(-gp))
        silu = gp * sigma
        u = (silu * up).astype(BF16).astype(F32)
        dgate = jnp.sum(du * u, axis=-1, keepdims=True)
        du = gate * du
        dgp = (du * up * sigma * (1.0 + gp * (1.0 - sigma))).astype(BF16)
        dup = (du * silu).astype(BF16)
        dgp_ref[rows_of(i)] = dgp
        dup_ref[rows_of(i)] = dup
        ug_ref[rows_of(i)] = (gate * u).astype(BF16)
        db = dot_nt(dgp, wg[...]) + dot_nt(dup, wu[...])
        dbs[(*place_of(i), slice(0, width))] = db.astype(BF16).reshape(2, 2, 2, quarter, width)
        dbs[(*place_of(i), slice(width, width + TAIL))] = (
            jnp.where(lane == expert, dgate, 0.0).astype(BF16).reshape(2, 2, 2, quarter, TAIL)
        )

    loop(0, steps, expert_block)
    x_dbs = PlaneScatter(plane, dbs, dbs_half, dbs_line, dbs_column, dbs_last, l_dbs, s_dbs)
    x_dbs.start()

    def down_block(i):
        y = dot(ug_ref[rows_of(i)], wd[...])
        ys[place_of(i)] = y.astype(BF16).reshape(2, 2, 2, quarter, width)

    loop(0, steps, down_block)
    x_dbs.send()
    x_ys = PlaneScatter(plane, ys, ys_half, ys_line, ys_column, ys_last, l_ys, s_ys)
    x_ys.start()

    tables = ((gg, gg_land, gg_relay, gg_out), (gu, gu_land, gu_relay, gu_out), (gd, gd_land, gd_relay, gd_out))

    def grad_place(i, dp, ten):
        return (f_rows(ten), d_rows(dp)) if i == 2 else (d_rows(dp), f_rows(ten))

    def relay_grad(i, side):
        table, _, relay, _ = tables[i]
        part = table.at[grad_place(i, side, lax.rem(r + 2, n_ten))]
        sems = s_grad.at[2 * i, n_ten + side], s_grad.at[2 * i + 1, n_ten + side]
        return remote(part, relay.at[side], *sems, tensor(sides_y[side]))

    def grad_copy(i, side):
        table, land = tables[i][:2]
        k = sides_y[side]
        ten = lax.rem(r + k, n_ten)
        part = table.at[f_rows(ten)] if i == 2 else table.at[:, f_rows(ten)]
        sems = s_grad.at[2 * i, k], s_grad.at[2 * i + 1, k]
        return remote(part, land.at[side], *sems, tensor(k))

    def start_relays(i):
        for side in range(2):
            relay_grad(i, side).start()

    def start_grads(i):
        table, _, relay, _ = tables[i]
        for side in range(2):
            relay_grad(i, side).wait_recv()
            place = grad_place(i, side, lax.rem(r + sides_y[side], n_ten))
            table[place] = (table[place].astype(F32) + relay[side].astype(F32)).astype(BF16)
            grad_copy(i, side).start()

    def half_sum(i, dp):
        table, land = tables[i][:2]
        total = table[grad_place(i, dp, r)].astype(F32)
        for side in range(2):
            part = land[side, :, d_rows(dp)] if i == 2 else land[side, d_rows(dp)]
            total = total + part.astype(F32)
        return total

    def half_copy(i):
        out = tables[i][3]
        sems = s_grad.at[2 * i, 0], s_grad.at[2 * i + 1, 0]
        return remote(out.at[0], out.at[1], *sems, partner_dp)

    def sum_grads(i, out):
        for side in range(2):
            grad_copy(i, side).wait_recv()
        tables[i][3][0] = half_sum(i, 1 - d).astype(BF16)
        half_copy(i).start()
        out[d] = half_sum(i, d)

    all_cot = cotall[...].reshape(nq * 2 * quarter, width)
    all_b = ball[:, :, :, :, :, 0:width].reshape(nq * 2 * quarter, width)
    gd[...] = dot_tn(ug_ref[...], all_cot).astype(BF16)
    start_relays(2)
    gg[...] = dot_tn(all_b, dgp_ref[...]).astype(BF16)
    start_relays(0)
    x_dbs.middle()
    gu[...] = dot_tn(all_b, dup_ref[...]).astype(BF16)
    start_relays(1)

    summed = x_dbs.total()
    dprobs = routed * summed[:, width : width + TAIL]
    dlogits = probs * (dprobs - jnp.sum(probs * dprobs, axis=-1, keepdims=True))
    dlogits = jnp.where(lane < 32, dlogits, 0.0).astype(BF16)
    db = summed[:, 0:width] + dot_nt(dlogits, tails)
    w_db = db * ffn_gain
    grad_hidden = (
        cotall[own].astype(F32)
        + inv_two * w_db
        - hidden * inv_two**3 * (jnp.sum(w_db * hidden, axis=-1, keepdims=True) / width)
    )
    ffn_gain_rows = (db * hidden * inv_two).astype(BF16)
    dall[r] = grad_hidden.astype(BF16)

    def spread(table, sems, k):
        mine = table.at[r]
        return remote(mine, mine, sems.at[0, k], sems.at[1, k], tensor(k))

    loop(1, n_ten, lambda k: spread(dall, s_dall, k).start())
    x_ys.send()
    start_grads(2)
    one_hot = lax.broadcasted_iota(jnp.int32, (rows, TAIL), 1)
    ones_ffn = jnp.where(one_hot[0:quarter] == 32, 1.0, 0.0).astype(BF16)
    ones_attn = jnp.where(one_hot == 33, 1.0, 0.0).astype(BF16)
    tail_grad = dot_tn(b_own, dlogits) + dot_tn(ffn_gain_rows, ones_ffn)
    loop(1, n_ten, lambda k: spread(dall, s_dall, k).wait_recv())

    d_attn = dall[...].reshape(rows, width)

    def to_rows(grad):
        return grad.astype(BF16).reshape(n_dp, nx, 2, 2, 32, grad.shape[1])

    wgo[...] = to_rows(dot_tn(d_attn, o_low))
    x_wgo = PlaneScatter(plane, wgo, wgo_half, wgo_line, wgo_column, wgo_last, l_wgo, s_wgo)
    x_wgo.start()
    do = dot(d_attn, w_out).astype(BF16)
    for t in range(2):
        tile = do[:, 128 * t : 128 * t + 128].astype(F32)
        for g in range(2):
            dos[2 * t + g] = jnp.where(group_of == g, tile, 0.0).astype(BF16)

    dq_ref[...] = jnp.zeros_like(dq_ref)
    x_wgo.send()
    start_grads(0)

    def head_backward(i):
        go = dos[i]
        delta = jnp.sum(go.astype(F32) * o_ref[i // 2], axis=-1, keepdims=True)
        dp = dot_nt(go, kv[:, :, :, 128:256].reshape(seq, 128))
        grad = (p_ref[i].astype(F32) * (dp - delta)).astype(BF16)
        ds_ref[i] = grad
        dq = dot(grad, kv[:, :, :, 0:128].reshape(seq, 128))
        dq_ref[i // 2] += jnp.where(group_of == lax.rem(i, 2), dq, 0.0)

    loop(0, 4, head_backward)
    all_q = qs[...].reshape(4 * rows, 128)
    all_do = dos[...].reshape(4 * rows, 128)
    for i in range(4):
        span = slice(i * (seq // 4), (i + 1) * (seq // 4))
        place = slice(i * (nj // 4), (i + 1) * (nj // 4))
        dk = dot_tn(ds_ref[:, :, span].reshape(4 * rows, seq // 4), all_q)
        dv = dot_tn(p_ref[:, :, span].reshape(4 * rows, seq // 4), all_do)
        dkv[place, :, :, 0:128] = dk.astype(BF16).reshape(nj // 4, 2, rows, 128)
        dkv[place, :, :, 128:256] = dv.astype(BF16).reshape(nj // 4, 2, rows, 128)
    x_dkv = Scatter(nj, j, core, along, sibling, dkv, dkv_half, dkv_land, s_dkv)
    x_dkv.start()

    a_low = a_ref[...]
    dq_lin = jnp.concatenate([unrope(dq_ref[0]), unrope(dq_ref[1])], axis=1) * 0.125
    dq_lin = dq_lin.astype(BF16)
    x_dkv.send()
    x_ys.middle()
    x_wgo.middle()
    wgq[...] = to_rows(dot_tn(a_low, dq_lin))
    x_wgq = PlaneScatter(plane, wgq, wgq_half, wgq_line, wgq_column, wgq_last, l_wgq, s_wgq)
    x_wgq.start()
    da = dot_nt(dq_lin, wall[:, :, :, :, :, 0:256].reshape(width, 256))
    x_wgq.send()
    sum_grads(2, od_ref)
    grad_kv = x_dkv.total()
    dkv_lin = jnp.concatenate([unrope(grad_kv[:, 0:128]), grad_kv[:, 128:256]], axis=1)
    dkv_lin = dkv_lin.astype(BF16)
    da = da + dot_nt(dkv_lin, wall[:, :, :, :, :, 256:512].reshape(width, 256))
    part[1] = da.astype(BF16).reshape(n_ten, quarter, width)
    loop(1, n_ten, lambda k: tensor_copy(1, s_y2, k).start())
    start_grads(1)
    wgk[:, :, :, :, :, 0:256] = to_rows(dot_tn(a_low, dkv_lin))
    attn_gain_rows = (da * x_ref[...].astype(F32) * inv).astype(BF16)
    wgk[:, :, :, :, :, 256:384] = to_rows(tail_grad + dot_tn(attn_gain_rows, ones_attn))
    x_wgk = PlaneScatter(plane, wgk, wgk_half, wgk_line, wgk_column, wgk_last, l_wgk, s_wgk)
    x_wgk.start()

    hall[r] = (hidden + x_ys.total()).astype(BF16)
    x_wgk.send()
    x_wgq.middle()
    sum_grads(0, og_ref)

    grad_a = part[1, r].astype(F32)
    for k in range(1, n_ten):
        tensor_copy(1, s_y2, k).wait_recv()
        grad_a = grad_a + ybuf[1, k].astype(F32)
    x_own = x_ref[wide].astype(F32)
    inv_own = lax.rsqrt(jnp.mean(x_own * x_own, axis=-1, keepdims=True) + EPS)
    w_da = grad_a * attn_gain
    grad_x = (
        grad_hidden
        + inv_own * w_da
        - x_own * inv_own**3 * (jnp.sum(w_da * x_own, axis=-1, keepdims=True) / width)
    )
    igall[r] = grad_x.astype(BF16)

    def spread_ig(k):
        mine = igall.at[r]
        return remote(mine, mine, s_fin.at[2, k], s_fin.at[3, k], tensor(k))

    loop(1, n_ten, lambda k: spread_ig(k).start())
    loop(1, n_ten, lambda k: spread(hall, s_fin, k).start())
    x_wgk.middle()

    sum_grads(1, ou_ref)

    stores = []

    def store(src, dst):
        stores.append(pltpu.make_async_copy(src, dst, s_out.at[len(stores)]))
        stores[-1].start()

    for i, out, dst in ((2, od_ref, o_wd), (0, og_ref, o_wg), (1, ou_ref, o_wu)):
        half_copy(i).wait_recv()
        out[1 - d] = tables[i][3][1].astype(F32)
        store(out, dst)

    loop(1, n_ten, lambda k: spread(hall, s_fin, k).wait_recv())
    store(hall, o_h)
    loop(1, n_ten, lambda k: spread_ig(k).wait_recv())
    ig_ref[...] = igall[...].astype(F32)
    store(ig_ref, o_ig)

    def store_pair(first, total, dst):
        for i, tile in enumerate(swap_heads(total)):
            w_ref[:, first + 128 * i : first + 128 * i + 128] = tile
        store(w_ref.at[:, first : first + 256], dst)

    store_pair(512, x_wgo.total(), o_o)
    store_pair(0, x_wgq.total(), o_q)
    grads = x_wgk.total()
    w_ref[:, 256:512] = grads[:, 0:256]
    store(w_ref.at[:, 256:384], o_k)
    store(w_ref.at[:, 384:512], o_v)
    tail_y[0] = grads[:, 256:384]

    def tail_copy(k):
        return remote(tail_y.at[0], tail_y.at[k], s_fin.at[4, k], s_fin.at[5, k], tensor(k))

    loop(1, n_ten, lambda k: tail_copy(k).start())
    tail_sum = grads[:, 256:384]
    for k in range(1, n_ten):
        tail_copy(k).wait_recv()
        tail_sum = tail_sum + tail_y[k]
    t_ref[...] = tail_sum
    store(t_ref, o_t)

    for copy in stores:
        copy.wait()
    for gather in (g_wall, g_wout, g_cot, g_kv, g_ball):
        gather.drain()
    for scatter in (x_dbs, x_ys, x_dkv, x_wgo, x_wgq, x_wgk):
        scatter.drain()

    def drain_tensor(k):
        tensor_copy(0, s_y1, k).wait_send()
        tensor_copy(1, s_y2, k).wait_send()
        spread(dall, s_dall, k).wait_send()
        spread(hall, s_fin, k).wait_send()
        spread_ig(k).wait_send()
        tail_copy(k).wait_send()

    loop(1, n_ten, drain_tensor)

    wait_send_all(across_copies())

    for side, k in enumerate(sides_y):
        wait_send_all(own_copies(k))
        wait_send_all(passed_copies(k))
        wait_send_all(relay_copies(d, 0, side))
        wait_send_all(relay_copies(1 - d, 6, side))
        wait_send_all([relay_grad(i, side) for i in range(3)])
        wait_send_all([grad_copy(i, side) for i in range(3)])
    for i in range(3):
        half_copy(i).wait_send()


def call_layer(sizes, xin, cot, seg, rts, gain_a, gain_f, wq, wk, wv, wo, wr, wgi, wui, wdi):
    n_dp, n_ctx, n_ten = sizes
    nj = n_ctx // 2
    nx = nj // 2
    nq = n_dp * nj
    rows, width = xin.shape
    seq = n_ctx * rows
    quarter = rows // n_ten
    half_d, cut = wgi.shape[1], wgi.shape[2]
    hidden_units = cut * n_ten
    all_rows = nq * 2 * quarter

    def shape(*dims, kind=F32):
        return jax.ShapeDtypeStruct(dims, kind)

    def low(*dims):
        return pltpu.VMEM(dims, BF16)

    def full(*dims):
        return pltpu.VMEM(dims, F32)

    def sems(*dims):
        return pltpu.SemaphoreType.DMA(dims)

    def table(chunk, columns):
        return low(n_dp, nx, 2, 2, chunk, columns)

    def summed(chunk, columns):
        return [
            table(chunk, columns),
            low(n_dp, nx, 2, chunk, columns),
            low(nx, nx, chunk // 2, columns),
            low(nx, n_dp, 2, chunk // 2, columns),
            low(nx, chunk, columns),
        ]

    scratch = [
        table(32, 640),
        table(32, 256),
        table(quarter, width),
        table(quarter, width + TAIL),
        low(nj, 2, rows, 256),
        low(width, hidden_units),
        low(width, hidden_units),
        low(hidden_units, width),
        low(rows, width),
        full(rows, 128),
        full(n_ten, quarter, width),
        full(32, 768),
        full(32, TAIL),
        full(2, half_d, cut),
        full(2, half_d, cut),
        full(2, cut, half_d),
        low(rows, width),
        low(4, rows, 128),
        low(4, rows, seq),
        low(4, rows, seq),
        full(2, rows, 128),
        low(2, n_ten, quarter, width),
        low(2, n_ten, quarter, width),
        low(n_ten, quarter, width),
        low(n_ten, quarter, width),
        low(n_ten, quarter, width),
        low(all_rows, hidden_units),
        low(all_rows, hidden_units),
        low(all_rows, hidden_units),
        *summed(quarter, width + TAIL),
        *summed(quarter, width),
        low(width, hidden_units),
        low(width, hidden_units),
        low(hidden_units, width),
        low(2, width, cut),
        low(2, width, cut),
        low(2, cut, width),
        low(2, half_d, cut),
        low(2, half_d, cut),
        low(2, cut, half_d),
        low(2, half_d, cut),
        low(2, half_d, cut),
        low(2, cut, half_d),
        low(4, rows, 128),
        full(2, rows, 128),
        low(nj, 2, rows, 256),
        low(nj, rows, 256),
        low(nj, rows, 256),
        *summed(32, 256),
        *summed(32, 256),
        *summed(32, 384),
        full(n_ten, 32, TAIL),
        sems(2, nx),
        sems(4),
        sems(2, nx),
        sems(4),
        sems(2, nx),
        sems(4),
        sems(2, nx),
        sems(4),
        sems(nj),
        sems(3),
        sems(12, n_ten + 2),
        sems(2, n_ten),
        sems(2, nx),
        sems(4),
        sems(2, nx),
        sems(4),
        sems(6, n_ten + 2),
        sems(2, n_ten),
        sems(4),
        sems(2, n_ten),
        sems(2, nx),
        sems(4),
        sems(2, nx),
        sems(4),
        sems(2, nx),
        sems(4),
        sems(6, n_ten),
        sems(5),
        sems(10),
    ]
    far, near = pl.BlockSpec(memory_space=pltpu.HBM), pl.BlockSpec(memory_space=pltpu.VMEM)
    flops = 2 * (9 * all_rows * width * hidden_units + 4 * rows * width * 768)
    return pl.pallas_call(
        functools.partial(layer, sizes),
        out_shape=(
            shape(n_ten, quarter, width, kind=BF16),
            shape(n_ten, quarter, width),
            shape(32, 256),
            shape(32, 128),
            shape(32, 128),
            shape(32, 256),
            shape(32, TAIL),
            shape(2, half_d, cut),
            shape(2, half_d, cut),
            shape(2, cut, half_d),
        ),
        in_specs=[far, far] + [near] * 9 + [far] * 3,
        out_specs=[far] * 10,
        scratch_shapes=scratch,
        compiler_params=pltpu.CompilerParams(
            collective_id=0, has_side_effects=True, vmem_limit_bytes=VMEM_BYTES
        ),
        cost_estimate=pl.CostEstimate(flops=flops, bytes_accessed=8 << 20, transcendentals=0),
    )(xin, cot, seg, rts, gain_a, gain_f, wq, wk, wv, wo, wr, wgi, wui, wdi)


def hand_over(*refs):
    sources, tail = refs[:9], refs[9]
    results, gain_a, gain_f, router, sems = refs[10:19], *refs[19:]
    copies = [
        pltpu.make_async_copy(src, dst, sems.at[i])
        for i, (src, dst) in enumerate(zip(sources, results))
    ]
    for copy in copies:
        copy.start()
    router[...] = tail[:, 0:32]
    up = lax.broadcasted_iota(jnp.int32, (32, 32), 0)
    same = up == lax.broadcasted_iota(jnp.int32, (32, 32), 1)
    gain_a[...] = jnp.sum(jnp.where(same, tail[:, 33:34], 0.0), axis=0, keepdims=True)
    gain_f[...] = jnp.sum(jnp.where(same, tail[:, 32:33], 0.0), axis=0, keepdims=True)
    for copy in copies:
        copy.wait()


def call_hand_over(arrays, tail):
    far, near = pl.BlockSpec(memory_space=pltpu.HBM), pl.BlockSpec(memory_space=pltpu.VMEM)
    small = [(1, 32), (1, 32), (32, 32)]
    return pl.pallas_call(
        hand_over,
        out_shape=[jax.ShapeDtypeStruct(a.shape, a.dtype) for a in arrays]
        + [jax.ShapeDtypeStruct(dims, F32) for dims in small],
        in_specs=[near] * (len(arrays) + 1),
        out_specs=[far] * len(arrays) + [near] * 3,
        scratch_shapes=[pltpu.SemaphoreType.DMA((len(arrays),))],
        compiler_params=pltpu.CompilerParams(vmem_limit_bytes=VMEM_BYTES),
    )(*arrays, tail)


def per_device(
    hidden_in,
    segments,
    routes,
    norm_attn,
    w_query,
    w_key,
    w_value,
    w_out,
    norm_ffn,
    w_router,
    w_gate,
    w_up,
    w_down,
    cotangent,
):
    sizes = (lax.axis_size("dp"), lax.axis_size("context"), lax.axis_size("tensor"))
    out, grad, wq, wk, wv, wo, tail, gate_grad, up_grad, down_grad = call_layer(
        sizes,
        hidden_in,
        cotangent,
        segments,
        routes[0].T,
        norm_attn,
        norm_ffn,
        w_query[0],
        w_key[0],
        w_value[0],
        w_out[0].T,
        w_router[0],
        w_gate[0],
        w_up[0],
        w_down[0],
    )
    arrays = (
        out.reshape(hidden_in.shape),
        grad.reshape(hidden_in.shape),
        wq,
        wk,
        wv,
        wo,
        gate_grad,
        up_grad,
        down_grad,
    )
    results = call_hand_over(arrays, tail)
    out, grad, wq, wk, wv, wo, gate_grad, up_grad, down_grad, gain_a, gain_f, router = results
    return (
        out,
        grad,
        gain_a,
        wq[None],
        wk[None],
        wv[None],
        wo.T[None],
        gain_f,
        router[None],
        gate_grad[None],
        up_grad[None],
        down_grad[None],
    )


def solution(mesh):
    in_specs = (
        P(("dp", "context"), None),
        P("dp", "context"),
        P(None, ("dp", "context"), None),
        P(None, ("dp", "context")),
        P(None, ("dp", "context"), "tensor"),
        P(None, ("dp", "context"), "tensor"),
        P(None, ("dp", "context"), "tensor"),
        P(None, "tensor", ("dp", "context")),
        P(None, ("dp", "context")),
        P(None, ("dp", "context"), None),
        P(None, "context", "dp", "tensor"),
        P(None, "context", "dp", "tensor"),
        P(None, "context", "tensor", "dp"),
        P(("dp", "context"), None),
    )
    out_specs = (
        P(("dp", "context"), None),
        P(("dp", "context"), None),
        P(None, ("dp", "context")),
        P(None, ("dp", "context"), "tensor"),
        P(None, ("dp", "context"), "tensor"),
        P(None, ("dp", "context"), "tensor"),
        P(None, "tensor", ("dp", "context")),
        P(None, ("dp", "context")),
        P(None, ("dp", "context"), None),
        P(None, "context", "dp", "tensor"),
        P(None, "context", "dp", "tensor"),
        P(None, "context", "tensor", "dp"),
    )
    return jax.shard_map(
        per_device, mesh=mesh, in_specs=in_specs, out_specs=out_specs, check_vma=False
    )
```

```python
import functools
import math

import jax
import jax.numpy as jnp
from jax import lax
from jax.experimental import pallas as pl
from jax.experimental.pallas import tpu as pltpu
from jax.sharding import PartitionSpec as P

HEAD = 64
EPS = 1e-06
NEG = -1e30
F32 = jnp.float32
BF16 = jnp.bfloat16
TAIL = 128
VMEM_BYTES = 60 * 1024 * 1024


def dot(a, b):
    return jnp.dot(a, b, preferred_element_type=F32)


def dot_nt(a, b):
    return lax.dot_general(a, b, (((1,), (1,)), ((), ())), preferred_element_type=F32)


def dot_tn(a, b):
    return lax.dot_general(a, b, (((0,), (0,)), ((), ())), preferred_element_type=F32)


def remote(src, dst, send_sem, recv_sem, device):
    return pltpu.make_async_remote_copy(
        src_ref=src,
        dst_ref=dst,
        send_sem=send_sem,
        recv_sem=recv_sem,
        device_id=device,
        device_id_type=pl.DeviceIdType.MESH,
    )


def loop(start, stop, step):
    def body(k, carry):
        step(k)
        return carry

    lax.fori_loop(start, stop, body, 0)


class Gather:
    def __init__(self, count, me, core, peer, sibling, table, landed, sems):
        self.count, self.me, self.core = count, me, core
        self.peer, self.sibling, self.table = peer, sibling, table
        self.landed, self.sems = landed, sems

    def far(self, k):
        mine = self.table.at[self.me, self.core]
        return remote(mine, mine, self.sems.at[0], self.landed.at[k], self.peer(k))

    def near(self, k):
        chunk = self.table.at[lax.rem(self.me + self.count - k, self.count), self.core]
        return remote(chunk, chunk, self.sems.at[1], self.sems.at[2], self.sibling)

    def start(self):
        loop(1, self.count, lambda k: self.far(k).start())
        self.near(0).start()

    def forward(self):
        def step(k):
            self.far(k).wait_recv()
            self.near(k).start()

        loop(1, self.count, step)

    def near_all(self, side):
        whole = self.table.at[:, side]
        return remote(whole, whole, self.sems.at[1], self.sems.at[2], self.sibling)

    def finish(self):
        self.near_all(1 - self.core).wait_recv()

    def drain(self):
        others = self.table.at[pl.ds(0, self.count - 1), self.core]
        remote(others, others, self.sems.at[0], self.landed.at[0], self.sibling).wait_send()
        self.near_all(self.core).wait_send()


class Scatter:
    def __init__(self, count, me, core, peer, sibling, parts, half, landed, sems):
        self.count, self.me, self.core = count, me, core
        self.peer, self.sibling = peer, sibling
        self.parts, self.half, self.landed, self.sems = parts, half, landed, sems

    def near(self):
        return remote(
            self.parts.at[:, 1 - self.core],
            self.half,
            self.sems.at[0],
            self.sems.at[1],
            self.sibling,
        )

    def far(self, k):
        there = lax.rem(self.me + k, self.count)
        return remote(
            self.half.at[there],
            self.landed.at[k],
            self.sems.at[2],
            self.sems.at[3],
            self.peer(k),
        )

    def far_all(self):
        return remote(
            self.half.at[pl.ds(1, self.count - 1)],
            self.landed.at[pl.ds(1, self.count - 1)],
            self.sems.at[2],
            self.sems.at[3],
            self.sibling,
        )

    def start(self):
        self.near().start()

    def send(self):
        self.near().wait_recv()

        def add(there):
            mine = self.parts[there, self.core].astype(F32)
            self.half[there] = (mine + self.half[there].astype(F32)).astype(BF16)

        def step(k):
            add(lax.rem(self.me + k, self.count))
            self.far(k).start()

        loop(1, self.count, step)
        add(self.me)

    def total(self):
        self.far_all().wait_recv()

        def step(k, acc):
            return acc + self.landed[k].astype(F32)

        return lax.fori_loop(1, self.count, step, self.half[self.me].astype(F32))

    def drain(self):
        self.near().wait_send()
        self.far_all().wait_send()


class Plane:
    def __init__(self, d, x, zh, nx, core, sibling, x_peer, z_peer):
        self.d, self.x, self.zh, self.nx = d, x, zh, nx
        self.core, self.sibling = core, sibling
        self.x_peer, self.z_peer = x_peer, z_peer

    def x_at(self, k):
        return lax.rem(self.x + k + self.nx, self.nx)

    def z_at(self, k):
        z = lax.rem(2 * self.d + self.zh + k + 4, 4)
        return z // 2, lax.rem(z, 2)


def upper(rows):
    return pl.ds(0, rows // 2)


def lower(rows):
    return pl.ds(rows // 2, rows // 2)


class PlaneGather:
    def __init__(self, plane, table, landed, sems):
        self.plane, self.table, self.landed, self.sems = plane, table, landed, sems
        rows = table.shape[4]
        self.up, self.down = upper(rows), lower(rows)

    def line(self, k):
        d, zh = self.plane.z_at(k)
        return self.table.at[d, :, zh, self.plane.core, self.up]

    def column(self, k):
        return self.table.at[:, self.plane.x_at(k), :, self.plane.core, self.down]

    def send(self, part, stage, k, device):
        remote(part, part, self.sems.at[stage], self.landed.at[stage, k], device).start()

    def landing(self, part, stage, k):
        return remote(
            part, part, self.sems.at[stage], self.landed.at[stage, k], self.plane.sibling
        )

    def pass_on(self, k):
        for part in (self.line(-k), self.column(-k)):
            remote(part, part, self.sems.at[2], self.sems.at[3], self.plane.sibling).start()

    def start(self):
        p = self.plane
        chunk = self.table.at[p.d, p.x, p.zh, p.core]

        def step(k):
            self.send(chunk.at[self.up], 0, k, p.x_peer(k))
            self.send(chunk.at[self.down], 0, k, p.z_peer(k))

        loop(1, p.nx, step)

    def forward(self):
        p = self.plane
        loop(1, p.nx, lambda k: self.landing(self.table.at[0, 0, 0, p.core], 0, k).wait_recv())

        def step(k):
            self.send(self.line(0), 1, k, p.z_peer(k))
            self.send(self.column(0), 1, k, p.x_peer(k))

        loop(1, p.nx, step)
        self.pass_on(0)

    def forward_rest(self):
        p = self.plane

        def arrive(k):
            self.landing(self.table.at[0, :, 0, p.core], 1, k).wait_recv()
            self.pass_on(k)

        loop(1, p.nx, arrive)

    def near_all(self, side):
        whole = self.table.at[:, :, :, side]
        return remote(whole, whole, self.sems.at[2], self.sems.at[3], self.plane.sibling)

    def finish(self):
        self.near_all(1 - self.plane.core).wait_recv()

    def drain(self):
        core, others = self.plane.core, pl.ds(0, self.plane.nx - 1)
        self.landing(self.table.at[0, others, 0, core], 0, 0).wait_send()
        self.landing(self.table.at[:, others, :, core], 1, 0).wait_send()
        self.near_all(core).wait_send()


class PlaneScatter:
    def __init__(self, plane, parts, half, line, column, last, landed, sems):
        self.plane, self.parts, self.half = plane, parts, half
        self.line, self.column, self.last = line, column, last
        self.landed, self.sems = landed, sems
        rows = parts.shape[4]
        self.up, self.down = upper(rows), lower(rows)

    def copy(self, src, dst, stage, k, device):
        return remote(src, dst, self.sems.at[stage], self.landed.at[stage, k], device)

    def near(self):
        p = self.plane
        away = self.parts.at[:, :, :, 1 - p.core]
        return remote(away, self.half, self.sems.at[2], self.sems.at[3], p.sibling)

    def start(self):
        self.near().start()

    def send(self):
        p = self.plane
        self.near().wait_recv()

        def add(i):
            spot = (i // (2 * p.nx), lax.rem(i // 2, p.nx), lax.rem(i, 2))
            mine = self.parts[(*spot, p.core)].astype(F32)
            self.half[spot] = (mine + self.half[spot].astype(F32)).astype(BF16)

        loop(0, 4 * p.nx, add)

        def step(k):
            d, zh = p.z_at(k)
            there = self.half.at[d, :, zh, self.up]
            self.copy(there, self.line.at[k], 0, k, p.z_peer(k)).start()
            there = self.half.at[:, p.x_at(k), :, self.down]
            self.copy(there, self.column.at[k], 0, k, p.x_peer(k)).start()

        loop(1, p.nx, step)

    def middle(self):
        p = self.plane

        def arrive(k):
            two = self.line.at[pl.ds(0, 2)]
            self.copy(two, two, 0, k, p.sibling).wait_recv()

        loop(1, p.nx, arrive)

        def add_line(k):
            spot = (p.d, p.x_at(k), p.zh, self.up)
            total = self.half[spot].astype(F32)
            for i in range(1, p.nx):
                total = total + self.line[i, p.x_at(k)].astype(F32)
            self.half[spot] = total.astype(BF16)

        def add_column(k):
            d, zh = p.z_at(k)
            spot = (d, p.x, zh, self.down)
            total = self.half[spot].astype(F32)
            for i in range(1, p.nx):
                total = total + self.column[i, d, zh].astype(F32)
            self.half[spot] = total.astype(BF16)

        def step(k):
            add_line(k)
            spot = self.half.at[p.d, p.x_at(k), p.zh, self.up]
            self.copy(spot, self.last.at[k, self.up], 1, k, p.x_peer(k)).start()
            add_column(k)
            d, zh = p.z_at(k)
            spot = self.half.at[d, p.x, zh, self.down]
            self.copy(spot, self.last.at[k, self.down], 1, k, p.z_peer(k)).start()

        loop(1, p.nx, step)
        add_line(0)
        add_column(0)

    def total(self):
        p = self.plane
        total = self.half[p.d, p.x, p.zh].astype(F32)
        for k in range(1, p.nx):
            self.copy(self.last.at[k], self.last.at[k], 1, k, p.sibling).wait_recv()
            total = total + self.last[k].astype(F32)
        return total

    def drain(self):
        p, others = self.plane, pl.ds(0, self.plane.nx - 1)
        self.near().wait_send()
        first = self.half.at[:, others]
        self.copy(first, first, 0, 0, p.sibling).wait_send()
        second = self.half.at[0, others, 0]
        self.copy(second, second, 1, 0, p.sibling).wait_send()


def layer(
    sizes,
    xin,
    cot,
    seg,
    rts,
    gain_a,
    gain_f,
    wq,
    wk,
    wv,
    wo,
    wr,
    wgi,
    wui,
    wdi,
    o_h,
    o_ig,
    o_q,
    o_k,
    o_v,
    o_o,
    o_t,
    o_wg,
    o_wu,
    o_wd,
    wall,
    wall_out,
    cotall,
    ball,
    kv,
    wg,
    wu,
    wd,
    x_ref,
    rt_ref,
    ig_ref,
    w_ref,
    t_ref,
    og_ref,
    ou_ref,
    od_ref,
    a_ref,
    qs,
    p_ref,
    ds_ref,
    o_ref,
    part,
    ybuf,
    hall,
    dall,
    igall,
    dgp_ref,
    dup_ref,
    ug_ref,
    dbs,
    dbs_half,
    dbs_line,
    dbs_column,
    dbs_last,
    ys,
    ys_half,
    ys_line,
    ys_column,
    ys_last,
    gg,
    gu,
    gd,
    gg_land,
    gu_land,
    gd_land,
    gg_relay,
    gu_relay,
    gd_relay,
    gg_out,
    gu_out,
    gd_out,
    dos,
    dq_ref,
    dkv,
    dkv_half,
    dkv_land,
    wgo,
    wgo_half,
    wgo_line,
    wgo_column,
    wgo_last,
    wgq,
    wgq_half,
    wgq_line,
    wgq_column,
    wgq_last,
    wgk,
    wgk_half,
    wgk_line,
    wgk_column,
    wgk_last,
    tail_y,
    l_wall,
    s_wall,
    l_wout,
    s_wout,
    l_cot,
    s_cot,
    l_ball,
    s_ball,
    l_kv,
    s_kv,
    s_exp,
    s_y1,
    l_dbs,
    s_dbs,
    l_ys,
    s_ys,
    s_grad,
    s_dall,
    s_dkv,
    s_y2,
    l_wgo,
    s_wgo,
    l_wgq,
    s_wgq,
    l_wgk,
    s_wgk,
    s_fin,
    s_in,
    s_out,
):
    n_dp, n_ctx, n_ten = sizes
    nj = n_ctx // 2
    nq = n_dp * nj
    rows, width = xin.shape
    seq = n_ctx * rows
    quarter = rows // n_ten
    d, c, r = lax.axis_index("dp"), lax.axis_index("context"), lax.axis_index("tensor")
    core, j = lax.rem(c, 2), c // 2

    def at(dp, context, tensor):
        return {"dp": dp, "context": context, "tensor": tensor}

    nx = nj // 2
    x_here, zh = j // 2, lax.rem(j, 2)

    def x_peer(k):
        return at(d, (lax.rem(x_here + k, nx) * 2 + zh) * 2 + core, r)

    def z_peer(k):
        z = lax.rem(2 * d + zh + k, 4)
        return at(z // 2, (x_here * 2 + lax.rem(z, 2)) * 2 + core, r)

    def along(k):
        return at(d, lax.rem(j + k, nj) * 2 + core, r)

    def tensor(k):
        return at(d, c, lax.rem(r + k, n_ten))

    partner_dp = at(1 - d, c, r)
    sibling = at(d, c + 1 - 2 * core, r)
    plane = Plane(d, x_here, zh, nx, core, sibling, x_peer, z_peer)
    own = (d, x_here, zh, core)

    wide = pl.ds(pl.multiple_of(r * quarter, quarter), quarter)
    half_d, cut = wgi.shape[1], wgi.shape[2]

    def d_rows(dp):
        return pl.ds(pl.multiple_of(dp * half_d, half_d), half_d)

    def f_rows(ten):
        return pl.ds(pl.multiple_of(ten * cut, cut), cut)

    here_g, here_u, here_d = (d_rows(d), f_rows(r)), (d_rows(d), f_rows(r)), (f_rows(r), d_rows(d))
    there_g, there_d = (d_rows(1 - d), f_rows(r)), (f_rows(r), d_rows(1 - d))

    barrier = pltpu.get_barrier_semaphore()

    def greet(device):
        pl.semaphore_signal(barrier, inc=1, device_id=device, device_id_type=pl.DeviceIdType.MESH)

    loop(1, nj, lambda k: greet(along(k)))
    loop(1, nx, lambda k: greet(z_peer(k)))
    greet(sibling)
    loop(1, n_ten, lambda k: greet(tensor(k)))

    loads = [
        pltpu.make_async_copy(src, dst, s_in.at[i])
        for i, (src, dst) in enumerate(
            (
                (xin, x_ref),
                (cot.at[wide], cotall.at[own]),
                (wgi.at[d], wg.at[here_g]),
                (wui.at[d], wu.at[here_u]),
                (wdi.at[d], wd.at[here_d]),
            )
        )
    ]
    for load in loads:
        load.start()

    lane = lax.broadcasted_iota(jnp.int32, (1, 128), 1)
    group_of = lane // HEAD

    def swap_heads(table):
        one, two = table[:, 0:128], table[:, 128:256]
        return (
            jnp.where(group_of == 0, one, pltpu.roll(two, HEAD, 1)),
            jnp.where(group_of == 0, pltpu.roll(one, HEAD, 1), two),
        )

    def diagonal(count, extent, first):
        up = lax.broadcasted_iota(jnp.int32, (count, extent), 0)
        return up + first == lax.broadcasted_iota(jnp.int32, (count, extent), 1)

    def as_column(row, count, first):
        picked = jnp.where(diagonal(count, row.shape[1], first), row, 0.0)
        return jnp.sum(picked, axis=1, keepdims=True)

    for i, tile in enumerate(swap_heads(wq[...].astype(F32))):
        wall[(*own, slice(None), slice(128 * i, 128 * i + 128))] = tile.astype(BF16)
    for i, tile in enumerate(swap_heads(wo[...].astype(F32))):
        wall_out[(*own, slice(None), slice(128 * i, 128 * i + 128))] = tile.astype(BF16)
    wall[(*own, slice(None), slice(256, 384))] = wk[...]
    wall[(*own, slice(None), slice(384, 512))] = wv[...]
    numbers_here = seg[...].astype(F32)
    tail = jnp.where(lane == 32, as_column(gain_a[...].astype(F32), 32, 0), 0.0)
    tail = jnp.where(lane == 33, as_column(gain_f[...].astype(F32), 32, 0), tail)
    for i in range(rows // 32):
        tail = jnp.where(lane == 34 + i, as_column(numbers_here, 32, 32 * i), tail)
    wall[(*own, slice(None), slice(512, 640))] = tail.astype(BF16)
    wall[(*own, slice(None), slice(512, 544))] = wr[...]

    pl.semaphore_wait(barrier, nj + nx + n_ten - 2)

    g_wall = PlaneGather(plane, wall, l_wall, s_wall)
    g_wall.start()
    g_wout = PlaneGather(plane, wall_out, l_wout, s_wout)

    def triple(sources, places, first_sem, k, device):
        return [
            remote(src, dst, s_exp.at[first_sem + 2 * i, k], s_exp.at[first_sem + 2 * i + 1, k], device)
            for i, (src, dst) in enumerate(zip(sources, places))
        ]

    landing = (wg.at[here_g], wu.at[here_u], wd.at[here_d])
    passed_on = (wg.at[there_g], wu.at[there_g], wd.at[there_d])
    sides_y = (1, n_ten - 1)

    def own_copies(k):
        return triple((wgi.at[d], wui.at[d], wdi.at[d]), landing, 0, k, tensor(k))

    def across_copies():
        return triple((wgi.at[1 - d], wui.at[1 - d], wdi.at[1 - d]), landing, 0, 0, partner_dp)

    def passed_copy(i, k):
        place = passed_on[i]
        return remote(place, place, s_exp.at[6 + 2 * i, k], s_exp.at[7 + 2 * i, k], tensor(k))

    def passed_copies(k):
        return [passed_copy(i, k) for i in range(3)]

    def relay_copies(dp, first_sem, side):
        ten = lax.rem(r + sides_y[1 - side], n_ten)
        step, narrow = half_d // 2, cut // 2
        d_half = pl.ds(pl.multiple_of(dp * half_d + side * step, step), step)
        f_half = pl.ds(pl.multiple_of(ten * cut + side * narrow, narrow), narrow)
        parts = (
            wg.at[d_half, f_rows(ten)],
            wu.at[d_half, f_rows(ten)],
            wd.at[f_half, d_rows(dp)],
        )
        return triple(parts, parts, first_sem, n_ten + side, tensor(sides_y[side]))

    def start_all(copies):
        for copy in copies:
            copy.start()

    def wait_recv_all(copies):
        for copy in copies:
            copy.wait_recv()

    def wait_send_all(copies):
        for copy in copies:
            copy.wait_send()

    for k in sides_y:
        start_all(own_copies(k))

    loads[0].wait()
    x = x_ref[...].astype(F32)
    inv = lax.rsqrt(jnp.mean(x * x, axis=-1, keepdims=True) + EPS)
    low_half = lax.rem(lane, HEAD) < HEAD // 2
    rate = jnp.exp(
        lax.rem(lane, HEAD // 2).astype(F32) * (-2.0 * math.log(10000.0) / HEAD)
    )
    row_index = c * rows + lax.broadcasted_iota(jnp.int32, (rows, 1), 0)
    angle = row_index.astype(F32) * rate
    cosine = jnp.cos(angle)
    sine = jnp.where(low_half, -1.0, 1.0) * jnp.sin(angle)

    def partner(z):
        return jnp.where(
            low_half, pltpu.roll(z, 128 - HEAD // 2, 1), pltpu.roll(z, HEAD // 2, 1)
        )

    def rope(z):
        return z * cosine + partner(z) * sine

    def unrope(z):
        return z * cosine - partner(z) * sine

    named = jnp.zeros((128, rows), F32)
    of_expert = lax.broadcasted_iota(jnp.int32, (128, rows), 0)
    for k in range(rts.shape[0]):
        named = named + jnp.where(rts[k : k + 1, :] == of_expert, 1.0, 0.0)
    rt_ref[...] = named.T
    for load in loads[1:]:
        load.wait()
    g_cot = PlaneGather(plane, cotall, l_cot, s_cot)

    g_wall.forward()
    start_all(across_copies())
    g_wall.forward_rest()
    g_wall.finish()

    tails = wall[:, :, :, :, :, 512:640].reshape(width, TAIL)
    gains = tails.astype(F32).T
    attn_gain, ffn_gain = gains[32:33], gains[33:34]
    a_ref[...] = (x * inv * attn_gain).astype(BF16)

    qkv = dot(a_ref[...], wall[:, :, :, :, :, 0:512].reshape(width, 512))
    for t in range(2):
        turned = rope(qkv[:, 128 * t : 128 * t + 128]) * 0.125
        for g in range(2):
            qs[2 * t + g] = jnp.where(group_of == g, turned, 0.0).astype(BF16)
    kv[j, core, :, 0:128] = rope(qkv[:, 256:384]).astype(BF16)
    kv[j, core, :, 128:256] = qkv[:, 384:512].astype(BF16)
    g_kv = Gather(nj, j, core, along, sibling, kv, l_kv, s_kv)
    g_kv.start()
    g_wout.start()
    for k in sides_y:
        wait_recv_all(own_copies(k))
    for side in range(2):
        start_all(relay_copies(d, 0, side))

    numbers = wall[d, :, :, :, :, 512:640].reshape(nj * 64, TAIL).astype(F32)
    held = jnp.where((lane >= 34) & (lane < 38), numbers, 1e9)
    mine = as_column(numbers_here, rows, 0)
    first = jnp.zeros((rows, 1), F32)
    for s in range(1, 4):
        below = jnp.sum(jnp.where(held < s - 0.5, 1.0, 0.0), axis=0, keepdims=True)
        below = jnp.sum(below, axis=1, keepdims=True)
        first = jnp.where(mine == s, below, first)
    first = first.astype(jnp.int32)
    columns = lax.broadcasted_iota(jnp.int32, (rows, seq), 1)
    allowed = (columns >= first) & (columns <= row_index)

    g_kv.forward()
    g_wout.forward()
    g_kv.finish()
    g_cot.start()
    wait_recv_all(across_copies())
    for k in sides_y:
        passed_copy(0, k).start()

    o_ref[...] = jnp.zeros_like(o_ref)

    def head_forward(i):
        scores = dot_nt(qs[i], kv[:, :, :, 0:128].reshape(seq, 128))
        scores = jnp.where(allowed, scores, NEG)
        top = jnp.max(scores, axis=-1, keepdims=True)
        expo = jnp.where(allowed, jnp.exp(scores - top), 0.0)
        weights = (expo * (1.0 / jnp.sum(expo, axis=-1, keepdims=True))).astype(BF16)
        p_ref[i] = weights
        out = dot(weights, kv[:, :, :, 128:256].reshape(seq, 128))
        o_ref[i // 2] += jnp.where(group_of == lax.rem(i, 2), out, 0.0)

    loop(0, 4, head_forward)
    g_wout.forward_rest()
    g_wout.finish()
    o_low = jnp.concatenate([o_ref[0], o_ref[1]], axis=1).astype(BF16)
    w_out = wall_out[...].reshape(width, 256)
    part[0] = dot_nt(o_low, w_out).astype(BF16).reshape(n_ten, quarter, width)

    def tensor_copy(which, sems, k):
        return remote(
            part.at[which, lax.rem(r + k, n_ten)],
            ybuf.at[which, k],
            sems.at[0, k],
            sems.at[1, k],
            tensor(k),
        )

    loop(1, n_ten, lambda k: tensor_copy(0, s_y1, k).start())
    g_cot.forward()
    hidden = x_ref[wide].astype(F32) + part[0, r].astype(F32)
    for k in range(1, n_ten):
        tensor_copy(0, s_y1, k).wait_recv()
        hidden = hidden + ybuf[0, k].astype(F32)

    inv_two = lax.rsqrt(jnp.mean(hidden * hidden, axis=-1, keepdims=True) + EPS)
    b_own = (hidden * inv_two * ffn_gain).astype(BF16)
    logits = jnp.where(lane < 32, dot(b_own, tails), NEG)
    expo = jnp.exp(logits - jnp.max(logits, axis=-1, keepdims=True))
    probs = expo / jnp.sum(expo, axis=-1, keepdims=True)
    routed = rt_ref[wide]
    gates = probs * routed
    gates_high = gates.astype(BF16).astype(F32)
    ball[(*own, slice(None), slice(0, width))] = b_own
    ball[(*own, slice(None), slice(width, width + TAIL))] = (
        gates_high + pltpu.roll(gates - gates_high, 32, 1)
    ).astype(BF16)
    g_ball = PlaneGather(plane, ball, l_ball, s_ball)
    g_ball.start()
    for k in sides_y:
        start_all([passed_copy(1, k), passed_copy(2, k)])
    g_ball.forward()
    g_cot.forward_rest()
    for k in sides_y:
        wait_recv_all(passed_copies(k))
    for side in range(2):
        start_all(relay_copies(1 - d, 6, side))
    g_ball.forward_rest()
    for side in range(2):
        wait_recv_all(relay_copies(d, 0, side))
        wait_recv_all(relay_copies(1 - d, 6, side))
    g_cot.finish()
    g_ball.finish()

    expert = 2 * c + d
    gate_lane = (lane == expert) | (lane == expert + 32)
    block = 8 * quarter
    steps = 4

    def place_of(i):
        whole = slice(None)
        return (i // 2, pl.ds(2 * lax.rem(i, 2), 2), whole, whole, whole)

    def tokens(ref, i, cut_at, cut_to):
        return ref[(*place_of(i), slice(cut_at, cut_to))].reshape(block, cut_to - cut_at)

    def rows_of(i):
        return pl.ds(pl.multiple_of(i * block, block), block)

    def expert_block(i):
        b = tokens(ball, i, 0, width)
        packed = tokens(ball, i, width, width + TAIL).astype(F32)
        gate = jnp.sum(jnp.where(gate_lane, packed, 0.0), axis=-1, keepdims=True)
        gp = dot(b, wg[...])
        up = dot(b, wu[...])
        du = dot_nt(tokens(cotall, i, 0, width), wd[...])
        sigma = 1.0 / (1.0 + jnp.exp(-gp))
        silu = gp * sigma
        u = (silu * up).astype(BF16).astype(F32)
        dgate = jnp.sum(du * u, axis=-1, keepdims=True)
        du = gate * du
        dgp = (du * up * sigma * (1.0 + gp * (1.0 - sigma))).astype(BF16)
        dup = (du * silu).astype(BF16)
        dgp_ref[rows_of(i)] = dgp
        dup_ref[rows_of(i)] = dup
        ug_ref[rows_of(i)] = (gate * u).astype(BF16)
        db = dot_nt(dgp, wg[...]) + dot_nt(dup, wu[...])
        dbs[(*place_of(i), slice(0, width))] = db.astype(BF16).reshape(2, 2, 2, quarter, width)
        dbs[(*place_of(i), slice(width, width + TAIL))] = (
            jnp.where(lane == expert, dgate, 0.0).astype(BF16).reshape(2, 2, 2, quarter, TAIL)
        )

    loop(0, steps, expert_block)
    x_dbs = PlaneScatter(plane, dbs, dbs_half, dbs_line, dbs_column, dbs_last, l_dbs, s_dbs)
    x_dbs.start()

    def down_block(i):
        y = dot(ug_ref[rows_of(i)], wd[...])
        ys[place_of(i)] = y.astype(BF16).reshape(2, 2, 2, quarter, width)

    loop(0, steps, down_block)
    x_dbs.send()
    x_ys = PlaneScatter(plane, ys, ys_half, ys_line, ys_column, ys_last, l_ys, s_ys)
    x_ys.start()

    tables = ((gg, gg_land, gg_relay, gg_out), (gu, gu_land, gu_relay, gu_out), (gd, gd_land, gd_relay, gd_out))

    def grad_place(i, dp, ten):
        return (f_rows(ten), d_rows(dp)) if i == 2 else (d_rows(dp), f_rows(ten))

    def relay_grad(i, side):
        table, _, relay, _ = tables[i]
        part = table.at[grad_place(i, side, lax.rem(r + 2, n_ten))]
        sems = s_grad.at[2 * i, n_ten + side], s_grad.at[2 * i + 1, n_ten + side]
        return remote(part, relay.at[side], *sems, tensor(sides_y[side]))

    def grad_copy(i, side):
        table, land = tables[i][:2]
        k = sides_y[side]
        ten = lax.rem(r + k, n_ten)
        part = table.at[f_rows(ten)] if i == 2 else table.at[:, f_rows(ten)]
        sems = s_grad.at[2 * i, k], s_grad.at[2 * i + 1, k]
        return remote(part, land.at[side], *sems, tensor(k))

    def start_relays(i):
        for side in range(2):
            relay_grad(i, side).start()

    def start_grads(i):
        table, _, relay, _ = tables[i]
        for side in range(2):
            relay_grad(i, side).wait_recv()
            place = grad_place(i, side, lax.rem(r + sides_y[side], n_ten))
            table[place] = (table[place].astype(F32) + relay[side].astype(F32)).astype(BF16)
            grad_copy(i, side).start()

    def half_sum(i, dp):
        table, land = tables[i][:2]
        total = table[grad_place(i, dp, r)].astype(F32)
        for side in range(2):
            part = land[side, :, d_rows(dp)] if i == 2 else land[side, d_rows(dp)]
            total = total + part.astype(F32)
        return total

    def half_copy(i):
        out = tables[i][3]
        sems = s_grad.at[2 * i, 0], s_grad.at[2 * i + 1, 0]
        return remote(out.at[0], out.at[1], *sems, partner_dp)

    def sum_grads(i, out):
        for side in range(2):
            grad_copy(i, side).wait_recv()
        tables[i][3][0] = half_sum(i, 1 - d).astype(BF16)
        half_copy(i).start()
        out[d] = half_sum(i, d)

    all_cot = cotall[...].reshape(nq * 2 * quarter, width)
    all_b = ball[:, :, :, :, :, 0:width].reshape(nq * 2 * quarter, width)
    gd[...] = dot_tn(ug_ref[...], all_cot).astype(BF16)
    start_relays(2)
    gg[...] = dot_tn(all_b, dgp_ref[...]).astype(BF16)
    start_relays(0)
    x_dbs.middle()
    gu[...] = dot_tn(all_b, dup_ref[...]).astype(BF16)
    start_relays(1)

    summed = x_dbs.total()
    dprobs = routed * summed[:, width : width + TAIL]
    dlogits = probs * (dprobs - jnp.sum(probs * dprobs, axis=-1, keepdims=True))
    dlogits = jnp.where(lane < 32, dlogits, 0.0).astype(BF16)
    db = summed[:, 0:width] + dot_nt(dlogits, tails)
    w_db = db * ffn_gain
    grad_hidden = (
        cotall[own].astype(F32)
        + inv_two * w_db
        - hidden * inv_two**3 * (jnp.sum(w_db * hidden, axis=-1, keepdims=True) / width)
    )
    ffn_gain_rows = (db * hidden * inv_two).astype(BF16)
    dall[r] = grad_hidden.astype(BF16)

    def spread(table, sems, k):
        mine = table.at[r]
        return remote(mine, mine, sems.at[0, k], sems.at[1, k], tensor(k))

    loop(1, n_ten, lambda k: spread(dall, s_dall, k).start())
    x_ys.send()
    start_grads(2)
    one_hot = lax.broadcasted_iota(jnp.int32, (rows, TAIL), 1)
    ones_ffn = jnp.where(one_hot[0:quarter] == 32, 1.0, 0.0).astype(BF16)
    ones_attn = jnp.where(one_hot == 33, 1.0, 0.0).astype(BF16)
    tail_grad = dot_tn(b_own, dlogits) + dot_tn(ffn_gain_rows, ones_ffn)
    loop(1, n_ten, lambda k: spread(dall, s_dall, k).wait_recv())

    d_attn = dall[...].reshape(rows, width)

    def to_rows(grad):
        return grad.astype(BF16).reshape(n_dp, nx, 2, 2, 32, grad.shape[1])

    do = dot(d_attn, w_out).astype(BF16)
    for t in range(2):
        tile = do[:, 128 * t : 128 * t + 128].astype(F32)
        for g in range(2):
            dos[2 * t + g] = jnp.where(group_of == g, tile, 0.0).astype(BF16)

    dq_ref[...] = jnp.zeros_like(dq_ref)
    start_grads(0)

    def head_backward(i):
        go = dos[i]
        delta = jnp.sum(go.astype(F32) * o_ref[i // 2], axis=-1, keepdims=True)
        dp = dot_nt(go, kv[:, :, :, 128:256].reshape(seq, 128))
        grad = (p_ref[i].astype(F32) * (dp - delta)).astype(BF16)
        ds_ref[i] = grad
        dq = dot(grad, kv[:, :, :, 0:128].reshape(seq, 128))
        dq_ref[i // 2] += jnp.where(group_of == lax.rem(i, 2), dq, 0.0)

    loop(0, 4, head_backward)
    all_q = qs[...].reshape(4 * rows, 128)
    all_do = dos[...].reshape(4 * rows, 128)
    for i in range(4):
        span = slice(i * (seq // 4), (i + 1) * (seq // 4))
        place = slice(i * (nj // 4), (i + 1) * (nj // 4))
        dk = dot_tn(ds_ref[:, :, span].reshape(4 * rows, seq // 4), all_q)
        dv = dot_tn(p_ref[:, :, span].reshape(4 * rows, seq // 4), all_do)
        dkv[place, :, :, 0:128] = dk.astype(BF16).reshape(nj // 4, 2, rows, 128)
        dkv[place, :, :, 128:256] = dv.astype(BF16).reshape(nj // 4, 2, rows, 128)
    x_dkv = Scatter(nj, j, core, along, sibling, dkv, dkv_half, dkv_land, s_dkv)
    x_dkv.start()

    a_low = a_ref[...]
    dq_lin = jnp.concatenate([unrope(dq_ref[0]), unrope(dq_ref[1])], axis=1) * 0.125
    dq_lin = dq_lin.astype(BF16)
    wgo[...] = to_rows(dot_tn(d_attn, o_low))
    x_wgo = PlaneScatter(plane, wgo, wgo_half, wgo_line, wgo_column, wgo_last, l_wgo, s_wgo)
    x_dkv.send()
    x_wgo.start()
    x_ys.middle()
    wgq[...] = to_rows(dot_tn(a_low, dq_lin))
    x_wgq = PlaneScatter(plane, wgq, wgq_half, wgq_line, wgq_column, wgq_last, l_wgq, s_wgq)
    x_wgq.start()
    x_wgo.send()
    da = dot_nt(dq_lin, wall[:, :, :, :, :, 0:256].reshape(width, 256))
    x_wgq.send()
    sum_grads(2, od_ref)
    x_wgo.middle()
    grad_kv = x_dkv.total()
    dkv_lin = jnp.concatenate([unrope(grad_kv[:, 0:128]), grad_kv[:, 128:256]], axis=1)
    dkv_lin = dkv_lin.astype(BF16)
    da = da + dot_nt(dkv_lin, wall[:, :, :, :, :, 256:512].reshape(width, 256))
    part[1] = da.astype(BF16).reshape(n_ten, quarter, width)
    loop(1, n_ten, lambda k: tensor_copy(1, s_y2, k).start())
    start_grads(1)
    wgk[:, :, :, :, :, 0:256] = to_rows(dot_tn(a_low, dkv_lin))
    attn_gain_rows = (da * x_ref[...].astype(F32) * inv).astype(BF16)
    wgk[:, :, :, :, :, 256:384] = to_rows(tail_grad + dot_tn(attn_gain_rows, ones_attn))
    x_wgk = PlaneScatter(plane, wgk, wgk_half, wgk_line, wgk_column, wgk_last, l_wgk, s_wgk)
    x_wgk.start()

    hall[r] = (hidden + x_ys.total()).astype(BF16)
    x_wgk.send()

    grad_a = part[1, r].astype(F32)
    for k in range(1, n_ten):
        tensor_copy(1, s_y2, k).wait_recv()
        grad_a = grad_a + ybuf[1, k].astype(F32)
    x_own = x_ref[wide].astype(F32)
    inv_own = lax.rsqrt(jnp.mean(x_own * x_own, axis=-1, keepdims=True) + EPS)
    w_da = grad_a * attn_gain
    grad_x = (
        grad_hidden
        + inv_own * w_da
        - x_own * inv_own**3 * (jnp.sum(w_da * x_own, axis=-1, keepdims=True) / width)
    )
    igall[r] = grad_x.astype(BF16)

    def spread_ig(k):
        mine = igall.at[r]
        return remote(mine, mine, s_fin.at[2, k], s_fin.at[3, k], tensor(k))

    loop(1, n_ten, lambda k: spread_ig(k).start())
    loop(1, n_ten, lambda k: spread(hall, s_fin, k).start())
    x_wgk.middle()
    x_wgq.middle()
    sum_grads(0, og_ref)

    sum_grads(1, ou_ref)

    stores = []

    def store(src, dst):
        stores.append(pltpu.make_async_copy(src, dst, s_out.at[len(stores)]))
        stores[-1].start()

    for i, out, dst in ((2, od_ref, o_wd), (0, og_ref, o_wg), (1, ou_ref, o_wu)):
        half_copy(i).wait_recv()
        out[1 - d] = tables[i][3][1].astype(F32)
        store(out, dst)

    loop(1, n_ten, lambda k: spread(hall, s_fin, k).wait_recv())
    store(hall, o_h)
    loop(1, n_ten, lambda k: spread_ig(k).wait_recv())
    ig_ref[...] = igall[...].astype(F32)
    store(ig_ref, o_ig)

    def store_pair(first, total, dst):
        for i, tile in enumerate(swap_heads(total)):
            w_ref[:, first + 128 * i : first + 128 * i + 128] = tile
        store(w_ref.at[:, first : first + 256], dst)

    store_pair(512, x_wgo.total(), o_o)
    store_pair(0, x_wgq.total(), o_q)
    grads = x_wgk.total()
    w_ref[:, 256:512] = grads[:, 0:256]
    store(w_ref.at[:, 256:384], o_k)
    store(w_ref.at[:, 384:512], o_v)
    tail_y[0] = grads[:, 256:384]

    def tail_copy(k):
        return remote(tail_y.at[0], tail_y.at[k], s_fin.at[4, k], s_fin.at[5, k], tensor(k))

    loop(1, n_ten, lambda k: tail_copy(k).start())
    tail_sum = grads[:, 256:384]
    for k in range(1, n_ten):
        tail_copy(k).wait_recv()
        tail_sum = tail_sum + tail_y[k]
    t_ref[...] = tail_sum
    store(t_ref, o_t)

    for copy in stores:
        copy.wait()
    for gather in (g_wall, g_wout, g_cot, g_kv, g_ball):
        gather.drain()
    for scatter in (x_dbs, x_ys, x_dkv, x_wgo, x_wgq, x_wgk):
        scatter.drain()

    def drain_tensor(k):
        tensor_copy(0, s_y1, k).wait_send()
        tensor_copy(1, s_y2, k).wait_send()
        spread(dall, s_dall, k).wait_send()
        spread(hall, s_fin, k).wait_send()
        spread_ig(k).wait_send()
        tail_copy(k).wait_send()

    loop(1, n_ten, drain_tensor)

    wait_send_all(across_copies())

    for side, k in enumerate(sides_y):
        wait_send_all(own_copies(k))
        wait_send_all(passed_copies(k))
        wait_send_all(relay_copies(d, 0, side))
        wait_send_all(relay_copies(1 - d, 6, side))
        wait_send_all([relay_grad(i, side) for i in range(3)])
        wait_send_all([grad_copy(i, side) for i in range(3)])
    for i in range(3):
        half_copy(i).wait_send()


def call_layer(sizes, xin, cot, seg, rts, gain_a, gain_f, wq, wk, wv, wo, wr, wgi, wui, wdi):
    n_dp, n_ctx, n_ten = sizes
    nj = n_ctx // 2
    nx = nj // 2
    nq = n_dp * nj
    rows, width = xin.shape
    seq = n_ctx * rows
    quarter = rows // n_ten
    half_d, cut = wgi.shape[1], wgi.shape[2]
    hidden_units = cut * n_ten
    all_rows = nq * 2 * quarter

    def shape(*dims, kind=F32):
        return jax.ShapeDtypeStruct(dims, kind)

    def low(*dims):
        return pltpu.VMEM(dims, BF16)

    def full(*dims):
        return pltpu.VMEM(dims, F32)

    def sems(*dims):
        return pltpu.SemaphoreType.DMA(dims)

    def table(chunk, columns):
        return low(n_dp, nx, 2, 2, chunk, columns)

    def summed(chunk, columns):
        return [
            table(chunk, columns),
            low(n_dp, nx, 2, chunk, columns),
            low(nx, nx, chunk // 2, columns),
            low(nx, n_dp, 2, chunk // 2, columns),
            low(nx, chunk, columns),
        ]

    scratch = [
        table(32, 640),
        table(32, 256),
        table(quarter, width),
        table(quarter, width + TAIL),
        low(nj, 2, rows, 256),
        low(width, hidden_units),
        low(width, hidden_units),
        low(hidden_units, width),
        low(rows, width),
        full(rows, 128),
        full(n_ten, quarter, width),
        full(32, 768),
        full(32, TAIL),
        full(2, half_d, cut),
        full(2, half_d, cut),
        full(2, cut, half_d),
        low(rows, width),
        low(4, rows, 128),
        low(4, rows, seq),
        low(4, rows, seq),
        full(2, rows, 128),
        low(2, n_ten, quarter, width),
        low(2, n_ten, quarter, width),
        low(n_ten, quarter, width),
        low(n_ten, quarter, width),
        low(n_ten, quarter, width),
        low(all_rows, hidden_units),
        low(all_rows, hidden_units),
        low(all_rows, hidden_units),
        *summed(quarter, width + TAIL),
        *summed(quarter, width),
        low(width, hidden_units),
        low(width, hidden_units),
        low(hidden_units, width),
        low(2, width, cut),
        low(2, width, cut),
        low(2, cut, width),
        low(2, half_d, cut),
        low(2, half_d, cut),
        low(2, cut, half_d),
        low(2, half_d, cut),
        low(2, half_d, cut),
        low(2, cut, half_d),
        low(4, rows, 128),
        full(2, rows, 128),
        low(nj, 2, rows, 256),
        low(nj, rows, 256),
        low(nj, rows, 256),
        *summed(32, 256),
        *summed(32, 256),
        *summed(32, 384),
        full(n_ten, 32, TAIL),
        sems(2, nx),
        sems(4),
        sems(2, nx),
        sems(4),
        sems(2, nx),
        sems(4),
        sems(2, nx),
        sems(4),
        sems(nj),
        sems(3),
        sems(12, n_ten + 2),
        sems(2, n_ten),
        sems(2, nx),
        sems(4),
        sems(2, nx),
        sems(4),
        sems(6, n_ten + 2),
        sems(2, n_ten),
        sems(4),
        sems(2, n_ten),
        sems(2, nx),
        sems(4),
        sems(2, nx),
        sems(4),
        sems(2, nx),
        sems(4),
        sems(6, n_ten),
        sems(5),
        sems(10),
    ]
    far, near = pl.BlockSpec(memory_space=pltpu.HBM), pl.BlockSpec(memory_space=pltpu.VMEM)
    flops = 2 * (9 * all_rows * width * hidden_units + 4 * rows * width * 768)
    return pl.pallas_call(
        functools.partial(layer, sizes),
        out_shape=(
            shape(n_ten, quarter, width, kind=BF16),
            shape(n_ten, quarter, width),
            shape(32, 256),
            shape(32, 128),
            shape(32, 128),
            shape(32, 256),
            shape(32, TAIL),
            shape(2, half_d, cut),
            shape(2, half_d, cut),
            shape(2, cut, half_d),
        ),
        in_specs=[far, far] + [near] * 9 + [far] * 3,
        out_specs=[far] * 10,
        scratch_shapes=scratch,
        compiler_params=pltpu.CompilerParams(
            collective_id=0, has_side_effects=True, vmem_limit_bytes=VMEM_BYTES
        ),
        cost_estimate=pl.CostEstimate(flops=flops, bytes_accessed=8 << 20, transcendentals=0),
    )(xin, cot, seg, rts, gain_a, gain_f, wq, wk, wv, wo, wr, wgi, wui, wdi)


def hand_over(*refs):
    sources, tail = refs[:9], refs[9]
    results, gain_a, gain_f, router, sems = refs[10:19], *refs[19:]
    copies = [
        pltpu.make_async_copy(src, dst, sems.at[i])
        for i, (src, dst) in enumerate(zip(sources, results))
    ]
    for copy in copies:
        copy.start()
    router[...] = tail[:, 0:32]
    up = lax.broadcasted_iota(jnp.int32, (32, 32), 0)
    same = up == lax.broadcasted_iota(jnp.int32, (32, 32), 1)
    gain_a[...] = jnp.sum(jnp.where(same, tail[:, 33:34], 0.0), axis=0, keepdims=True)
    gain_f[...] = jnp.sum(jnp.where(same, tail[:, 32:33], 0.0), axis=0, keepdims=True)
    for copy in copies:
        copy.wait()


def call_hand_over(arrays, tail):
    far, near = pl.BlockSpec(memory_space=pltpu.HBM), pl.BlockSpec(memory_space=pltpu.VMEM)
    small = [(1, 32), (1, 32), (32, 32)]
    return pl.pallas_call(
        hand_over,
        out_shape=[jax.ShapeDtypeStruct(a.shape, a.dtype) for a in arrays]
        + [jax.ShapeDtypeStruct(dims, F32) for dims in small],
        in_specs=[near] * (len(arrays) + 1),
        out_specs=[far] * len(arrays) + [near] * 3,
        scratch_shapes=[pltpu.SemaphoreType.DMA((len(arrays),))],
        compiler_params=pltpu.CompilerParams(vmem_limit_bytes=VMEM_BYTES),
    )(*arrays, tail)


def per_device(
    hidden_in,
    segments,
    routes,
    norm_attn,
    w_query,
    w_key,
    w_value,
    w_out,
    norm_ffn,
    w_router,
    w_gate,
    w_up,
    w_down,
    cotangent,
):
    sizes = (lax.axis_size("dp"), lax.axis_size("context"), lax.axis_size("tensor"))
    out, grad, wq, wk, wv, wo, tail, gate_grad, up_grad, down_grad = call_layer(
        sizes,
        hidden_in,
        cotangent,
        segments,
        routes[0].T,
        norm_attn,
        norm_ffn,
        w_query[0],
        w_key[0],
        w_value[0],
        w_out[0].T,
        w_router[0],
        w_gate[0],
        w_up[0],
        w_down[0],
    )
    arrays = (
        out.reshape(hidden_in.shape),
        grad.reshape(hidden_in.shape),
        wq,
        wk,
        wv,
        wo,
        gate_grad,
        up_grad,
        down_grad,
    )
    results = call_hand_over(arrays, tail)
    out, grad, wq, wk, wv, wo, gate_grad, up_grad, down_grad, gain_a, gain_f, router = results
    return (
        out,
        grad,
        gain_a,
        wq[None],
        wk[None],
        wv[None],
        wo.T[None],
        gain_f,
        router[None],
        gate_grad[None],
        up_grad[None],
        down_grad[None],
    )


def solution(mesh):
    in_specs = (
        P(("dp", "context"), None),
        P("dp", "context"),
        P(None, ("dp", "context"), None),
        P(None, ("dp", "context")),
        P(None, ("dp", "context"), "tensor"),
        P(None, ("dp", "context"), "tensor"),
        P(None, ("dp", "context"), "tensor"),
        P(None, "tensor", ("dp", "context")),
        P(None, ("dp", "context")),
        P(None, ("dp", "context"), None),
        P(None, "context", "dp", "tensor"),
        P(None, "context", "dp", "tensor"),
        P(None, "context", "tensor", "dp"),
        P(("dp", "context"), None),
    )
    out_specs = (
        P(("dp", "context"), None),
        P(("dp", "context"), None),
        P(None, ("dp", "context")),
        P(None, ("dp", "context"), "tensor"),
        P(None, ("dp", "context"), "tensor"),
        P(None, ("dp", "context"), "tensor"),
        P(None, "tensor", ("dp", "context")),
        P(None, ("dp", "context")),
        P(None, ("dp", "context"), None),
        P(None, "context", "dp", "tensor"),
        P(None, "context", "dp", "tensor"),
        P(None, "context", "tensor", "dp"),
    )
    return jax.shard_map(
        per_device, mesh=mesh, in_specs=in_specs, out_specs=out_specs, check_vma=False
    )
```

```python
import functools
import math

import jax
import jax.numpy as jnp
from jax import lax
from jax.experimental import pallas as pl
from jax.experimental.pallas import tpu as pltpu
from jax.sharding import PartitionSpec as P

HEAD = 64
EPS = 1e-06
NEG = -1e30
F32 = jnp.float32
BF16 = jnp.bfloat16
TAIL = 128
VMEM_BYTES = 60 * 1024 * 1024


def dot(a, b):
    return jnp.dot(a, b, preferred_element_type=F32)


def dot_nt(a, b):
    return lax.dot_general(a, b, (((1,), (1,)), ((), ())), preferred_element_type=F32)


def dot_tn(a, b):
    return lax.dot_general(a, b, (((0,), (0,)), ((), ())), preferred_element_type=F32)


def remote(src, dst, send_sem, recv_sem, device):
    return pltpu.make_async_remote_copy(
        src_ref=src,
        dst_ref=dst,
        send_sem=send_sem,
        recv_sem=recv_sem,
        device_id=device,
        device_id_type=pl.DeviceIdType.MESH,
    )


def loop(start, stop, step):
    def body(k, carry):
        step(k)
        return carry

    lax.fori_loop(start, stop, body, 0)


class Gather:
    def __init__(self, count, me, core, peer, sibling, table, landed, sems):
        self.count, self.me, self.core = count, me, core
        self.peer, self.sibling, self.table = peer, sibling, table
        self.landed, self.sems = landed, sems

    def far(self, k):
        mine = self.table.at[self.me, self.core]
        return remote(mine, mine, self.sems.at[0], self.landed.at[k], self.peer(k))

    def near(self, k):
        chunk = self.table.at[lax.rem(self.me + self.count - k, self.count), self.core]
        return remote(chunk, chunk, self.sems.at[1], self.sems.at[2], self.sibling)

    def start(self):
        loop(1, self.count, lambda k: self.far(k).start())
        self.near(0).start()

    def forward(self):
        def step(k):
            self.far(k).wait_recv()
            self.near(k).start()

        loop(1, self.count, step)

    def near_all(self, side):
        whole = self.table.at[:, side]
        return remote(whole, whole, self.sems.at[1], self.sems.at[2], self.sibling)

    def finish(self):
        self.near_all(1 - self.core).wait_recv()

    def drain(self):
        others = self.table.at[pl.ds(0, self.count - 1), self.core]
        remote(others, others, self.sems.at[0], self.landed.at[0], self.sibling).wait_send()
        self.near_all(self.core).wait_send()


class Scatter:
    def __init__(self, count, me, core, peer, sibling, parts, half, landed, sems):
        self.count, self.me, self.core = count, me, core
        self.peer, self.sibling = peer, sibling
        self.parts, self.half, self.landed, self.sems = parts, half, landed, sems

    def near(self):
        return remote(
            self.parts.at[:, 1 - self.core],
            self.half,
            self.sems.at[0],
            self.sems.at[1],
            self.sibling,
        )

    def far(self, k):
        there = lax.rem(self.me + k, self.count)
        return remote(
            self.half.at[there],
            self.landed.at[k],
            self.sems.at[2],
            self.sems.at[3],
            self.peer(k),
        )

    def far_all(self):
        return remote(
            self.half.at[pl.ds(1, self.count - 1)],
            self.landed.at[pl.ds(1, self.count - 1)],
            self.sems.at[2],
            self.sems.at[3],
            self.sibling,
        )

    def start_part(self, place):
        away, half = self.parts.at[place, 1 - self.core], self.half.at[place]
        remote(away, half, self.sems.at[0], self.sems.at[1], self.sibling).start()

    def start(self):
        self.near().start()

    def send(self):
        self.near().wait_recv()

        def add(there):
            mine = self.parts[there, self.core].astype(F32)
            self.half[there] = (mine + self.half[there].astype(F32)).astype(BF16)

        def step(k):
            add(lax.rem(self.me + k, self.count))
            self.far(k).start()

        loop(1, self.count, step)
        add(self.me)

    def total(self):
        self.far_all().wait_recv()

        def step(k, acc):
            return acc + self.landed[k].astype(F32)

        return lax.fori_loop(1, self.count, step, self.half[self.me].astype(F32))

    def drain(self):
        self.near().wait_send()
        self.far_all().wait_send()


class Plane:
    def __init__(self, d, x, zh, nx, core, sibling, x_peer, z_peer):
        self.d, self.x, self.zh, self.nx = d, x, zh, nx
        self.core, self.sibling = core, sibling
        self.x_peer, self.z_peer = x_peer, z_peer

    def x_at(self, k):
        return lax.rem(self.x + k + self.nx, self.nx)

    def z_at(self, k):
        z = lax.rem(2 * self.d + self.zh + k + 4, 4)
        return z // 2, lax.rem(z, 2)


def upper(rows):
    return pl.ds(0, rows // 2)


def lower(rows):
    return pl.ds(rows // 2, rows // 2)


class PlaneGather:
    def __init__(self, plane, table, landed, sems):
        self.plane, self.table, self.landed, self.sems = plane, table, landed, sems
        rows = table.shape[4]
        self.up, self.down = upper(rows), lower(rows)

    def line(self, k):
        d, zh = self.plane.z_at(k)
        return self.table.at[d, :, zh, self.plane.core, self.up]

    def column(self, k):
        return self.table.at[:, self.plane.x_at(k), :, self.plane.core, self.down]

    def send(self, part, stage, k, device):
        remote(part, part, self.sems.at[stage], self.landed.at[stage, k], device).start()

    def landing(self, part, stage, k):
        return remote(
            part, part, self.sems.at[stage], self.landed.at[stage, k], self.plane.sibling
        )

    def pass_on(self, k):
        for part in (self.line(-k), self.column(-k)):
            remote(part, part, self.sems.at[2], self.sems.at[3], self.plane.sibling).start()

    def start(self):
        p = self.plane
        chunk = self.table.at[p.d, p.x, p.zh, p.core]

        def step(k):
            self.send(chunk.at[self.up], 0, k, p.x_peer(k))
            self.send(chunk.at[self.down], 0, k, p.z_peer(k))

        loop(1, p.nx, step)

    def forward(self):
        p = self.plane
        loop(1, p.nx, lambda k: self.landing(self.table.at[0, 0, 0, p.core], 0, k).wait_recv())

        def step(k):
            self.send(self.line(0), 1, k, p.z_peer(k))
            self.send(self.column(0), 1, k, p.x_peer(k))

        loop(1, p.nx, step)
        self.pass_on(0)

    def forward_rest(self):
        p = self.plane

        def arrive(k):
            self.landing(self.table.at[0, :, 0, p.core], 1, k).wait_recv()
            self.pass_on(k)

        loop(1, p.nx, arrive)

    def near_all(self, side):
        whole = self.table.at[:, :, :, side]
        return remote(whole, whole, self.sems.at[2], self.sems.at[3], self.plane.sibling)

    def finish(self):
        self.near_all(1 - self.plane.core).wait_recv()

    def drain(self):
        core, others = self.plane.core, pl.ds(0, self.plane.nx - 1)
        self.landing(self.table.at[0, others, 0, core], 0, 0).wait_send()
        self.landing(self.table.at[:, others, :, core], 1, 0).wait_send()
        self.near_all(core).wait_send()


class PlaneScatter:
    def __init__(self, plane, parts, half, line, column, last, landed, sems):
        self.plane, self.parts, self.half = plane, parts, half
        self.line, self.column, self.last = line, column, last
        self.landed, self.sems = landed, sems
        rows = parts.shape[4]
        self.up, self.down = upper(rows), lower(rows)

    def copy(self, src, dst, stage, k, device):
        return remote(src, dst, self.sems.at[stage], self.landed.at[stage, k], device)

    def near(self):
        p = self.plane
        away = self.parts.at[:, :, :, 1 - p.core]
        return remote(away, self.half, self.sems.at[2], self.sems.at[3], p.sibling)

    def start_part(self, d, xs):
        p = self.plane
        away, half = self.parts.at[d, xs, :, 1 - p.core], self.half.at[d, xs]
        remote(away, half, self.sems.at[2], self.sems.at[3], p.sibling).start()

    def start(self):
        self.near().start()

    def send(self):
        p = self.plane
        self.near().wait_recv()

        def add(i):
            spot = (i // (2 * p.nx), lax.rem(i // 2, p.nx), lax.rem(i, 2))
            mine = self.parts[(*spot, p.core)].astype(F32)
            self.half[spot] = (mine + self.half[spot].astype(F32)).astype(BF16)

        loop(0, 4 * p.nx, add)

        def step(k):
            d, zh = p.z_at(k)
            there = self.half.at[d, :, zh, self.up]
            self.copy(there, self.line.at[k], 0, k, p.z_peer(k)).start()
            there = self.half.at[:, p.x_at(k), :, self.down]
            self.copy(there, self.column.at[k], 0, k, p.x_peer(k)).start()

        loop(1, p.nx, step)

    def middle(self):
        p = self.plane

        def arrive(k):
            two = self.line.at[pl.ds(0, 2)]
            self.copy(two, two, 0, k, p.sibling).wait_recv()

        loop(1, p.nx, arrive)

        def add_line(k):
            spot = (p.d, p.x_at(k), p.zh, self.up)
            total = self.half[spot].astype(F32)
            for i in range(1, p.nx):
                total = total + self.line[i, p.x_at(k)].astype(F32)
            self.half[spot] = total.astype(BF16)

        def add_column(k):
            d, zh = p.z_at(k)
            spot = (d, p.x, zh, self.down)
            total = self.half[spot].astype(F32)
            for i in range(1, p.nx):
                total = total + self.column[i, d, zh].astype(F32)
            self.half[spot] = total.astype(BF16)

        def step(k):
            add_line(k)
            spot = self.half.at[p.d, p.x_at(k), p.zh, self.up]
            self.copy(spot, self.last.at[k, self.up], 1, k, p.x_peer(k)).start()
            add_column(k)
            d, zh = p.z_at(k)
            spot = self.half.at[d, p.x, zh, self.down]
            self.copy(spot, self.last.at[k, self.down], 1, k, p.z_peer(k)).start()

        loop(1, p.nx, step)
        add_line(0)
        add_column(0)

    def total(self):
        p = self.plane
        total = self.half[p.d, p.x, p.zh].astype(F32)
        for k in range(1, p.nx):
            self.copy(self.last.at[k], self.last.at[k], 1, k, p.sibling).wait_recv()
            total = total + self.last[k].astype(F32)
        return total

    def drain(self):
        p, others = self.plane, pl.ds(0, self.plane.nx - 1)
        self.near().wait_send()
        first = self.half.at[:, others]
        self.copy(first, first, 0, 0, p.sibling).wait_send()
        second = self.half.at[0, others, 0]
        self.copy(second, second, 1, 0, p.sibling).wait_send()


def layer(
    sizes,
    xin,
    cot,
    seg,
    rts,
    gain_a,
    gain_f,
    wq,
    wk,
    wv,
    wo,
    wr,
    wgi,
    wui,
    wdi,
    o_h,
    o_ig,
    o_q,
    o_k,
    o_v,
    o_o,
    o_t,
    o_wg,
    o_wu,
    o_wd,
    wall,
    wall_out,
    cotall,
    ball,
    kv,
    wg,
    wu,
    wd,
    x_ref,
    rt_ref,
    ig_ref,
    w_ref,
    t_ref,
    og_ref,
    ou_ref,
    od_ref,
    a_ref,
    qs,
    p_ref,
    ds_ref,
    o_ref,
    part,
    ybuf,
    hall,
    dall,
    igall,
    dgp_ref,
    dup_ref,
    ug_ref,
    dbs,
    dbs_half,
    dbs_line,
    dbs_column,
    dbs_last,
    ys,
    ys_half,
    ys_line,
    ys_column,
    ys_last,
    gg,
    gu,
    gd,
    gg_land,
    gu_land,
    gd_land,
    gg_relay,
    gu_relay,
    gd_relay,
    gg_out,
    gu_out,
    gd_out,
    dos,
    dq_ref,
    dkv,
    dkv_half,
    dkv_land,
    wgo,
    wgo_half,
    wgo_line,
    wgo_column,
    wgo_last,
    wgq,
    wgq_half,
    wgq_line,
    wgq_column,
    wgq_last,
    wgk,
    wgk_half,
    wgk_line,
    wgk_column,
    wgk_last,
    tail_y,
    l_wall,
    s_wall,
    l_wout,
    s_wout,
    l_cot,
    s_cot,
    l_ball,
    s_ball,
    l_kv,
    s_kv,
    s_exp,
    s_y1,
    l_dbs,
    s_dbs,
    l_ys,
    s_ys,
    s_grad,
    s_dall,
    s_dkv,
    s_y2,
    l_wgo,
    s_wgo,
    l_wgq,
    s_wgq,
    l_wgk,
    s_wgk,
    s_fin,
    s_in,
    s_out,
):
    n_dp, n_ctx, n_ten = sizes
    nj = n_ctx // 2
    nq = n_dp * nj
    rows, width = xin.shape
    seq = n_ctx * rows
    quarter = rows // n_ten
    d, c, r = lax.axis_index("dp"), lax.axis_index("context"), lax.axis_index("tensor")
    core, j = lax.rem(c, 2), c // 2

    def at(dp, context, tensor):
        return {"dp": dp, "context": context, "tensor": tensor}

    nx = nj // 2
    x_here, zh = j // 2, lax.rem(j, 2)

    def x_peer(k):
        return at(d, (lax.rem(x_here + k, nx) * 2 + zh) * 2 + core, r)

    def z_peer(k):
        z = lax.rem(2 * d + zh + k, 4)
        return at(z // 2, (x_here * 2 + lax.rem(z, 2)) * 2 + core, r)

    def along(k):
        return at(d, lax.rem(j + k, nj) * 2 + core, r)

    def tensor(k):
        return at(d, c, lax.rem(r + k, n_ten))

    partner_dp = at(1 - d, c, r)
    sibling = at(d, c + 1 - 2 * core, r)
    plane = Plane(d, x_here, zh, nx, core, sibling, x_peer, z_peer)
    own = (d, x_here, zh, core)

    wide = pl.ds(pl.multiple_of(r * quarter, quarter), quarter)
    half_d, cut = wgi.shape[1], wgi.shape[2]

    def d_rows(dp):
        return pl.ds(pl.multiple_of(dp * half_d, half_d), half_d)

    def f_rows(ten):
        return pl.ds(pl.multiple_of(ten * cut, cut), cut)

    here_g, here_u, here_d = (d_rows(d), f_rows(r)), (d_rows(d), f_rows(r)), (f_rows(r), d_rows(d))
    there_g, there_d = (d_rows(1 - d), f_rows(r)), (f_rows(r), d_rows(1 - d))

    barrier = pltpu.get_barrier_semaphore()

    def greet(device):
        pl.semaphore_signal(barrier, inc=1, device_id=device, device_id_type=pl.DeviceIdType.MESH)

    loop(1, nj, lambda k: greet(along(k)))
    loop(1, nx, lambda k: greet(z_peer(k)))
    greet(sibling)
    loop(1, n_ten, lambda k: greet(tensor(k)))

    loads = [
        pltpu.make_async_copy(src, dst, s_in.at[i])
        for i, (src, dst) in enumerate(
            (
                (xin, x_ref),
                (cot.at[wide], cotall.at[own]),
                (wgi.at[d], wg.at[here_g]),
                (wui.at[d], wu.at[here_u]),
                (wdi.at[d], wd.at[here_d]),
            )
        )
    ]
    for load in loads:
        load.start()

    lane = lax.broadcasted_iota(jnp.int32, (1, 128), 1)
    group_of = lane // HEAD

    def swap_heads(table):
        one, two = table[:, 0:128], table[:, 128:256]
        return (
            jnp.where(group_of == 0, one, pltpu.roll(two, HEAD, 1)),
            jnp.where(group_of == 0, pltpu.roll(one, HEAD, 1), two),
        )

    def diagonal(count, extent, first):
        up = lax.broadcasted_iota(jnp.int32, (count, extent), 0)
        return up + first == lax.broadcasted_iota(jnp.int32, (count, extent), 1)

    def as_column(row, count, first):
        picked = jnp.where(diagonal(count, row.shape[1], first), row, 0.0)
        return jnp.sum(picked, axis=1, keepdims=True)

    for i, tile in enumerate(swap_heads(wq[...].astype(F32))):
        wall[(*own, slice(None), slice(128 * i, 128 * i + 128))] = tile.astype(BF16)
    for i, tile in enumerate(swap_heads(wo[...].astype(F32))):
        wall_out[(*own, slice(None), slice(128 * i, 128 * i + 128))] = tile.astype(BF16)
    wall[(*own, slice(None), slice(256, 384))] = wk[...]
    wall[(*own, slice(None), slice(384, 512))] = wv[...]
    numbers_here = seg[...].astype(F32)
    tail = jnp.where(lane == 32, as_column(gain_a[...].astype(F32), 32, 0), 0.0)
    tail = jnp.where(lane == 33, as_column(gain_f[...].astype(F32), 32, 0), tail)
    for i in range(rows // 32):
        tail = jnp.where(lane == 34 + i, as_column(numbers_here, 32, 32 * i), tail)
    wall[(*own, slice(None), slice(512, 640))] = tail.astype(BF16)
    wall[(*own, slice(None), slice(512, 544))] = wr[...]

    pl.semaphore_wait(barrier, nj + nx + n_ten - 2)

    g_wall = PlaneGather(plane, wall, l_wall, s_wall)
    g_wall.start()
    g_wout = PlaneGather(plane, wall_out, l_wout, s_wout)

    def triple(sources, places, first_sem, k, device):
        return [
            remote(src, dst, s_exp.at[first_sem + 2 * i, k], s_exp.at[first_sem + 2 * i + 1, k], device)
            for i, (src, dst) in enumerate(zip(sources, places))
        ]

    landing = (wg.at[here_g], wu.at[here_u], wd.at[here_d])
    passed_on = (wg.at[there_g], wu.at[there_g], wd.at[there_d])
    sides_y = (1, n_ten - 1)

    def own_copies(k):
        return triple((wgi.at[d], wui.at[d], wdi.at[d]), landing, 0, k, tensor(k))

    def across_copies():
        return triple((wgi.at[1 - d], wui.at[1 - d], wdi.at[1 - d]), landing, 0, 0, partner_dp)

    def passed_copy(i, k):
        place = passed_on[i]
        return remote(place, place, s_exp.at[6 + 2 * i, k], s_exp.at[7 + 2 * i, k], tensor(k))

    def passed_copies(k):
        return [passed_copy(i, k) for i in range(3)]

    def relay_copies(dp, first_sem, side):
        ten = lax.rem(r + sides_y[1 - side], n_ten)
        step, narrow = half_d // 2, cut // 2
        d_half = pl.ds(pl.multiple_of(dp * half_d + side * step, step), step)
        f_half = pl.ds(pl.multiple_of(ten * cut + side * narrow, narrow), narrow)
        parts = (
            wg.at[d_half, f_rows(ten)],
            wu.at[d_half, f_rows(ten)],
            wd.at[f_half, d_rows(dp)],
        )
        return triple(parts, parts, first_sem, n_ten + side, tensor(sides_y[side]))

    def start_all(copies):
        for copy in copies:
            copy.start()

    def wait_recv_all(copies):
        for copy in copies:
            copy.wait_recv()

    def wait_send_all(copies):
        for copy in copies:
            copy.wait_send()

    for k in sides_y:
        start_all(own_copies(k))

    loads[0].wait()
    x = x_ref[...].astype(F32)
    inv = lax.rsqrt(jnp.mean(x * x, axis=-1, keepdims=True) + EPS)
    low_half = lax.rem(lane, HEAD) < HEAD // 2
    rate = jnp.exp(
        lax.rem(lane, HEAD // 2).astype(F32) * (-2.0 * math.log(10000.0) / HEAD)
    )
    row_index = c * rows + lax.broadcasted_iota(jnp.int32, (rows, 1), 0)
    angle = row_index.astype(F32) * rate
    cosine = jnp.cos(angle)
    sine = jnp.where(low_half, -1.0, 1.0) * jnp.sin(angle)

    def partner(z):
        return jnp.where(
            low_half, pltpu.roll(z, 128 - HEAD // 2, 1), pltpu.roll(z, HEAD // 2, 1)
        )

    def rope(z):
        return z * cosine + partner(z) * sine

    def unrope(z):
        return z * cosine - partner(z) * sine

    named = jnp.zeros((128, rows), F32)
    of_expert = lax.broadcasted_iota(jnp.int32, (128, rows), 0)
    for k in range(rts.shape[0]):
        named = named + jnp.where(rts[k : k + 1, :] == of_expert, 1.0, 0.0)
    rt_ref[...] = named.T
    for load in loads[1:]:
        load.wait()
    g_cot = PlaneGather(plane, cotall, l_cot, s_cot)

    g_wall.forward()
    start_all(across_copies())
    g_wall.forward_rest()
    g_wall.finish()

    tails = wall[:, :, :, :, :, 512:640].reshape(width, TAIL)
    gains = tails.astype(F32).T
    attn_gain, ffn_gain = gains[32:33], gains[33:34]
    a_ref[...] = (x * inv * attn_gain).astype(BF16)

    qkv = dot(a_ref[...], wall[:, :, :, :, :, 0:512].reshape(width, 512))
    for t in range(2):
        turned = rope(qkv[:, 128 * t : 128 * t + 128]) * 0.125
        for g in range(2):
            qs[2 * t + g] = jnp.where(group_of == g, turned, 0.0).astype(BF16)
    kv[j, core, :, 0:128] = rope(qkv[:, 256:384]).astype(BF16)
    kv[j, core, :, 128:256] = qkv[:, 384:512].astype(BF16)
    g_kv = Gather(nj, j, core, along, sibling, kv, l_kv, s_kv)
    g_kv.start()
    g_wout.start()
    for k in sides_y:
        wait_recv_all(own_copies(k))
    for side in range(2):
        start_all(relay_copies(d, 0, side))

    numbers = wall[d, :, :, :, :, 512:640].reshape(nj * 64, TAIL).astype(F32)
    held = jnp.where((lane >= 34) & (lane < 38), numbers, 1e9)
    mine = as_column(numbers_here, rows, 0)
    first = jnp.zeros((rows, 1), F32)
    for s in range(1, 4):
        below = jnp.sum(jnp.where(held < s - 0.5, 1.0, 0.0), axis=0, keepdims=True)
        below = jnp.sum(below, axis=1, keepdims=True)
        first = jnp.where(mine == s, below, first)
    first = first.astype(jnp.int32)
    columns = lax.broadcasted_iota(jnp.int32, (rows, seq), 1)
    allowed = (columns >= first) & (columns <= row_index)

    g_kv.forward()
    g_wout.forward()
    g_kv.finish()
    g_cot.start()
    wait_recv_all(across_copies())
    for k in sides_y:
        passed_copy(0, k).start()

    o_ref[...] = jnp.zeros_like(o_ref)

    def head_forward(i):
        scores = dot_nt(qs[i], kv[:, :, :, 0:128].reshape(seq, 128))
        scores = jnp.where(allowed, scores, NEG)
        top = jnp.max(scores, axis=-1, keepdims=True)
        expo = jnp.where(allowed, jnp.exp(scores - top), 0.0)
        weights = (expo * (1.0 / jnp.sum(expo, axis=-1, keepdims=True))).astype(BF16)
        p_ref[i] = weights
        out = dot(weights, kv[:, :, :, 128:256].reshape(seq, 128))
        o_ref[i // 2] += jnp.where(group_of == lax.rem(i, 2), out, 0.0)

    loop(0, 4, head_forward)
    g_wout.forward_rest()
    g_wout.finish()
    o_low = jnp.concatenate([o_ref[0], o_ref[1]], axis=1).astype(BF16)
    w_out = wall_out[...].reshape(width, 256)
    part[0] = dot_nt(o_low, w_out).astype(BF16).reshape(n_ten, quarter, width)

    def tensor_copy(which, sems, k):
        return remote(
            part.at[which, lax.rem(r + k, n_ten)],
            ybuf.at[which, k],
            sems.at[0, k],
            sems.at[1, k],
            tensor(k),
        )

    loop(1, n_ten, lambda k: tensor_copy(0, s_y1, k).start())
    g_cot.forward()
    hidden = x_ref[wide].astype(F32) + part[0, r].astype(F32)
    for k in range(1, n_ten):
        tensor_copy(0, s_y1, k).wait_recv()
        hidden = hidden + ybuf[0, k].astype(F32)

    inv_two = lax.rsqrt(jnp.mean(hidden * hidden, axis=-1, keepdims=True) + EPS)
    b_own = (hidden * inv_two * ffn_gain).astype(BF16)
    logits = jnp.where(lane < 32, dot(b_own, tails), NEG)
    expo = jnp.exp(logits - jnp.max(logits, axis=-1, keepdims=True))
    probs = expo / jnp.sum(expo, axis=-1, keepdims=True)
    routed = rt_ref[wide]
    gates = probs * routed
    gates_high = gates.astype(BF16).astype(F32)
    ball[(*own, slice(None), slice(0, width))] = b_own
    ball[(*own, slice(None), slice(width, width + TAIL))] = (
        gates_high + pltpu.roll(gates - gates_high, 32, 1)
    ).astype(BF16)
    g_ball = PlaneGather(plane, ball, l_ball, s_ball)
    g_ball.start()
    for k in sides_y:
        start_all([passed_copy(1, k), passed_copy(2, k)])
    g_ball.forward()
    g_cot.forward_rest()
    for k in sides_y:
        wait_recv_all(passed_copies(k))
    for side in range(2):
        start_all(relay_copies(1 - d, 6, side))
    g_ball.forward_rest()
    for side in range(2):
        wait_recv_all(relay_copies(d, 0, side))
        wait_recv_all(relay_copies(1 - d, 6, side))
    g_cot.finish()
    g_ball.finish()

    expert = 2 * c + d
    gate_lane = (lane == expert) | (lane == expert + 32)
    block = 8 * quarter
    steps = 4

    def place_of(i):
        whole = slice(None)
        return (i // 2, pl.ds(2 * lax.rem(i, 2), 2), whole, whole, whole)

    def tokens(ref, i, cut_at, cut_to):
        return ref[(*place_of(i), slice(cut_at, cut_to))].reshape(block, cut_to - cut_at)

    def rows_of(i):
        return pl.ds(pl.multiple_of(i * block, block), block)

    x_dbs = PlaneScatter(plane, dbs, dbs_half, dbs_line, dbs_column, dbs_last, l_dbs, s_dbs)

    def expert_block(i):
        b = tokens(ball, i, 0, width)
        packed = tokens(ball, i, width, width + TAIL).astype(F32)
        gate = jnp.sum(jnp.where(gate_lane, packed, 0.0), axis=-1, keepdims=True)
        gp = dot(b, wg[...])
        up = dot(b, wu[...])
        du = dot_nt(tokens(cotall, i, 0, width), wd[...])
        sigma = 1.0 / (1.0 + jnp.exp(-gp))
        silu = gp * sigma
        u = (silu * up).astype(BF16).astype(F32)
        dgate = jnp.sum(du * u, axis=-1, keepdims=True)
        du = gate * du
        dgp = (du * up * sigma * (1.0 + gp * (1.0 - sigma))).astype(BF16)
        dup = (du * silu).astype(BF16)
        dgp_ref[rows_of(i)] = dgp
        dup_ref[rows_of(i)] = dup
        ug_ref[rows_of(i)] = (gate * u).astype(BF16)
        db = dot_nt(dgp, wg[...]) + dot_nt(dup, wu[...])
        dbs[(*place_of(i), slice(0, width))] = db.astype(BF16).reshape(2, 2, 2, quarter, width)
        dbs[(*place_of(i), slice(width, width + TAIL))] = (
            jnp.where(lane == expert, dgate, 0.0).astype(BF16).reshape(2, 2, 2, quarter, TAIL)
        )
        x_dbs.start_part(*place_of(i)[:2])

    loop(0, steps, expert_block)

    x_dbs.send()

    tables = ((gg, gg_land, gg_relay, gg_out), (gu, gu_land, gu_relay, gu_out), (gd, gd_land, gd_relay, gd_out))

    def grad_place(i, dp, ten):
        return (f_rows(ten), d_rows(dp)) if i == 2 else (d_rows(dp), f_rows(ten))

    def relay_grad(i, side):
        table, _, relay, _ = tables[i]
        part = table.at[grad_place(i, side, lax.rem(r + 2, n_ten))]
        sems = s_grad.at[2 * i, n_ten + side], s_grad.at[2 * i + 1, n_ten + side]
        return remote(part, relay.at[side], *sems, tensor(sides_y[side]))

    def grad_copy(i, side):
        table, land = tables[i][:2]
        k = sides_y[side]
        ten = lax.rem(r + k, n_ten)
        part = table.at[f_rows(ten)] if i == 2 else table.at[:, f_rows(ten)]
        sems = s_grad.at[2 * i, k], s_grad.at[2 * i + 1, k]
        return remote(part, land.at[side], *sems, tensor(k))

    def start_relays(i):
        for side in range(2):
            relay_grad(i, side).start()

    def start_grads(i):
        table, _, relay, _ = tables[i]
        for side in range(2):
            relay_grad(i, side).wait_recv()
            place = grad_place(i, side, lax.rem(r + sides_y[side], n_ten))
            table[place] = (table[place].astype(F32) + relay[side].astype(F32)).astype(BF16)
            grad_copy(i, side).start()

    def half_sum(i, dp):
        table, land = tables[i][:2]
        total = table[grad_place(i, dp, r)].astype(F32)
        for side in range(2):
            part = land[side, :, d_rows(dp)] if i == 2 else land[side, d_rows(dp)]
            total = total + part.astype(F32)
        return total

    def half_copy(i):
        out = tables[i][3]
        sems = s_grad.at[2 * i, 0], s_grad.at[2 * i + 1, 0]
        return remote(out.at[0], out.at[1], *sems, partner_dp)

    def sum_grads(i, out):
        for side in range(2):
            grad_copy(i, side).wait_recv()
        tables[i][3][0] = half_sum(i, 1 - d).astype(BF16)
        half_copy(i).start()
        out[d] = half_sum(i, d)

    all_cot = cotall[...].reshape(nq * 2 * quarter, width)
    all_b = ball[:, :, :, :, :, 0:width].reshape(nq * 2 * quarter, width)
    gd[...] = dot_tn(ug_ref[...], all_cot).astype(BF16)
    start_relays(2)

    def down_block(i):
        y = dot(ug_ref[rows_of(i)], wd[...])
        ys[place_of(i)] = y.astype(BF16).reshape(2, 2, 2, quarter, width)

    loop(0, steps, down_block)
    x_ys = PlaneScatter(plane, ys, ys_half, ys_line, ys_column, ys_last, l_ys, s_ys)
    x_ys.start()
    gg[...] = dot_tn(all_b, dgp_ref[...]).astype(BF16)
    start_relays(0)
    x_dbs.middle()
    gu[...] = dot_tn(all_b, dup_ref[...]).astype(BF16)
    start_relays(1)

    summed = x_dbs.total()
    dprobs = routed * summed[:, width : width + TAIL]
    dlogits = probs * (dprobs - jnp.sum(probs * dprobs, axis=-1, keepdims=True))
    dlogits = jnp.where(lane < 32, dlogits, 0.0).astype(BF16)
    db = summed[:, 0:width] + dot_nt(dlogits, tails)
    w_db = db * ffn_gain
    grad_hidden = (
        cotall[own].astype(F32)
        + inv_two * w_db
        - hidden * inv_two**3 * (jnp.sum(w_db * hidden, axis=-1, keepdims=True) / width)
    )
    ffn_gain_rows = (db * hidden * inv_two).astype(BF16)
    dall[r] = grad_hidden.astype(BF16)

    def spread(table, sems, k):
        mine = table.at[r]
        return remote(mine, mine, sems.at[0, k], sems.at[1, k], tensor(k))

    loop(1, n_ten, lambda k: spread(dall, s_dall, k).start())
    x_ys.send()
    start_grads(2)
    one_hot = lax.broadcasted_iota(jnp.int32, (rows, TAIL), 1)
    ones_ffn = jnp.where(one_hot[0:quarter] == 32, 1.0, 0.0).astype(BF16)
    ones_attn = jnp.where(one_hot == 33, 1.0, 0.0).astype(BF16)
    tail_grad = dot_tn(b_own, dlogits) + dot_tn(ffn_gain_rows, ones_ffn)
    loop(1, n_ten, lambda k: spread(dall, s_dall, k).wait_recv())

    d_attn = dall[...].reshape(rows, width)

    def to_rows(grad):
        return grad.astype(BF16).reshape(n_dp, nx, 2, 2, 32, grad.shape[1])

    do = dot(d_attn, w_out).astype(BF16)
    for t in range(2):
        tile = do[:, 128 * t : 128 * t + 128].astype(F32)
        for g in range(2):
            dos[2 * t + g] = jnp.where(group_of == g, tile, 0.0).astype(BF16)

    dq_ref[...] = jnp.zeros_like(dq_ref)
    start_grads(0)

    def head_backward(i):
        go = dos[i]
        delta = jnp.sum(go.astype(F32) * o_ref[i // 2], axis=-1, keepdims=True)
        dp = dot_nt(go, kv[:, :, :, 128:256].reshape(seq, 128))
        grad = (p_ref[i].astype(F32) * (dp - delta)).astype(BF16)
        ds_ref[i] = grad
        dq = dot(grad, kv[:, :, :, 0:128].reshape(seq, 128))
        dq_ref[i // 2] += jnp.where(group_of == lax.rem(i, 2), dq, 0.0)

    loop(0, 4, head_backward)
    x_dkv = Scatter(nj, j, core, along, sibling, dkv, dkv_half, dkv_land, s_dkv)
    all_q = qs[...].reshape(4 * rows, 128)
    all_do = dos[...].reshape(4 * rows, 128)
    for i in range(4):
        span = slice(i * (seq // 4), (i + 1) * (seq // 4))
        place = slice(i * (nj // 4), (i + 1) * (nj // 4))
        dk = dot_tn(ds_ref[:, :, span].reshape(4 * rows, seq // 4), all_q)
        dv = dot_tn(p_ref[:, :, span].reshape(4 * rows, seq // 4), all_do)
        dkv[place, :, :, 0:128] = dk.astype(BF16).reshape(nj // 4, 2, rows, 128)
        dkv[place, :, :, 128:256] = dv.astype(BF16).reshape(nj // 4, 2, rows, 128)
        x_dkv.start_part(place)

    a_low = a_ref[...]
    dq_lin = jnp.concatenate([unrope(dq_ref[0]), unrope(dq_ref[1])], axis=1) * 0.125
    dq_lin = dq_lin.astype(BF16)
    wgo[...] = to_rows(dot_tn(d_attn, o_low))
    x_wgo = PlaneScatter(plane, wgo, wgo_half, wgo_line, wgo_column, wgo_last, l_wgo, s_wgo)
    x_dkv.send()
    x_wgo.start()
    start_grads(1)
    x_ys.middle()
    wgq[...] = to_rows(dot_tn(a_low, dq_lin))
    x_wgq = PlaneScatter(plane, wgq, wgq_half, wgq_line, wgq_column, wgq_last, l_wgq, s_wgq)
    x_wgq.start()
    x_wgo.send()
    da = dot_nt(dq_lin, wall[:, :, :, :, :, 0:256].reshape(width, 256))
    x_wgq.send()
    sum_grads(2, od_ref)
    sum_grads(0, og_ref)
    x_wgo.middle()
    grad_kv = x_dkv.total()
    dkv_lin = jnp.concatenate([unrope(grad_kv[:, 0:128]), grad_kv[:, 128:256]], axis=1)
    dkv_lin = dkv_lin.astype(BF16)
    da = da + dot_nt(dkv_lin, wall[:, :, :, :, :, 256:512].reshape(width, 256))
    part[1] = da.astype(BF16).reshape(n_ten, quarter, width)
    loop(1, n_ten, lambda k: tensor_copy(1, s_y2, k).start())
    wgk[:, :, :, :, :, 0:256] = to_rows(dot_tn(a_low, dkv_lin))
    attn_gain_rows = (da * x_ref[...].astype(F32) * inv).astype(BF16)
    wgk[:, :, :, :, :, 256:384] = to_rows(tail_grad + dot_tn(attn_gain_rows, ones_attn))
    x_wgk = PlaneScatter(plane, wgk, wgk_half, wgk_line, wgk_column, wgk_last, l_wgk, s_wgk)
    x_wgk.start()

    hall[r] = (hidden + x_ys.total()).astype(BF16)
    x_wgk.send()

    grad_a = part[1, r].astype(F32)
    for k in range(1, n_ten):
        tensor_copy(1, s_y2, k).wait_recv()
        grad_a = grad_a + ybuf[1, k].astype(F32)
    x_own = x_ref[wide].astype(F32)
    inv_own = lax.rsqrt(jnp.mean(x_own * x_own, axis=-1, keepdims=True) + EPS)
    w_da = grad_a * attn_gain
    grad_x = (
        grad_hidden
        + inv_own * w_da
        - x_own * inv_own**3 * (jnp.sum(w_da * x_own, axis=-1, keepdims=True) / width)
    )
    igall[r] = grad_x.astype(BF16)

    def spread_ig(k):
        mine = igall.at[r]
        return remote(mine, mine, s_fin.at[2, k], s_fin.at[3, k], tensor(k))

    loop(1, n_ten, lambda k: spread_ig(k).start())
    loop(1, n_ten, lambda k: spread(hall, s_fin, k).start())
    sum_grads(1, ou_ref)
    x_wgk.middle()
    x_wgq.middle()

    stores = []

    def store(src, dst):
        stores.append(pltpu.make_async_copy(src, dst, s_out.at[len(stores)]))
        stores[-1].start()

    for i, out, dst in ((2, od_ref, o_wd), (0, og_ref, o_wg), (1, ou_ref, o_wu)):
        half_copy(i).wait_recv()
        out[1 - d] = tables[i][3][1].astype(F32)
        store(out, dst)

    loop(1, n_ten, lambda k: spread(hall, s_fin, k).wait_recv())
    store(hall, o_h)
    loop(1, n_ten, lambda k: spread_ig(k).wait_recv())
    ig_ref[...] = igall[...].astype(F32)
    store(ig_ref, o_ig)

    def store_pair(first, total, dst):
        for i, tile in enumerate(swap_heads(total)):
            w_ref[:, first + 128 * i : first + 128 * i + 128] = tile
        store(w_ref.at[:, first : first + 256], dst)

    store_pair(512, x_wgo.total(), o_o)
    store_pair(0, x_wgq.total(), o_q)
    grads = x_wgk.total()
    w_ref[:, 256:512] = grads[:, 0:256]
    store(w_ref.at[:, 256:384], o_k)
    store(w_ref.at[:, 384:512], o_v)
    tail_y[0] = grads[:, 256:384]

    def tail_copy(k):
        return remote(tail_y.at[0], tail_y.at[k], s_fin.at[4, k], s_fin.at[5, k], tensor(k))

    loop(1, n_ten, lambda k: tail_copy(k).start())
    tail_sum = grads[:, 256:384]
    for k in range(1, n_ten):
        tail_copy(k).wait_recv()
        tail_sum = tail_sum + tail_y[k]
    t_ref[...] = tail_sum
    store(t_ref, o_t)

    for copy in stores:
        copy.wait()
    for gather in (g_wall, g_wout, g_cot, g_kv, g_ball):
        gather.drain()
    for scatter in (x_dbs, x_ys, x_dkv, x_wgo, x_wgq, x_wgk):
        scatter.drain()

    def drain_tensor(k):
        tensor_copy(0, s_y1, k).wait_send()
        tensor_copy(1, s_y2, k).wait_send()
        spread(dall, s_dall, k).wait_send()
        spread(hall, s_fin, k).wait_send()
        spread_ig(k).wait_send()
        tail_copy(k).wait_send()

    loop(1, n_ten, drain_tensor)

    wait_send_all(across_copies())

    for side, k in enumerate(sides_y):
        wait_send_all(own_copies(k))
        wait_send_all(passed_copies(k))
        wait_send_all(relay_copies(d, 0, side))
        wait_send_all(relay_copies(1 - d, 6, side))
        wait_send_all([relay_grad(i, side) for i in range(3)])
        wait_send_all([grad_copy(i, side) for i in range(3)])
    for i in range(3):
        half_copy(i).wait_send()


def call_layer(sizes, xin, cot, seg, rts, gain_a, gain_f, wq, wk, wv, wo, wr, wgi, wui, wdi):
    n_dp, n_ctx, n_ten = sizes
    nj = n_ctx // 2
    nx = nj // 2
    nq = n_dp * nj
    rows, width = xin.shape
    seq = n_ctx * rows
    quarter = rows // n_ten
    half_d, cut = wgi.shape[1], wgi.shape[2]
    hidden_units = cut * n_ten
    all_rows = nq * 2 * quarter

    def shape(*dims, kind=F32):
        return jax.ShapeDtypeStruct(dims, kind)

    def low(*dims):
        return pltpu.VMEM(dims, BF16)

    def full(*dims):
        return pltpu.VMEM(dims, F32)

    def sems(*dims):
        return pltpu.SemaphoreType.DMA(dims)

    def table(chunk, columns):
        return low(n_dp, nx, 2, 2, chunk, columns)

    def summed(chunk, columns):
        return [
            table(chunk, columns),
            low(n_dp, nx, 2, chunk, columns),
            low(nx, nx, chunk // 2, columns),
            low(nx, n_dp, 2, chunk // 2, columns),
            low(nx, chunk, columns),
        ]

    scratch = [
        table(32, 640),
        table(32, 256),
        table(quarter, width),
        table(quarter, width + TAIL),
        low(nj, 2, rows, 256),
        low(width, hidden_units),
        low(width, hidden_units),
        low(hidden_units, width),
        low(rows, width),
        full(rows, 128),
        full(n_ten, quarter, width),
        full(32, 768),
        full(32, TAIL),
        full(2, half_d, cut),
        full(2, half_d, cut),
        full(2, cut, half_d),
        low(rows, width),
        low(4, rows, 128),
        low(4, rows, seq),
        low(4, rows, seq),
        full(2, rows, 128),
        low(2, n_ten, quarter, width),
        low(2, n_ten, quarter, width),
        low(n_ten, quarter, width),
        low(n_ten, quarter, width),
        low(n_ten, quarter, width),
        low(all_rows, hidden_units),
        low(all_rows, hidden_units),
        low(all_rows, hidden_units),
        *summed(quarter, width + TAIL),
        *summed(quarter, width),
        low(width, hidden_units),
        low(width, hidden_units),
        low(hidden_units, width),
        low(2, width, cut),
        low(2, width, cut),
        low(2, cut, width),
        low(2, half_d, cut),
        low(2, half_d, cut),
        low(2, cut, half_d),
        low(2, half_d, cut),
        low(2, half_d, cut),
        low(2, cut, half_d),
        low(4, rows, 128),
        full(2, rows, 128),
        low(nj, 2, rows, 256),
        low(nj, rows, 256),
        low(nj, rows, 256),
        *summed(32, 256),
        *summed(32, 256),
        *summed(32, 384),
        full(n_ten, 32, TAIL),
        sems(2, nx),
        sems(4),
        sems(2, nx),
        sems(4),
        sems(2, nx),
        sems(4),
        sems(2, nx),
        sems(4),
        sems(nj),
        sems(3),
        sems(12, n_ten + 2),
        sems(2, n_ten),
        sems(2, nx),
        sems(4),
        sems(2, nx),
        sems(4),
        sems(6, n_ten + 2),
        sems(2, n_ten),
        sems(4),
        sems(2, n_ten),
        sems(2, nx),
        sems(4),
        sems(2, nx),
        sems(4),
        sems(2, nx),
        sems(4),
        sems(6, n_ten),
        sems(5),
        sems(10),
    ]
    far, near = pl.BlockSpec(memory_space=pltpu.HBM), pl.BlockSpec(memory_space=pltpu.VMEM)
    flops = 2 * (9 * all_rows * width * hidden_units + 4 * rows * width * 768)
    return pl.pallas_call(
        functools.partial(layer, sizes),
        out_shape=(
            shape(n_ten, quarter, width, kind=BF16),
            shape(n_ten, quarter, width),
            shape(32, 256),
            shape(32, 128),
            shape(32, 128),
            shape(32, 256),
            shape(32, TAIL),
            shape(2, half_d, cut),
            shape(2, half_d, cut),
            shape(2, cut, half_d),
        ),
        in_specs=[far, far] + [near] * 9 + [far] * 3,
        out_specs=[far] * 10,
        scratch_shapes=scratch,
        compiler_params=pltpu.CompilerParams(
            collective_id=0, has_side_effects=True, vmem_limit_bytes=VMEM_BYTES
        ),
        cost_estimate=pl.CostEstimate(flops=flops, bytes_accessed=8 << 20, transcendentals=0),
    )(xin, cot, seg, rts, gain_a, gain_f, wq, wk, wv, wo, wr, wgi, wui, wdi)


def hand_over(*refs):
    sources, tail = refs[:9], refs[9]
    results, gain_a, gain_f, router, sems = refs[10:19], *refs[19:]
    copies = [
        pltpu.make_async_copy(src, dst, sems.at[i])
        for i, (src, dst) in enumerate(zip(sources, results))
    ]
    for copy in copies:
        copy.start()
    router[...] = tail[:, 0:32]
    up = lax.broadcasted_iota(jnp.int32, (32, 32), 0)
    same = up == lax.broadcasted_iota(jnp.int32, (32, 32), 1)
    gain_a[...] = jnp.sum(jnp.where(same, tail[:, 33:34], 0.0), axis=0, keepdims=True)
    gain_f[...] = jnp.sum(jnp.where(same, tail[:, 32:33], 0.0), axis=0, keepdims=True)
    for copy in copies:
        copy.wait()


def call_hand_over(arrays, tail):
    far, near = pl.BlockSpec(memory_space=pltpu.HBM), pl.BlockSpec(memory_space=pltpu.VMEM)
    small = [(1, 32), (1, 32), (32, 32)]
    return pl.pallas_call(
        hand_over,
        out_shape=[jax.ShapeDtypeStruct(a.shape, a.dtype) for a in arrays]
        + [jax.ShapeDtypeStruct(dims, F32) for dims in small],
        in_specs=[near] * (len(arrays) + 1),
        out_specs=[far] * len(arrays) + [near] * 3,
        scratch_shapes=[pltpu.SemaphoreType.DMA((len(arrays),))],
        compiler_params=pltpu.CompilerParams(vmem_limit_bytes=VMEM_BYTES),
    )(*arrays, tail)


def per_device(
    hidden_in,
    segments,
    routes,
    norm_attn,
    w_query,
    w_key,
    w_value,
    w_out,
    norm_ffn,
    w_router,
    w_gate,
    w_up,
    w_down,
    cotangent,
):
    sizes = (lax.axis_size("dp"), lax.axis_size("context"), lax.axis_size("tensor"))
    out, grad, wq, wk, wv, wo, tail, gate_grad, up_grad, down_grad = call_layer(
        sizes,
        hidden_in,
        cotangent,
        segments,
        routes[0].T,
        norm_attn,
        norm_ffn,
        w_query[0],
        w_key[0],
        w_value[0],
        w_out[0].T,
        w_router[0],
        w_gate[0],
        w_up[0],
        w_down[0],
    )
    arrays = (
        out.reshape(hidden_in.shape),
        grad.reshape(hidden_in.shape),
        wq,
        wk,
        wv,
        wo,
        gate_grad,
        up_grad,
        down_grad,
    )
    results = call_hand_over(arrays, tail)
    out, grad, wq, wk, wv, wo, gate_grad, up_grad, down_grad, gain_a, gain_f, router = results
    return (
        out,
        grad,
        gain_a,
        wq[None],
        wk[None],
        wv[None],
        wo.T[None],
        gain_f,
        router[None],
        gate_grad[None],
        up_grad[None],
        down_grad[None],
    )


def solution(mesh):
    in_specs = (
        P(("dp", "context"), None),
        P("dp", "context"),
        P(None, ("dp", "context"), None),
        P(None, ("dp", "context")),
        P(None, ("dp", "context"), "tensor"),
        P(None, ("dp", "context"), "tensor"),
        P(None, ("dp", "context"), "tensor"),
        P(None, "tensor", ("dp", "context")),
        P(None, ("dp", "context")),
        P(None, ("dp", "context"), None),
        P(None, "context", "dp", "tensor"),
        P(None, "context", "dp", "tensor"),
        P(None, "context", "tensor", "dp"),
        P(("dp", "context"), None),
    )
    out_specs = (
        P(("dp", "context"), None),
        P(("dp", "context"), None),
        P(None, ("dp", "context")),
        P(None, ("dp", "context"), "tensor"),
        P(None, ("dp", "context"), "tensor"),
        P(None, ("dp", "context"), "tensor"),
        P(None, "tensor", ("dp", "context")),
        P(None, ("dp", "context")),
        P(None, ("dp", "context"), None),
        P(None, "context", "dp", "tensor"),
        P(None, "context", "dp", "tensor"),
        P(None, "context", "tensor", "dp"),
    )
    return jax.shard_map(
        per_device, mesh=mesh, in_specs=in_specs, out_specs=out_specs, check_vma=False
    )
```
